128 devices in a mesh: seq: 32 (over y, x, core), dp: 4 (over z).
Axes of the slice: x: 4, y: 4, z: 4, core: 2. Of those that a mesh axis runs over, the one named last changes fastest.
Arguments:
- query: bfloat16 [4, 4096, 2048], P('dp', 'seq'), may hold values from -90 to 90
- keys: bfloat16 [4, 4096, 512], P('dp', 'seq'), may hold values from -5 to 5
- values: bfloat16 [4, 4096, 512], P('dp', 'seq'), may hold values from -6 to 6
- output_gradient: bfloat16 [4, 4096, 2048], P('dp', 'seq'), may hold values from -6 to 6
- forward_output: bfloat16 [4, 4096, 2048], P('dp', 'seq'), may hold values from -6 to 6
- doc_ids: int32 [4, 4096], P('dp', 'seq'), may hold values from 0 to 7, never falling along the last dimension, each value on 1 to 2048 neighbouring positions
Outputs:
- grad_query: bfloat16 [4, 4096, 2048], P('dp', 'seq')
- grad_keys: bfloat16 [4, 4096, 512], P('dp', 'seq')
- grad_values: bfloat16 [4, 4096, 512], P('dp', 'seq')
The draws below stay inside these ranges and needn't reach their ends.
Inputs may be any that keep to these rules, and one draw needn't show every extreme that they name: `doc_ids`: document numbers never fall along a sequence; each document has 1 to 2048 tokens, and one document of each sequence has exactly 2048.
All inputs are finite; a program needn't handle non-finite values.
Results may differ from the reference program's by a relative error of at most 0.0049.
Values may be sent and summed in bfloat16 or wider, within the bound.
A program may use at most 128 MiB of HBM per device.

```python
import math
import jax
import jax.numpy as jnp
import numpy as np
from jax import lax

QUERY_HEADS = 16
KEY_VALUE_HEADS = 4
HEAD_WIDTH = 128
DOCS = 8
SEQUENCE_LENGTH = 4096
LONGEST = 2048
PACKED_SEQUENCES = 4


def shared_keys(key):
    base_offset = jax.random.normal(key, (PACKED_SEQUENCES, SEQUENCE_LENGTH, KEY_VALUE_HEADS * HEAD_WIDTH), jnp.float32)
    return jnp.clip(base_offset, -5.0, 5.0)


def draw_keys(key, part):
    result = shared_keys(key)
    return result.astype(jnp.bfloat16)


def draw_query(key, part):
    key = jax.random.fold_in(key, 5)
    result = jnp.clip(jax.random.normal(key, (PACKED_SEQUENCES, SEQUENCE_LENGTH, QUERY_HEADS * HEAD_WIDTH), jnp.float32), -6.0, 6.0)
    return result.astype(jnp.bfloat16)


def level_of(rng, dims, shards, smallest, top_value):
    gain, own = 1.0, jax.random.fold_in(rng, 6)
    for position, shards_of in shards:
        heights = jnp.exp(jax.random.uniform(jax.random.fold_in(own, position), (shards_of,), jnp.float32, smallest / len(shards), top_value / len(shards)))
        gain = gain * jnp.repeat(heights, dims[position] // shards_of).reshape([-1 if axis == position else 1 for axis in range(len(dims))])
    return gain


def profile(count, total, bound, skew):
    portions = [(1 << 20) // math.isqrt(grade ** skew) + 1 for grade in range(2, count + 1)]
    surplus, holding = total - bound - (count - 1), [1] * (count - 1)
    while surplus > 0:
        movable = [i for i in range(count - 1) if holding[i] < bound]
        pool, remaining = sum([portions[i] for i in movable]), surplus
        for i in movable:
            extra = min(bound - holding[i], max(1, remaining * portions[i] // pool), surplus)
            holding[i] = holding[i] + extra
            surplus = surplus - extra
    return np.array([bound] + holding)


def uneven_parts(stream_key, number_of, total, reach, skew):
    if number_of == 2:
        one = jax.random.randint(stream_key, (), max(1, total - reach), min(reach, total - 1) + 1)
        return jnp.stack([one, total - one])
    sizes = jnp.asarray(profile(number_of, total, reach, skew), jnp.int32)
    twos = (number_of - 1) // 2
    donor, taker = sizes[1:1 + 2 * twos:2], sizes[2:2 + 2 * twos:2]
    slack = jnp.minimum(donor - 1, reach - taker)
    passed = jax.random.randint(jax.random.fold_in(stream_key, 1), (twos,), 0, 1 << 20) % (slack + 1)
    sizes = sizes.at[1:1 + 2 * twos:2].set(donor - passed).at[2:2 + 2 * twos:2].set(taker + passed)
    return sizes[jax.random.permutation(jax.random.fold_in(stream_key, 2), number_of)]


def gaussian(own_key, dims, deviation, most, split=(), kind=jnp.bfloat16):
    gain = level_of(own_key, dims, split, -0.22, 0.18) if split else 1.0
    entries = jax.random.normal(own_key, dims, jnp.float32) * deviation * gain
    return jnp.minimum(jnp.maximum(entries, -most), most).astype(kind)


def setup_inputs(seed: int = 0) -> dict:
    streams_of = jax.random.split(jax.random.key(seed), 7)
    return {
        "query": draw_query(jax.random.fold_in(streams_of[6], 71), 0),
        "keys": draw_keys(jax.random.fold_in(streams_of[6], 71), 0),
        "values": gaussian(streams_of[2], (PACKED_SEQUENCES, SEQUENCE_LENGTH, KEY_VALUE_HEADS * HEAD_WIDTH), 1.0, 6.0, ((0, 4), (1, 32))),
        "output_gradient": gaussian(streams_of[3], (PACKED_SEQUENCES, SEQUENCE_LENGTH, QUERY_HEADS * HEAD_WIDTH), 1.0, 6.0, ((0, 4), (1, 32))),
        "forward_output": gaussian(streams_of[4], (PACKED_SEQUENCES, SEQUENCE_LENGTH, QUERY_HEADS * HEAD_WIDTH), 1.0, 6.0, ((0, 4), (1, 32))),
        "doc_ids": jax.vmap(lambda own: jnp.searchsorted(jnp.cumsum(uneven_parts(own, DOCS, SEQUENCE_LENGTH, LONGEST, 2)), jnp.arange(SEQUENCE_LENGTH), side="right"))(jax.random.split(streams_of[5], PACKED_SEQUENCES)).reshape((PACKED_SEQUENCES, SEQUENCE_LENGTH)).astype(jnp.int32),
    }


MASKED_LOW = -1e+30

def head_grads(q_group, k_one, v_one, dout_group, out_group, ids):
    token_length = ids.shape[0]
    softmax_scale = 1.0 / math.sqrt(HEAD_WIDTH)
    positions = jnp.arange(token_length, dtype=jnp.int32)
    allowed = (ids[None, :] == ids[:, None]) & (positions[None, :] <= positions[:, None])
    q_wide = q_group.astype(jnp.float32)
    k_wide = k_one.astype(jnp.float32)
    v_wide = v_one.astype(jnp.float32)
    dout_wide = dout_group.astype(jnp.float32)
    out_wide = out_group.astype(jnp.float32)
    logits = jnp.einsum('tgd,sd->gts', q_wide, k_wide) * softmax_scale
    masked = jnp.where(allowed[None], logits, MASKED_LOW)
    row_max = lax.optimization_barrier(jnp.max(masked, axis=2, keepdims=True))
    total = lax.optimization_barrier(jnp.sum(jnp.where(allowed[None], jnp.exp(masked - row_max), 0.0), axis=2, keepdims=True))
    lse = row_max + jnp.log(total)
    attn_probs = jnp.where(allowed[None], jnp.exp(logits - lse), 0.0)
    probs_low = lax.optimization_barrier(attn_probs.astype(jnp.bfloat16)).astype(jnp.float32)
    value_gradient = jnp.einsum('gts,tgd->sd', probs_low, dout_wide)
    prob_grads = jnp.einsum('tgd,sd->gts', dout_wide, v_wide)
    row_dots = jnp.transpose(lax.optimization_barrier(jnp.sum(dout_wide * out_wide, axis=2)), (1, 0))
    score_grads = attn_probs * (prob_grads - row_dots[:, :, None])
    score_low = lax.optimization_barrier(score_grads.astype(jnp.bfloat16)).astype(jnp.float32)
    grad_q = jnp.einsum('gts,sd->tgd', score_low, k_wide) * softmax_scale
    key_gradient = jnp.einsum('gts,tgd->sd', score_low, q_wide) * softmax_scale
    return (grad_q, key_gradient, value_gradient)

def sequence_grads(operands):
    query, keys, values, output_gradient, forward_output, ids = operands
    token_length = ids.shape[0]
    group_count = QUERY_HEADS // KEY_VALUE_HEADS
    query_split = jnp.transpose(query.reshape(token_length, KEY_VALUE_HEADS, group_count, HEAD_WIDTH), (1, 0, 2, 3))
    cotangent_split = jnp.transpose(output_gradient.reshape(token_length, KEY_VALUE_HEADS, group_count, HEAD_WIDTH), (1, 0, 2, 3))
    output_split = jnp.transpose(forward_output.reshape(token_length, KEY_VALUE_HEADS, group_count, HEAD_WIDTH), (1, 0, 2, 3))
    key_split = jnp.transpose(keys.reshape(token_length, KEY_VALUE_HEADS, HEAD_WIDTH), (1, 0, 2))
    value_split = jnp.transpose(values.reshape(token_length, KEY_VALUE_HEADS, HEAD_WIDTH), (1, 0, 2))

    def one_head(parts):
        return head_grads(parts[0], parts[1], parts[2], parts[3], parts[4], ids)
    grad_q, key_gradient, value_gradient = lax.map(one_head, (query_split, key_split, value_split, cotangent_split, output_split))
    grad_q = jnp.transpose(grad_q, (1, 0, 2, 3)).reshape(token_length, QUERY_HEADS * HEAD_WIDTH)
    key_gradient = jnp.transpose(key_gradient, (1, 0, 2)).reshape(token_length, KEY_VALUE_HEADS * HEAD_WIDTH)
    value_gradient = jnp.transpose(value_gradient, (1, 0, 2)).reshape(token_length, KEY_VALUE_HEADS * HEAD_WIDTH)
    return (grad_q.astype(jnp.bfloat16), key_gradient.astype(jnp.bfloat16), value_gradient.astype(jnp.bfloat16))

def reference(query, keys, values, output_gradient, forward_output, doc_ids):
    grad_query, grad_keys, grad_values = lax.map(sequence_grads, (query, keys, values, output_gradient, forward_output, doc_ids))
    return (grad_query, grad_keys, grad_values)
```

```python
import functools
import math

import jax
import jax.numpy as jnp
from jax import lax
from jax.experimental import pallas as pl
from jax.experimental.pallas import tpu as pltpu
from jax.sharding import PartitionSpec as P

HEAD_WIDTH = 128
LONGEST = 2048
DOC_ROWS = 16
MASKED_LOW = -1e30
SCALE = 1.0 / math.sqrt(HEAD_WIDTH)
LOG2_E = math.log2(math.e)


def nn(a, b):
    return jnp.dot(a, b, preferred_element_type=jnp.float32)


def tn(a, b):
    return lax.dot_general(a, b, (((0,), (0,)), ((), ())), preferred_element_type=jnp.float32)


def kernel(
    chips, window, kv, group,
    q_ref, k_ref, v_ref, do_ref, o_ref, id_ref,
    dq_out, dk_out, dv_out,
    ksend, vsend, kbuf, vbuf, k_t,
    qsend, dosend, rdsend, qbuf, dobuf, rdbuf,
    q_h, q_t, do_h, do_t, rd_h,
    e_all, m_all, l_all, r_all,
    p_low, s_low, dq_t,
    psend, precv, diag, acc, dqsend, dqrecv,
    ks_sem, kr_sem, vs_sem, vr_sem, ps_sem, pr_sem, xs_sem, xr_sem,
):
    tok = q_ref.shape[0]
    span = 2 * tok
    heads = kv * group
    half = heads * HEAD_WIDTH
    kvf = kv * HEAD_WIDTH
    me = lax.axis_index("seq")
    chip = me // 2
    core = me % 2
    other = 1 - core
    partner = chip * 2 + other
    n_back = jnp.minimum(chip, window)
    n_fwd = jnp.minimum(chips - 1 - chip, window)

    barrier = pltpu.get_barrier_semaphore()
    pl.semaphore_signal(barrier, inc=1, device_id={"seq": partner})

    def greet_back(o, c):
        for side in range(2):
            pl.semaphore_signal(barrier, inc=1, device_id={"seq": (chip - o) * 2 + side})
        return c

    def greet_fwd(o, c):
        for side in range(2):
            pl.semaphore_signal(barrier, inc=1, device_id={"seq": (chip + o) * 2 + side})
        return c

    lax.fori_loop(1, n_back + 1, greet_back, 0)
    lax.fori_loop(1, n_fwd + 1, greet_fwd, 0)

    ids = id_ref[...]
    rows = lax.broadcasted_iota(jnp.int32, (DOC_ROWS, tok), 0)
    onehot = jnp.where(rows == ids, 1.0, 0.0).astype(jnp.bfloat16)
    for side in range(2):
        ksend[side, :tok, :] = k_ref[:, side * kvf:(side + 1) * kvf]
        ksend[side, tok:, :tok] = onehot
        ksend[side, tok:, tok:] = jnp.zeros((DOC_ROWS, kvf - tok), jnp.bfloat16)
        vsend[side] = v_ref[:, side * kvf:(side + 1) * kvf]
    kbuf[0, core] = ksend[core]
    vbuf[0, core] = vsend[core]
    own_cols = pl.ds(pl.multiple_of(core * half, half), half)
    other_cols = pl.ds(pl.multiple_of(other * half, half), half)
    qsend[...] = q_ref[:, other_cols]
    dosend[...] = do_ref[:, other_cols]
    qbuf[core] = q_ref[:, own_cols]
    dobuf[core] = do_ref[:, own_cols]

    pl.semaphore_wait(barrier, 1 + 2 * (n_back + n_fwd))

    def swap(src, dst, slot):
        return pltpu.make_async_remote_copy(
            src_ref=src, dst_ref=dst, send_sem=xs_sem.at[slot], recv_sem=xr_sem.at[slot],
            device_id={"seq": partner},
        )

    def k_copy(o, side, slot_side, target):
        return pltpu.make_async_remote_copy(
            src_ref=ksend.at[side], dst_ref=kbuf.at[o, slot_side],
            send_sem=ks_sem.at[o, side], recv_sem=kr_sem.at[o, slot_side],
            device_id={"seq": target},
        )

    def v_copy(o, side, slot_side, target):
        return pltpu.make_async_remote_copy(
            src_ref=vsend.at[side], dst_ref=vbuf.at[o, slot_side],
            send_sem=vs_sem.at[o, side], recv_sem=vr_sem.at[o, slot_side],
            device_id={"seq": target},
        )

    def p_copy(o, side, slot_side, target):
        return pltpu.make_async_remote_copy(
            src_ref=psend.at[o, side], dst_ref=precv.at[o, slot_side],
            send_sem=ps_sem.at[o, side], recv_sem=pr_sem.at[o, slot_side],
            device_id={"seq": target},
        )

    q_swap = swap(qsend, qbuf.at[core], 0)
    do_swap = swap(dosend, dobuf.at[core], 1)
    rd_swap = swap(rdsend, rdbuf.at[core], 2)
    dq_swap = swap(dqsend, dqrecv, 3)
    q_swap.start()
    k_copy(0, other, core, partner).start()

    def send_k(o, c):
        for side in range(2):
            k_copy(o, side, core, (chip + o) * 2 + side).start()
        return c

    def send_v(o, c):
        for side in range(2):
            v_copy(o, side, core, (chip + o) * 2 + side).start()
        return c

    lax.fori_loop(1, n_fwd + 1, send_k, 0)
    do_swap.start()
    v_copy(0, other, core, partner).start()
    lax.fori_loop(1, n_fwd + 1, send_v, 0)

    def dots_of(cols):
        prod = do_ref[:, cols].astype(jnp.float32) * o_ref[:, cols].astype(jnp.float32)
        return jnp.sum(jnp.transpose(prod), axis=0, keepdims=True)

    for h in range(heads):
        rdsend[h:h + 1, :] = dots_of(
            pl.ds(pl.multiple_of(other * half + h * HEAD_WIDTH, HEAD_WIDTH), HEAD_WIDTH))
        rdbuf[core, h:h + 1, :] = dots_of(
            pl.ds(pl.multiple_of(core * half + h * HEAD_WIDTH, HEAD_WIDTH), HEAD_WIDTH))
    rd_swap.start()

    swap(qsend, qbuf.at[other], 0).wait_recv()
    for h in range(heads):
        cols = slice(h * HEAD_WIDTH, (h + 1) * HEAD_WIDTH)
        both = jnp.concatenate([qbuf[0, :, cols], qbuf[1, :, cols]], axis=0)
        q_h[h // group, (h % group) * span:(h % group + 1) * span, :] = both
        q_t[:, h * span:(h + 1) * span] = jnp.transpose(both)
    k_copy(0, other, other, partner).wait_recv()
    onehot_q = jnp.concatenate(
        [kbuf[0, 0, tok:, :tok], kbuf[0, 1, tok:, :tok]], axis=1)

    def stats(o, c):
        @pl.when(o > 0)
        def _():
            for side in range(2):
                k_copy(o, side, side, partner).wait_recv()

        onehot_k = jnp.concatenate([kbuf[o, 0, tok:, :tok], kbuf[o, 1, tok:, :tok]], axis=1)
        same = tn(onehot_k, onehot_q)
        key_pos = lax.broadcasted_iota(jnp.int32, (span, span), 0)
        query_pos = lax.broadcasted_iota(jnp.int32, (span, span), 1)
        allowed = (same > 0.5) & (key_pos <= query_pos + o * span)
        bias = jnp.where(allowed, 0.0, MASKED_LOW)
        for j in range(kv):
            cols = slice(j * HEAD_WIDTH, (j + 1) * HEAD_WIDTH)
            k_j = jnp.concatenate([kbuf[o, 0, :tok, cols], kbuf[o, 1, :tok, cols]], axis=0)
            k_t[o, j] = jnp.transpose(k_j)
            for g in range(group):
                h = j * group + g
                s = nn(k_j, q_t[:, h * span:(h + 1) * span]) * (SCALE * LOG2_E) + bias
                m = jnp.max(s, axis=0, keepdims=True)
                e = jnp.exp2(s - m)
                e_all[o, h] = e
                m_all[o, h:h + 1, :] = m
                l_all[o, h:h + 1, :] = jnp.sum(e, axis=0, keepdims=True)
        return c

    lax.fori_loop(0, n_back + 1, stats, 0)

    m_top = lax.fori_loop(1, n_back + 1, lambda o, m: jnp.maximum(m, m_all[o]), m_all[0])
    total = lax.fori_loop(
        0, n_back + 1, lambda o, t: t + l_all[o] * jnp.exp2(m_all[o] - m_top),
        jnp.zeros((heads, span), jnp.float32))
    inverse = 1.0 / total

    def ratios(o, c):
        r_all[o] = jnp.exp2(m_all[o] - m_top) * inverse
        return c

    lax.fori_loop(0, n_back + 1, ratios, 0)

    swap(dosend, dobuf.at[other], 1).wait_recv()
    swap(rdsend, rdbuf.at[other], 2).wait_recv()
    for h in range(heads):
        cols = slice(h * HEAD_WIDTH, (h + 1) * HEAD_WIDTH)
        both = jnp.concatenate([dobuf[0, :, cols], dobuf[1, :, cols]], axis=0)
        do_h[h // group, (h % group) * span:(h % group + 1) * span, :] = both
        do_t[:, h * span:(h + 1) * span] = jnp.transpose(both)
    rd_h[...] = jnp.concatenate([rdbuf[0], rdbuf[1]], axis=1)
    dq_t[...] = jnp.zeros(dq_t.shape, jnp.float32)
    v_copy(0, other, other, partner).wait_recv()

    def grads(step, c):
        o = n_back - step

        @pl.when(o > 0)
        def _():
            for side in range(2):
                v_copy(o, side, side, partner).wait_recv()

        for j in range(kv):
            cols = slice(j * HEAD_WIDTH, (j + 1) * HEAD_WIDTH)
            v_j = jnp.concatenate([vbuf[o, 0, :, cols], vbuf[o, 1, :, cols]], axis=0)
            for g in range(group):
                h = j * group + g
                dp = nn(v_j, do_t[:, h * span:(h + 1) * span])
                p = e_all[o, h] * r_all[o, h:h + 1, :]
                ds = p * (dp - rd_h[h:h + 1, :])
                p_low[j, :, g * span:(g + 1) * span] = p.astype(jnp.bfloat16)
                s_low[j, :, g * span:(g + 1) * span] = ds.astype(jnp.bfloat16)
            dv = nn(p_low[j], do_h[j])
            dk = nn(s_low[j], q_h[j]) * SCALE
            dq_t[j] += nn(k_t[o, j], s_low[j])
            for side in range(2):
                piece = slice(side * tok, (side + 1) * tok)
                psend[o, side, 0, :, cols] = dk[piece].astype(jnp.bfloat16)
                psend[o, side, 1, :, cols] = dv[piece].astype(jnp.bfloat16)

            @pl.when(o == 0)
            def _():
                for side in range(2):
                    piece = slice(side * tok, (side + 1) * tok)
                    diag[side, 0, :, cols] = dk[piece]
                    diag[side, 1, :, cols] = dv[piece]

        @pl.when(o > 0)
        def _():
            for side in range(2):
                p_copy(o, side, core, (chip - o) * 2 + side).start()

        return c

    lax.fori_loop(0, n_back + 1, grads, 0)
    p_copy(0, other, core, partner).start()

    for h in range(heads):
        cols = slice(h * HEAD_WIDTH, (h + 1) * HEAD_WIDTH)
        piece = jnp.transpose(
            dq_t[h // group, :, (h % group) * span:(h % group + 1) * span] * SCALE
        ).astype(jnp.bfloat16)
        dobuf[0, :, cols] = piece[:tok]
        dobuf[1, :, cols] = piece[tok:]
    dqsend[...] = dobuf[other]
    dq_swap.start()
    dq_out[:, own_cols] = dobuf[core]

    acc[core] = diag[core]
    p_copy(0, other, other, partner).wait_recv()
    acc[other] = precv[0, other].astype(jnp.float32)

    def collect(o, c):
        for side in range(2):
            p_copy(o, side, side, partner).wait_recv()
            acc[side] += precv[o, side].astype(jnp.float32)
        return c

    lax.fori_loop(1, n_fwd + 1, collect, 0)
    for side in range(2):
        cols = slice(side * kvf, (side + 1) * kvf)
        dk_out[:, cols] = acc[side, 0].astype(jnp.bfloat16)
        dv_out[:, cols] = acc[side, 1].astype(jnp.bfloat16)
    dq_swap.wait_recv()
    dq_out[:, other_cols] = dqrecv[...]

    q_swap.wait_send()
    do_swap.wait_send()
    rd_swap.wait_send()
    dq_swap.wait_send()
    k_copy(0, other, core, partner).wait_send()
    v_copy(0, other, core, partner).wait_send()
    p_copy(0, other, core, partner).wait_send()

    def sent_fwd(o, c):
        for side in range(2):
            k_copy(o, side, core, partner).wait_send()
            v_copy(o, side, core, partner).wait_send()
        return c

    def sent_back(o, c):
        for side in range(2):
            p_copy(o, side, core, partner).wait_send()
        return c

    lax.fori_loop(1, n_fwd + 1, sent_fwd, 0)
    lax.fori_loop(1, n_back + 1, sent_back, 0)


def on_device(seq_size, query, keys, values, output_gradient, forward_output, doc_ids):
    tok = query.shape[1]
    span = 2 * tok
    chips = seq_size // 2
    window = min(-(-LONGEST // span), chips - 1)
    kv = keys.shape[2] // HEAD_WIDTH // 2
    group = query.shape[2] // keys.shape[2]
    heads = kv * group
    half = heads * HEAD_WIDTH
    kvf = kv * HEAD_WIDTH
    slots = window + 1
    bf, f32 = jnp.bfloat16, jnp.float32
    vmem = pl.BlockSpec(memory_space=pltpu.VMEM)
    dma = pltpu.SemaphoreType.DMA
    grad_query, grad_keys, grad_values = pl.pallas_call(
        functools.partial(kernel, chips, window, kv, group),
        out_shape=(
            jax.ShapeDtypeStruct((tok, 2 * half), bf),
            jax.ShapeDtypeStruct((tok, 2 * kvf), bf),
            jax.ShapeDtypeStruct((tok, 2 * kvf), bf),
        ),
        in_specs=[vmem] * 6,
        out_specs=(vmem,) * 3,
        scratch_shapes=[
            pltpu.VMEM((2, tok + DOC_ROWS, kvf), bf),
            pltpu.VMEM((2, tok, kvf), bf),
            pltpu.VMEM((slots, 2, tok + DOC_ROWS, kvf), bf),
            pltpu.VMEM((slots, 2, tok, kvf), bf),
            pltpu.VMEM((slots, kv, HEAD_WIDTH, span), bf),
            pltpu.VMEM((tok, half), bf),
            pltpu.VMEM((tok, half), bf),
            pltpu.VMEM((heads, tok), f32),
            pltpu.VMEM((2, tok, half), bf),
            pltpu.VMEM((2, tok, half), bf),
            pltpu.VMEM((2, heads, tok), f32),
            pltpu.VMEM((kv, group * span, HEAD_WIDTH), bf),
            pltpu.VMEM((HEAD_WIDTH, heads * span), bf),
            pltpu.VMEM((kv, group * span, HEAD_WIDTH), bf),
            pltpu.VMEM((HEAD_WIDTH, heads * span), bf),
            pltpu.VMEM((heads, span), f32),
            pltpu.VMEM((slots, heads, span, span), f32),
            pltpu.VMEM((slots, heads, span), f32),
            pltpu.VMEM((slots, heads, span), f32),
            pltpu.VMEM((slots, heads, span), f32),
            pltpu.VMEM((kv, span, group * span), bf),
            pltpu.VMEM((kv, span, group * span), bf),
            pltpu.VMEM((kv, HEAD_WIDTH, group * span), f32),
            pltpu.VMEM((slots, 2, 2, tok, kvf), bf),
            pltpu.VMEM((slots, 2, 2, tok, kvf), bf),
            pltpu.VMEM((2, 2, tok, kvf), f32),
            pltpu.VMEM((2, 2, tok, kvf), f32),
            pltpu.VMEM((tok, half), bf),
            pltpu.VMEM((tok, half), bf),
            dma((slots, 2)), dma((slots, 2)), dma((slots, 2)), dma((slots, 2)),
            dma((slots, 2)), dma((slots, 2)), dma((4,)), dma((4,)),
        ],
        compiler_params=pltpu.CompilerParams(
            collective_id=0, has_side_effects=True, vmem_limit_bytes=56 * 1024 * 1024,
        ),
    )(query[0], keys[0], values[0], output_gradient[0], forward_output[0], doc_ids)
    return grad_query[None], grad_keys[None], grad_values[None]


def solution(mesh):
    wide = P("dp", "seq", None)
    return jax.shard_map(
        functools.partial(on_device, mesh.shape["seq"]),
        mesh=mesh,
        in_specs=(wide, wide, wide, wide, wide, P("dp", "seq")),
        out_specs=(wide, wide, wide),
        check_vma=False,
    )
```

```python
import functools
import math

import jax
import jax.numpy as jnp
from jax import lax
from jax.experimental import pallas as pl
from jax.experimental.pallas import tpu as pltpu
from jax.sharding import PartitionSpec as P

HEAD_WIDTH = 128
LONGEST = 2048
DOC_ROWS = 16
MASKED_LOW = -1e30
SCALE = 1.0 / math.sqrt(HEAD_WIDTH)
LOG2_SCALE = SCALE * math.log2(math.e)
CHIPS = 4
PAIR = 2
REMOTE = (1, 3, 2)


def nn(a, b):
    return jnp.dot(a, b, preferred_element_type=jnp.float32)


def kernel(
    rows, back,
    q_ref, k_ref, v_ref, do_ref, o_ref, id_ref,
    dq_out, dk_out, dv_out,
    ksend, kbuf, vbuf, k_x, k_t,
    rdsend, qbuf, dobuf, rdbuf, q_x, q_h, do_t, do_h, rd_h,
    e_all, m_all, l_all, r_all, dq_t,
    kv_acc, xrecv, ysend, yrecv, fsend, frecv, dqsend, dqrecv,
    ks, kr, vs, vr, qs, qr, gs, gr, rs, rr,
    kps, kpr, vps, vpr, kys, kyr, vys, vyr,
    xs, xr, ys, yr, fs, fr, ds, dr,
):
    tok = q_ref.shape[0]
    span = 2 * tok
    width = PAIR * HEAD_WIDTH
    hw = HEAD_WIDTH
    me = lax.axis_index("seq")
    core = me % 2
    other = 1 - core
    x = (me // 2) % CHIPS
    y = me // (2 * CHIPS)
    depth = jnp.minimum(y, back)
    reach = jnp.minimum(rows - 1 - y, back)

    def at(row, col, side):
        return {"seq": (row * CHIPS + col) * 2 + side}

    def turn(dx):
        return (x + dx) % CHIPS

    partner = at(y, x, other)

    barrier = pltpu.get_barrier_semaphore()
    pl.semaphore_signal(barrier, inc=1, device_id=partner)
    for dx in REMOTE:
        for side in range(2):
            pl.semaphore_signal(barrier, inc=1, device_id=at(y, turn(dx), side))

    def greet_back(r, c):
        pl.semaphore_signal(barrier, inc=1, device_id=at(y - r, x, core))
        return c

    def greet_fwd(r, c):
        pl.semaphore_signal(barrier, inc=1, device_id=at(y + r, x, core))
        return c

    lax.fori_loop(1, depth + 1, greet_back, 0)
    lax.fori_loop(1, reach + 1, greet_fwd, 0)

    def feats(head, count):
        return pl.ds(pl.multiple_of(head * hw, hw), count * hw)

    def pair_cols(col, side):
        return feats(col * 2 * PAIR + side * PAIR, PAIR)

    doc_rows = lax.broadcasted_iota(jnp.int32, (DOC_ROWS, tok), 0)
    barred = jnp.where(doc_rows == id_ref[...], 0.0, MASKED_LOW).astype(jnp.bfloat16)
    for col in range(CHIPS):
        ksend[col, :tok, :] = k_ref[:, col * hw:(col + 1) * hw]
        ksend[col, tok:, :] = barred
    kbuf[core, x] = ksend[x]
    vbuf[core, x] = v_ref[:, feats(x, 1)]
    qbuf[x, core] = q_ref[:, pair_cols(x, core)]
    dobuf[x, core] = do_ref[:, pair_cols(x, core)]

    pl.semaphore_wait(barrier, 2 * CHIPS - 1 + depth + reach)

    def remote(src, dst, send, recv, target):
        return pltpu.make_async_remote_copy(
            src_ref=src, dst_ref=dst, send_sem=send, recv_sem=recv, device_id=target)

    def k_copy(dx):
        return remote(ksend.at[turn(dx)], kbuf.at[core, x], ks.at[dx], kr.at[x],
                      at(y, turn(dx), core))

    def v_copy(dx):
        return remote(v_ref.at[:, feats(turn(dx), 1)], vbuf.at[core, x], vs.at[dx], vr.at[x],
                      at(y, turn(dx), core))

    def q_copy(dx, side):
        return remote(q_ref.at[:, pair_cols(turn(dx), side)], qbuf.at[x, core],
                      qs.at[dx, side], qr.at[x, core], at(y, turn(dx), side))

    def do_copy(dx, side):
        return remote(do_ref.at[:, pair_cols(turn(dx), side)], dobuf.at[x, core],
                      gs.at[dx, side], gr.at[x, core], at(y, turn(dx), side))

    def rd_copy(dx, side):
        return remote(rdsend.at[turn(dx), side], rdbuf.at[x, core],
                      rs.at[dx, side], rr.at[x, core], at(y, turn(dx), side))

    def k_from(col):
        return remote(ksend.at[0], kbuf.at[core, col], ks.at[0], kr.at[col], partner)

    def v_from(col):
        return remote(v_ref.at[:, :hw], vbuf.at[core, col], vs.at[0], vr.at[col], partner)

    def q_from(col, side):
        return remote(q_ref.at[:, :width], qbuf.at[col, side], qs.at[0, 0], qr.at[col, side],
                      partner)

    def do_from(col, side):
        return remote(do_ref.at[:, :width], dobuf.at[col, side], gs.at[0, 0], gr.at[col, side],
                      partner)

    def rd_from(col, side):
        return remote(rdsend.at[0, 0], rdbuf.at[col, side], rs.at[0, 0], rr.at[col, side], partner)

    def row_of(r):
        return pl.ds(r * CHIPS, CHIPS)

    def k_pass(r, side):
        return remote(kbuf.at[side, row_of(r)], kbuf.at[side, row_of(r)], kps.at[r], kpr.at[r],
                      partner)

    def v_pass(r, side):
        return remote(vbuf.at[side, row_of(r)], vbuf.at[side, row_of(r)], vps.at[r], vpr.at[r],
                      partner)

    def k_row(r):
        return remote(kbuf.at[core, row_of(0)], kbuf.at[core, row_of(r)], kys.at[r], kyr.at[r],
                      at(y + r, x, core))

    def v_row(r):
        return remote(vbuf.at[core, row_of(0)], vbuf.at[core, row_of(r)], vys.at[r], vyr.at[r],
                      at(y + r, x, core))

    for dx in REMOTE:
        k_copy(dx).start()
    q_copy(0, other).start()
    for dx in REMOTE:
        for side in range(2):
            q_copy(dx, side).start()
    for dx in REMOTE:
        v_copy(dx).start()
    do_copy(0, other).start()
    for dx in REMOTE:
        for side in range(2):
            do_copy(dx, side).start()

    for col in range(CHIPS):
        for side in range(2):
            for g in range(PAIR):
                h = (col * 2 + side) * PAIR + g
                cols = slice(h * hw, (h + 1) * hw)
                prod = do_ref[:, cols].astype(jnp.float32) * o_ref[:, cols].astype(jnp.float32)
                rdsend[col, side, g:g + 1, :] = jnp.sum(
                    jnp.transpose(prod), axis=0, keepdims=True)
            rdsend[col, side, PAIR:, :] = jnp.zeros((8 - PAIR, tok), jnp.float32)
    rdbuf[x, core] = rdsend[x, core]
    rd_copy(0, other).start()
    for dx in REMOTE:
        for side in range(2):
            rd_copy(dx, side).start()

    def start_k_row(r, c):
        k_row(r).start()
        return c

    def start_v_row(r, c):
        v_row(r).start()
        return c

    def build_keys(r):
        def one(i, c):
            slot = r * CHIPS + i
            both = jnp.concatenate([kbuf[0, slot, :tok, :], kbuf[1, slot, :tok, :]], axis=0)
            bars = jnp.concatenate([kbuf[0, slot, tok:, :], kbuf[1, slot, tok:, :]], axis=1)
            pad = jnp.zeros((hw - DOC_ROWS, span), jnp.bfloat16)
            k_x[slot, :, :hw] = both
            k_x[slot, :, hw:] = jnp.transpose(jnp.concatenate([bars, pad], axis=0))
            k_t[slot] = jnp.transpose(both)
            return c

        lax.fori_loop(0, CHIPS, one, 0)

    for dx in REMOTE:
        k_from(turn(dx)).wait_recv()
    k_pass(0, core).start()
    lax.fori_loop(1, reach + 1, start_k_row, 0)
    k_pass(0, other).wait_recv()
    build_keys(0)

    def order(i):
        return (x + i + i // 2 - 2 * (i // 3)) % CHIPS

    def first_row(r, c):
        @pl.when(r > 0)
        def _():
            remote(kbuf.at[core, row_of(0)], kbuf.at[core, row_of(r)], kys.at[r], kyr.at[r],
                   partner).wait_recv()
            k_pass(r, core).start()
            k_pass(r, other).wait_recv()
            build_keys(r)

        def first_chunk(i, c):
            qc = order(i)

            @pl.when(r == 0)
            def _():
                for side in range(2):
                    @pl.when((qc != x) | (core != side))
                    def _():
                        q_from(qc, side).wait_recv()
                for g in range(PAIR):
                    cols = slice(g * hw, (g + 1) * hw)
                    both = jnp.concatenate([qbuf[qc, 0, :, cols], qbuf[qc, 1, :, cols]], axis=0)
                    q_h[qc, g * span:(g + 1) * span, :] = both
                    q_x[qc, :hw, g * span:(g + 1) * span] = jnp.transpose(both)
                    for side in range(2):
                        start = g * span + side * tok
                        bars = kbuf[side, qc, tok:, :].astype(jnp.float32)
                        q_x[qc, hw:hw + DOC_ROWS, start:start + tok] = jnp.where(
                            bars == 0.0, 1.0, 0.0).astype(jnp.bfloat16)
                q_x[qc, hw + DOC_ROWS:, :] = jnp.zeros(
                    (hw - DOC_ROWS, PAIR * span), jnp.bfloat16)

            def tile(kc, c):
                o = r * CHIPS + qc - kc
                place = qc * (back * CHIPS + 1) + o

                def finish(s):
                    m = jnp.max(s, axis=0, keepdims=True)
                    e = jnp.exp2((s - m) * LOG2_SCALE)
                    e_all[place] = e
                    m_all[place] = m
                    l_all[place] = jnp.sum(e, axis=0, keepdims=True)

                @pl.when(o > 0)
                def _():
                    finish(nn(k_x[r * CHIPS + kc], q_x[qc]))

                @pl.when(o == 0)
                def _():
                    s = nn(k_x[r * CHIPS + kc], q_x[qc])
                    key_pos = lax.broadcasted_iota(jnp.int32, (span, PAIR * span), 0)
                    query_pos = lax.broadcasted_iota(jnp.int32, (span, PAIR * span), 1) % span
                    finish(jnp.where(key_pos <= query_pos, s, MASKED_LOW))

                return c

            low = jnp.where(r == back, qc, 0)
            high = jnp.where(r == 0, qc + 1, CHIPS)
            lax.fori_loop(low, high, tile, 0)
            return c

        lax.fori_loop(0, CHIPS, first_chunk, 0)

        @pl.when(r == 0)
        def _():
            for dx in REMOTE:
                v_from(turn(dx)).wait_recv()
            v_pass(0, core).start()
            lax.fori_loop(1, reach + 1, start_v_row, 0)

        return c

    lax.fori_loop(0, depth + 1, first_row, 0)

    v_pass(0, other).wait_recv()

    def take_values(r, c):
        remote(vbuf.at[core, row_of(0)], vbuf.at[core, row_of(r)], vys.at[r], vyr.at[r],
               partner).wait_recv()
        v_pass(r, core).start()
        return c

    def have_values(r, c):
        v_pass(r, other).wait_recv()
        return c

    lax.fori_loop(1, depth + 1, take_values, 0)

    def ready(i, c):
        qc = order(i)
        base = qc * (back * CHIPS + 1)
        last = jnp.minimum(y * CHIPS + qc, back * CHIPS)
        m_top = lax.fori_loop(
            1, last + 1, lambda o, m: jnp.maximum(m, m_all[base + o]), m_all[base])
        total = lax.fori_loop(
            0, last + 1,
            lambda o, t: t + l_all[base + o] * jnp.exp2((m_all[base + o] - m_top) * LOG2_SCALE),
            jnp.zeros((1, PAIR * span), jnp.float32))
        inverse = 1.0 / total

        def ratio(o, c):
            r_all[base + o] = jnp.exp2((m_all[base + o] - m_top) * LOG2_SCALE) * inverse
            return c

        lax.fori_loop(0, last + 1, ratio, 0)
        for side in range(2):
            @pl.when((qc != x) | (core != side))
            def _():
                do_from(qc, side).wait_recv()
                rd_from(qc, side).wait_recv()
        for g in range(PAIR):
            cols = slice(g * hw, (g + 1) * hw)
            both = jnp.concatenate([dobuf[qc, 0, :, cols], dobuf[qc, 1, :, cols]], axis=0)
            do_h[qc, g * span:(g + 1) * span, :] = both
            do_t[qc, :, g * span:(g + 1) * span] = jnp.transpose(both)
            for side in range(2):
                start = g * span + side * tok
                rd_h[qc, :, start:start + tok] = rdbuf[qc, side, g:g + 1, :]
        dq_t[qc] = jnp.zeros((hw, PAIR * span), jnp.float32)
        return c

    lax.fori_loop(0, CHIPS, ready, 0)
    lax.fori_loop(1, depth + 1, have_values, 0)

    def x_copy(slot):
        return remote(kv_acc.at[slot, other], xrecv.at[slot], xs.at[slot], xr.at[slot], partner)

    def y_copy(r, kc):
        return remote(ysend.at[r - 1, kc], yrecv.at[r - 1, kc], ys.at[r - 1, kc],
                      yr.at[r - 1, kc], at(y - r, x, core))

    def dq_copy(col, side):
        return remote(dqsend.at[col, side], dqrecv.at[x, core], ds.at[col, side],
                      dr.at[x, core], at(y, col, side))

    def settle(n):
        r = depth - n // CHIPS
        kc = n % CHIPS
        slot = r * CHIPS + kc
        x_copy(slot).wait_recv()
        kv_sum = kv_acc[slot, core] + xrecv[slot]

        @pl.when(r > 0)
        def _():
            ysend[r - 1, kc] = kv_sum.astype(jnp.bfloat16)
            y_copy(r, kc).start()

        @pl.when(r == 0)
        def _():
            xrecv[slot] = kv_sum

    def second(n, c):
        r = depth - n // CHIPS
        kc = n % CHIPS
        slot = r * CHIPS + kc
        v_both = jnp.concatenate([vbuf[0, slot], vbuf[1, slot]], axis=0)

        def tile(qc, sums):
            dk, dv = sums
            place = qc * (back * CHIPS + 1) + r * CHIPS + qc - kc
            dp = nn(v_both, do_t[qc])
            p = e_all[place] * r_all[place]
            p_low = p.astype(jnp.bfloat16)
            s_low = (p * (dp - rd_h[qc])).astype(jnp.bfloat16)
            dq_t[qc] += nn(k_t[slot], s_low)
            return dk + nn(s_low, q_h[qc]), dv + nn(p_low, do_h[qc])

        low = jnp.where(r == 0, kc, 0)
        high = jnp.where(r == back, kc + 1, CHIPS)
        zero = jnp.zeros((span, hw), jnp.float32)
        dk, dv = lax.fori_loop(low, high, tile, (zero, zero))
        dk = dk * SCALE
        for side in range(2):
            kv_acc[slot, side, 0] = dk[side * tok:(side + 1) * tok]
            kv_acc[slot, side, 1] = dv[side * tok:(side + 1) * tok]
        x_copy(slot).start()

        @pl.when(n > 0)
        def _():
            settle(n - 1)

        @pl.when(r == 0)
        def _():
            for g in range(PAIR):
                cols = slice(g * hw, (g + 1) * hw)
                piece = jnp.transpose(
                    dq_t[kc, :, g * span:(g + 1) * span] * SCALE).astype(jnp.bfloat16)
                dqsend[kc, 0, :, cols] = piece[:tok]
                dqsend[kc, 1, :, cols] = piece[tok:]
            for side in range(2):
                @pl.when((kc != x) | (core != side))
                def _():
                    dq_copy(kc, side).start()

        return c

    blocks = (depth + 1) * CHIPS
    lax.fori_loop(0, blocks, second, 0)
    settle(blocks - 1)

    def f_copy(col):
        return remote(fsend.at[col], frecv.at[x], fs.at[col], fr.at[x], at(y, col, core))

    def deliver(kc, c):
        def more(r, t):
            remote(ysend.at[0, 0], yrecv.at[r - 1, kc], ys.at[0, 0], yr.at[r - 1, kc],
                   partner).wait_recv()
            return t + yrecv[r - 1, kc].astype(jnp.float32)

        fsend[kc] = lax.fori_loop(1, reach + 1, more, xrecv[kc]).astype(jnp.bfloat16)

        @pl.when(kc != x)
        def _():
            f_copy(kc).start()

        return c

    lax.fori_loop(0, CHIPS, deliver, 0)

    frecv[x] = fsend[x]
    dqrecv[x, core] = dqsend[x, core]
    dq_from = lambda col, side: remote(
        dqsend.at[0, 0], dqrecv.at[col, side], ds.at[0, 0], dr.at[col, side], partner)
    dq_from(x, other).wait_recv()
    for dx in REMOTE:
        for side in range(2):
            dq_from(turn(dx), side).wait_recv()
    for col in range(CHIPS):
        for side in range(2):
            start = (col * 2 + side) * width
            dq_out[:, start:start + width] = dqrecv[col, side]
    for dx in REMOTE:
        remote(fsend.at[0], frecv.at[turn(dx)], fs.at[0], fr.at[turn(dx)], partner).wait_recv()
    for col in range(CHIPS):
        cols = slice(col * hw, (col + 1) * hw)
        dk_out[:, cols] = frecv[col, 0]
        dv_out[:, cols] = frecv[col, 1]

    q_copy(0, other).wait_send()
    do_copy(0, other).wait_send()
    rd_copy(0, other).wait_send()
    dq_copy(x, other).wait_send()
    for dx in REMOTE:
        k_copy(dx).wait_send()
        v_copy(dx).wait_send()
        f_copy(turn(dx)).wait_send()
        for side in range(2):
            q_copy(dx, side).wait_send()
            do_copy(dx, side).wait_send()
            rd_copy(dx, side).wait_send()
            dq_copy(turn(dx), side).wait_send()

    def sent_rows(r, c):
        k_row(r).wait_send()
        v_row(r).wait_send()
        return c

    def sent_on_chip(r, c):
        k_pass(r, core).wait_send()
        v_pass(r, core).wait_send()
        for kc in range(CHIPS):
            x_copy(r * CHIPS + kc).wait_send()
        return c

    def sent_terms(r, c):
        for kc in range(CHIPS):
            y_copy(r, kc).wait_send()
        return c

    lax.fori_loop(1, reach + 1, sent_rows, 0)
    lax.fori_loop(0, depth + 1, sent_on_chip, 0)
    lax.fori_loop(1, depth + 1, sent_terms, 0)


def on_device(seq_size, query, keys, values, output_gradient, forward_output, doc_ids):
    tok = query.shape[1]
    span = 2 * tok
    hw = HEAD_WIDTH
    width = PAIR * hw
    rows = seq_size // (2 * CHIPS)
    back = LONGEST // (CHIPS * span)
    slots = (back + 1) * CHIPS
    places = CHIPS * (back * CHIPS + 1)
    far = max(back, 1)
    bf, f32 = jnp.bfloat16, jnp.float32
    vmem = pl.BlockSpec(memory_space=pltpu.VMEM)
    dma = pltpu.SemaphoreType.DMA
    grad_query, grad_keys, grad_values = pl.pallas_call(
        functools.partial(kernel, rows, back),
        out_shape=(
            jax.ShapeDtypeStruct((tok, query.shape[2]), bf),
            jax.ShapeDtypeStruct((tok, keys.shape[2]), bf),
            jax.ShapeDtypeStruct((tok, keys.shape[2]), bf),
        ),
        in_specs=[vmem] * 6,
        out_specs=(vmem,) * 3,
        scratch_shapes=[
            pltpu.VMEM((CHIPS, tok + DOC_ROWS, hw), bf),
            pltpu.VMEM((2, slots, tok + DOC_ROWS, hw), bf),
            pltpu.VMEM((2, slots, tok, hw), bf),
            pltpu.VMEM((slots, span, 2 * hw), bf),
            pltpu.VMEM((slots, hw, span), bf),
            pltpu.VMEM((CHIPS, 2, 8, tok), f32),
            pltpu.VMEM((CHIPS, 2, tok, width), bf),
            pltpu.VMEM((CHIPS, 2, tok, width), bf),
            pltpu.VMEM((CHIPS, 2, 8, tok), f32),
            pltpu.VMEM((CHIPS, 2 * hw, PAIR * span), bf),
            pltpu.VMEM((CHIPS, PAIR * span, hw), bf),
            pltpu.VMEM((CHIPS, hw, PAIR * span), bf),
            pltpu.VMEM((CHIPS, PAIR * span, hw), bf),
            pltpu.VMEM((CHIPS, 1, PAIR * span), f32),
            pltpu.VMEM((places, span, PAIR * span), f32),
            pltpu.VMEM((places, 1, PAIR * span), f32),
            pltpu.VMEM((places, 1, PAIR * span), f32),
            pltpu.VMEM((places, 1, PAIR * span), f32),
            pltpu.VMEM((CHIPS, hw, PAIR * span), f32),
            pltpu.VMEM((slots, 2, 2, tok, hw), f32),
            pltpu.VMEM((slots, 2, tok, hw), f32),
            pltpu.VMEM((far, CHIPS, 2, tok, hw), bf),
            pltpu.VMEM((far, CHIPS, 2, tok, hw), bf),
            pltpu.VMEM((CHIPS, 2, tok, hw), bf),
            pltpu.VMEM((CHIPS, 2, tok, hw), bf),
            pltpu.VMEM((CHIPS, 2, tok, width), bf),
            pltpu.VMEM((CHIPS, 2, tok, width), bf),
            dma((CHIPS,)), dma((CHIPS,)), dma((CHIPS,)), dma((CHIPS,)),
            dma((CHIPS, 2)), dma((CHIPS, 2)), dma((CHIPS, 2)), dma((CHIPS, 2)),
            dma((CHIPS, 2)), dma((CHIPS, 2)),
            dma((back + 1,)), dma((back + 1,)), dma((back + 1,)), dma((back + 1,)),
            dma((back + 1,)), dma((back + 1,)), dma((back + 1,)), dma((back + 1,)),
            dma((slots,)), dma((slots,)), dma((far, CHIPS)), dma((far, CHIPS)),
            dma((CHIPS,)), dma((CHIPS,)), dma((CHIPS, 2)), dma((CHIPS, 2)),
        ],
        compiler_params=pltpu.CompilerParams(
            collective_id=0, has_side_effects=True, vmem_limit_bytes=56 * 1024 * 1024,
        ),
    )(query[0], keys[0], values[0], output_gradient[0], forward_output[0], doc_ids)
    return grad_query[None], grad_keys[None], grad_values[None]


def solution(mesh):
    wide = P("dp", "seq", None)
    return jax.shard_map(
        functools.partial(on_device, mesh.shape["seq"]),
        mesh=mesh,
        in_specs=(wide, wide, wide, wide, wide, P("dp", "seq")),
        out_specs=(wide, wide, wide),
        check_vma=False,
    )
```

```python
import functools
import math

import jax
import jax.numpy as jnp
from jax import lax
from jax.experimental import pallas as pl
from jax.experimental.pallas import tpu as pltpu
from jax.sharding import PartitionSpec as P

HEAD_WIDTH = 128
LONGEST = 2048
DOC_ROWS = 16
MASKED_LOW = -1e30
SCALE = 1.0 / math.sqrt(HEAD_WIDTH)
LOG2_SCALE = SCALE * math.log2(math.e)
CHIPS = 4
PAIR = 2


def nn(a, b):
    return jnp.dot(a, b, preferred_element_type=jnp.float32)


def kernel(
    rows, back,
    q_ref, k_ref, v_ref, do_ref, o_ref, id_ref,
    dq_out, dk_out, dv_out,
    ksend, kbuf, vbuf, k_x, k_t,
    rdsend, qbuf, dobuf, rdbuf, q_x, q_h, do_t, do_h, rd_h,
    e_all, m_all, p_low, s_low, dq_t,
    kv_acc, xrecv, ysend, yrecv, fsend, frecv, dqsend, dqrecv,
    ks, kr, vs, vr, qs, qr, gs, gr, rs, rr,
    kps, kpr, vps, vpr, kys, kyr, vys, vyr,
    xs, xr, ys, yr, fs, fr, ds, dr,
):
    tok = q_ref.shape[0]
    span = 2 * tok
    width = PAIR * HEAD_WIDTH
    hw = HEAD_WIDTH
    steps = back * CHIPS // 2 + 1
    me = lax.axis_index("seq")
    core = me % 2
    other = 1 - core
    x = (me // 2) % CHIPS
    y = me // (2 * CHIPS)
    mate = x + 1 - 2 * (x % 2)
    near, far = (mate + 2) % CHIPS, (x + 2) % CHIPS
    depth = jnp.minimum(y, back)
    reach = jnp.minimum(rows - 1 - y, back)

    def at(row, col, side):
        return {"seq": (row * CHIPS + col) * 2 + side}

    partner = at(y, x, other)

    barrier = pltpu.get_barrier_semaphore()
    pl.semaphore_signal(barrier, inc=1, device_id=partner)
    for col in (mate, near, far):
        for side in range(2):
            pl.semaphore_signal(barrier, inc=1, device_id=at(y, col, side))

    def greet_back(r, c):
        pl.semaphore_signal(barrier, inc=1, device_id=at(y - r, x, core))
        return c

    def greet_fwd(r, c):
        pl.semaphore_signal(barrier, inc=1, device_id=at(y + r, x, core))
        return c

    lax.fori_loop(1, depth + 1, greet_back, 0)
    lax.fori_loop(1, reach + 1, greet_fwd, 0)

    def feats(head, count):
        return pl.ds(pl.multiple_of(head * hw, hw), count * hw)

    def pair_cols(col, side):
        return feats(col * 2 * PAIR + side * PAIR, PAIR)

    doc_rows = lax.broadcasted_iota(jnp.int32, (DOC_ROWS, tok), 0)
    barred = jnp.where(doc_rows == id_ref[...], 0.0, MASKED_LOW).astype(jnp.bfloat16)
    for col in range(CHIPS):
        ksend[col, :tok, :] = k_ref[:, col * hw:(col + 1) * hw]
        ksend[col, tok:, :] = barred
    kbuf[core, x] = ksend[x]
    vbuf[core, x] = v_ref[:, feats(x, 1)]
    qbuf[x, core] = q_ref[:, pair_cols(x, core)]
    dobuf[x, core] = do_ref[:, pair_cols(x, core)]

    pl.semaphore_wait(barrier, 2 * CHIPS - 1 + depth + reach)

    def remote(src, dst, send, recv, target):
        return pltpu.make_async_remote_copy(
            src_ref=src, dst_ref=dst, send_sem=send, recv_sem=recv, device_id=target)

    def k_copy(col):
        return remote(ksend.at[col], kbuf.at[core, x], ks.at[col], kr.at[x], at(y, col, core))

    def v_copy(col):
        return remote(v_ref.at[:, feats(col, 1)], vbuf.at[core, x], vs.at[col], vr.at[x],
                      at(y, col, core))

    def q_copy(col, side):
        return remote(q_ref.at[:, pair_cols(col, side)], qbuf.at[x, core],
                      qs.at[col, side], qr.at[x, core], at(y, col, side))

    def do_copy(col, side):
        return remote(do_ref.at[:, pair_cols(col, side)], dobuf.at[x, core],
                      gs.at[col, side], gr.at[x, core], at(y, col, side))

    def rd_copy(col, side):
        return remote(rdsend.at[col, side], rdbuf.at[x, core],
                      rs.at[col, side], rr.at[x, core], at(y, col, side))

    def k_from(col):
        return remote(ksend.at[0], kbuf.at[core, col], ks.at[0], kr.at[col], partner)

    def v_from(col):
        return remote(v_ref.at[:, :hw], vbuf.at[core, col], vs.at[0], vr.at[col], partner)

    def q_from(col, side):
        return remote(q_ref.at[:, :width], qbuf.at[col, side], qs.at[0, 0], qr.at[col, side],
                      partner)

    def do_from(col, side):
        return remote(do_ref.at[:, :width], dobuf.at[col, side], gs.at[0, 0], gr.at[col, side],
                      partner)

    def rd_from(col, side):
        return remote(rdsend.at[0, 0], rdbuf.at[col, side], rs.at[0, 0], rr.at[col, side], partner)

    def row_of(r):
        return pl.ds(r * CHIPS, CHIPS)

    def k_pass(r, side):
        return remote(kbuf.at[side, row_of(r)], kbuf.at[side, row_of(r)], kps.at[r], kpr.at[r],
                      partner)

    def v_pass(r, side):
        return remote(vbuf.at[side, row_of(r)], vbuf.at[side, row_of(r)], vps.at[r], vpr.at[r],
                      partner)

    def k_row(r, target):
        return remote(kbuf.at[core, row_of(0)], kbuf.at[core, row_of(r)], kys.at[r], kyr.at[r],
                      target)

    def v_row(r, target):
        return remote(vbuf.at[core, row_of(0)], vbuf.at[core, row_of(r)], vys.at[r], vyr.at[r],
                      target)

    for col in (mate, far, near):
        k_copy(col).start()
    q_copy(x, other).start()
    for col in (mate, near):
        for side in range(2):
            q_copy(col, side).start()
    for col in (mate, far, near):
        v_copy(col).start()
    do_copy(x, other).start()
    for col in (mate, near):
        for side in range(2):
            do_copy(col, side).start()

    for col in range(CHIPS):
        for side in range(2):
            for g in range(PAIR):
                h = (col * 2 + side) * PAIR + g
                cols = slice(h * hw, (h + 1) * hw)
                prod = do_ref[:, cols].astype(jnp.float32) * o_ref[:, cols].astype(jnp.float32)
                rdsend[col, side, g:g + 1, :] = jnp.sum(
                    jnp.transpose(prod), axis=0, keepdims=True)
            rdsend[col, side, PAIR:, :] = jnp.zeros((8 - PAIR, tok), jnp.float32)
    rdbuf[x, core] = rdsend[x, core]
    rd_copy(x, other).start()
    for col in (mate, near, far):
        for side in range(2):
            rd_copy(col, side).start()
    kv_acc[...] = jnp.zeros(kv_acc.shape, jnp.float32)
    dq_t[...] = jnp.zeros(dq_t.shape, jnp.float32)

    def start_k_row(r, c):
        k_row(r, at(y + r, x, core)).start()
        return c

    def start_v_row(r, c):
        v_row(r, at(y + r, x, core)).start()
        return c

    def build_keys(r):
        def one(i, c):
            slot = r * CHIPS + i
            both = jnp.concatenate([kbuf[0, slot, :tok, :], kbuf[1, slot, :tok, :]], axis=0)
            bars = jnp.concatenate([kbuf[0, slot, tok:, :], kbuf[1, slot, tok:, :]], axis=1)
            pad = jnp.zeros((hw - DOC_ROWS, span), jnp.bfloat16)
            k_x[slot, :, :hw] = both
            k_x[slot, :, hw:] = jnp.transpose(jnp.concatenate([bars, pad], axis=0))
            k_t[slot] = jnp.transpose(both)
            return c

        lax.fori_loop(0, CHIPS, one, 0)

    for col in (mate, near, far):
        k_from(col).wait_recv()
    k_pass(0, core).start()
    lax.fori_loop(1, reach + 1, start_k_row, 0)
    k_pass(0, other).wait_recv()
    build_keys(0)

    tiles = [(c, g, slice((c * PAIR + g) * span, (c * PAIR + g + 1) * span))
             for c in range(2) for g in range(PAIR)]

    def x_copy(slot):
        return remote(kv_acc.at[slot, other], xrecv.at[slot], xs.at[slot], xr.at[slot], partner)

    def y_copy(r, kc):
        return remote(ysend.at[r - 1, kc], yrecv.at[r - 1, kc], ys.at[r - 1, kc],
                      yr.at[r - 1, kc], at(y - r, x, core))

    def dq_copy(col, side):
        return remote(dqsend.at[col, side], dqrecv.at[x, core], ds.at[col, side],
                      dr.at[x, core], at(y, col, side))

    def slot_of(block, u):
        chip = 2 * block + 1 - u
        return (y - chip // CHIPS) * CHIPS + chip % CHIPS

    def settle(block):
        for u in range(2):
            slot = slot_of(block, u)
            r, kc = slot // CHIPS, slot % CHIPS
            x_copy(slot).wait_recv()
            kv_sum = kv_acc[slot, core] + xrecv[slot]

            @pl.when(r > 0)
            def _():
                ysend[r - 1, kc] = kv_sum.astype(jnp.bfloat16)
                y_copy(r, kc).start()

            @pl.when(r == 0)
            def _():
                xrecv[slot] = kv_sum

    def pair_of_chunks(p, carry):
        a = (x // 2 + p) % 2
        b = 1 - a
        top = 2 * y + a
        count = jnp.minimum(top + 1, steps)

        for c in range(2):
            qc = 2 * a + c
            for side in range(2):
                @pl.when((qc != x) | (core != side))
                def _():
                    q_from(qc, side).wait_recv()
        for c, g, cols in tiles:
            qc = 2 * a + c
            head = slice(g * hw, (g + 1) * hw)
            both = jnp.concatenate([qbuf[qc, 0, :, head], qbuf[qc, 1, :, head]], axis=0)
            q_h[a, cols, :] = both
            q_x[a, :hw, cols] = jnp.transpose(both)
            bars = jnp.concatenate([kbuf[0, qc, tok:, :], kbuf[1, qc, tok:, :]], axis=1)
            q_x[a, hw:hw + DOC_ROWS, cols] = jnp.where(
                bars.astype(jnp.float32) == 0.0, 1.0, 0.0).astype(jnp.bfloat16)
        q_x[a, hw + DOC_ROWS:, :] = jnp.zeros((hw - DOC_ROWS, 2 * PAIR * span), jnp.bfloat16)

        def powers(t, stats, causal):
            out = []
            for (c, g, cols), (m_run, l_run) in zip(tiles, stats):
                for u in range(2):
                    s = nn(k_x[slot_of(top - t, u)], q_x[a, :, cols])
                    if causal and 1 - u == c:
                        key_pos = lax.broadcasted_iota(jnp.int32, (span, span), 0)
                        query_pos = lax.broadcasted_iota(jnp.int32, (span, span), 1)
                        s = jnp.where(key_pos <= query_pos, s, MASKED_LOW)
                    elif causal and 1 - u > c:
                        s = jnp.full((span, span), MASKED_LOW, jnp.float32)
                    m = jnp.max(s, axis=0, keepdims=True)
                    e = jnp.exp2((s - m) * LOG2_SCALE)
                    e_all[2 * t + u, :, cols] = e
                    m_all[2 * t + u, :, cols] = m
                    l = jnp.sum(e, axis=0, keepdims=True)
                    m_new = jnp.maximum(m_run, m)
                    l_run = (l_run * jnp.exp2((m_run - m_new) * LOG2_SCALE)
                             + l * jnp.exp2((m - m_new) * LOG2_SCALE))
                    m_run = m_new
                out.append((m_run, l_run))
            return tuple(out)

        def later_powers(t, stats):
            block = top - t
            r = y - block // 2

            @pl.when((p == 0) & (r > 0) & (block % 2 == 1))
            def _():
                k_row(r, partner).wait_recv()
                k_pass(r, core).start()
                k_pass(r, other).wait_recv()
                build_keys(r)

            return powers(t, stats, False)

        start = tuple((jnp.full((1, span), MASKED_LOW, jnp.float32),
                       jnp.zeros((1, span), jnp.float32)) for _ in tiles)
        stats = powers(0, start, True)

        @pl.when(p == 0)
        def _():
            for col in (mate, near, far):
                v_from(col).wait_recv()
            v_pass(0, core).start()
            lax.fori_loop(1, reach + 1, start_v_row, 0)

        stats = lax.fori_loop(1, count, later_powers, stats)
        m_top = jnp.concatenate([m for m, _ in stats], axis=1)
        inverse = 1.0 / jnp.concatenate([l for _, l in stats], axis=1)

        for c in range(2):
            qc = 2 * a + c
            for side in range(2):
                @pl.when((qc != x) | (core != side))
                def _():
                    do_from(qc, side).wait_recv()
                    rd_from(qc, side).wait_recv()

        @pl.when(p == 0)
        def _():
            for side in range(2):
                q_copy(far, side).start()
            for side in range(2):
                do_copy(far, side).start()
            v_pass(0, other).wait_recv()

        for c, g, cols in tiles:
            qc = 2 * a + c
            head = slice(g * hw, (g + 1) * hw)
            both = jnp.concatenate([dobuf[qc, 0, :, head], dobuf[qc, 1, :, head]], axis=0)
            do_h[a, cols, :] = both
            do_t[a, :, cols] = jnp.transpose(both)
            rd_h[a, :, cols] = jnp.concatenate(
                [rdbuf[qc, 0, g:g + 1, :], rdbuf[qc, 1, g:g + 1, :]], axis=1)

        def is_last(block):
            return (p == 1) | (block > 2 * y + b) | (block < 2 * y + b - steps + 1)

        def index(n):
            return jnp.where(p == 0, n, count - 1 - n)

        def terms(n, c):
            t = index(n)
            block = top - t
            r = y - block // 2

            @pl.when((p == 0) & (r > 0) & ((block % 2 == 1) | (n == 0)))
            def _():
                v_row(r, partner).wait_recv()
                v_pass(r, core).start()
                v_pass(r, other).wait_recv()

            for u in range(2):
                slot = slot_of(block, u)
                v_both = jnp.concatenate([vbuf[0, slot], vbuf[1, slot]], axis=0)
                ratio = jnp.exp2((m_all[2 * t + u] - m_top) * LOG2_SCALE) * inverse
                for _, _, cols in tiles:
                    dp = nn(v_both, do_t[a, :, cols])
                    pr = e_all[2 * t + u, :, cols] * ratio[:, cols]
                    p_low[u, :, cols] = pr.astype(jnp.bfloat16)
                    s_low[u, :, cols] = (pr * (dp - rd_h[a, :, cols])).astype(jnp.bfloat16)
                dv = nn(p_low[u], do_h[a])
                dk = nn(s_low[u], q_h[a]) * SCALE
                for side in range(2):
                    kv_acc[slot, side, 0] += dk[side * tok:(side + 1) * tok]
                    kv_acc[slot, side, 1] += dv[side * tok:(side + 1) * tok]
            dq_t[a] += nn(k_t[slot_of(block, 0)], s_low[0]) + nn(k_t[slot_of(block, 1)], s_low[1])

            @pl.when(is_last(block))
            def _():
                for u in range(2):
                    x_copy(slot_of(block, u)).start()

            @pl.when((n > 0) & is_last(top - index(n - 1)))
            def _():
                settle(top - index(n - 1))

            return c

        lax.fori_loop(0, count, terms, 0)

        @pl.when(is_last(top - index(count - 1)))
        def _():
            settle(top - index(count - 1))

        for c, g, cols in tiles:
            qc = 2 * a + c
            piece = jnp.transpose(dq_t[a, :, cols] * SCALE).astype(jnp.bfloat16)
            head = slice(g * hw, (g + 1) * hw)
            dqsend[qc, 0, :, head] = piece[:tok]
            dqsend[qc, 1, :, head] = piece[tok:]
        for c in range(2):
            qc = 2 * a + c
            for side in range(2):
                @pl.when((qc != x) | (core != side))
                def _():
                    dq_copy(qc, side).start()

        return carry

    lax.fori_loop(0, 2, pair_of_chunks, 0)

    def f_copy(col):
        return remote(fsend.at[col], frecv.at[x], fs.at[col], fr.at[x], at(y, col, core))

    def deliver(kc, c):
        def more(r, t):
            remote(ysend.at[0, 0], yrecv.at[r - 1, kc], ys.at[0, 0], yr.at[r - 1, kc],
                   partner).wait_recv()
            return t + yrecv[r - 1, kc].astype(jnp.float32)

        fsend[kc] = lax.fori_loop(1, reach + 1, more, xrecv[kc]).astype(jnp.bfloat16)

        @pl.when(kc != x)
        def _():
            f_copy(kc).start()

        return c

    lax.fori_loop(0, CHIPS, deliver, 0)

    frecv[x] = fsend[x]
    dqrecv[x, core] = dqsend[x, core]

    def dq_from(col, side):
        return remote(dqsend.at[0, 0], dqrecv.at[col, side], ds.at[0, 0], dr.at[col, side], partner)

    dq_from(x, other).wait_recv()
    for col in (mate, near, far):
        for side in range(2):
            dq_from(col, side).wait_recv()
    for col in range(CHIPS):
        for side in range(2):
            start = (col * 2 + side) * width
            dq_out[:, start:start + width] = dqrecv[col, side]
    for col in (mate, near, far):
        remote(fsend.at[0], frecv.at[col], fs.at[0], fr.at[col], partner).wait_recv()
    for col in range(CHIPS):
        cols = slice(col * hw, (col + 1) * hw)
        dk_out[:, cols] = frecv[col, 0]
        dv_out[:, cols] = frecv[col, 1]

    q_copy(x, other).wait_send()
    do_copy(x, other).wait_send()
    rd_copy(x, other).wait_send()
    dq_copy(x, other).wait_send()
    for col in (mate, near, far):
        k_copy(col).wait_send()
        v_copy(col).wait_send()
        f_copy(col).wait_send()
        for side in range(2):
            q_copy(col, side).wait_send()
            do_copy(col, side).wait_send()
            rd_copy(col, side).wait_send()
            dq_copy(col, side).wait_send()

    def sent_rows(r, c):
        k_row(r, partner).wait_send()
        v_row(r, partner).wait_send()
        return c

    def sent_on_chip(r, c):
        k_pass(r, core).wait_send()
        v_pass(r, core).wait_send()
        for kc in range(CHIPS):
            x_copy(r * CHIPS + kc).wait_send()
        return c

    def sent_terms(r, c):
        for kc in range(CHIPS):
            y_copy(r, kc).wait_send()
        return c

    lax.fori_loop(1, reach + 1, sent_rows, 0)
    lax.fori_loop(0, depth + 1, sent_on_chip, 0)
    lax.fori_loop(1, depth + 1, sent_terms, 0)


def on_device(seq_size, query, keys, values, output_gradient, forward_output, doc_ids):
    tok = query.shape[1]
    span = 2 * tok
    hw = HEAD_WIDTH
    width = PAIR * hw
    rows = seq_size // (2 * CHIPS)
    back = LONGEST // (CHIPS * span)
    slots = (back + 1) * CHIPS
    places = back * CHIPS + 2
    wide = 2 * PAIR * span
    far = max(back, 1)
    bf, f32 = jnp.bfloat16, jnp.float32
    vmem = pl.BlockSpec(memory_space=pltpu.VMEM)
    dma = pltpu.SemaphoreType.DMA
    grad_query, grad_keys, grad_values = pl.pallas_call(
        functools.partial(kernel, rows, back),
        out_shape=(
            jax.ShapeDtypeStruct((tok, query.shape[2]), bf),
            jax.ShapeDtypeStruct((tok, keys.shape[2]), bf),
            jax.ShapeDtypeStruct((tok, keys.shape[2]), bf),
        ),
        in_specs=[vmem] * 6,
        out_specs=(vmem,) * 3,
        scratch_shapes=[
            pltpu.VMEM((CHIPS, tok + DOC_ROWS, hw), bf),
            pltpu.VMEM((2, slots, tok + DOC_ROWS, hw), bf),
            pltpu.VMEM((2, slots, tok, hw), bf),
            pltpu.VMEM((slots, span, 2 * hw), bf),
            pltpu.VMEM((slots, hw, span), bf),
            pltpu.VMEM((CHIPS, 2, 8, tok), f32),
            pltpu.VMEM((CHIPS, 2, tok, width), bf),
            pltpu.VMEM((CHIPS, 2, tok, width), bf),
            pltpu.VMEM((CHIPS, 2, 8, tok), f32),
            pltpu.VMEM((2, 2 * hw, wide), bf),
            pltpu.VMEM((2, wide, hw), bf),
            pltpu.VMEM((2, hw, wide), bf),
            pltpu.VMEM((2, wide, hw), bf),
            pltpu.VMEM((2, 1, wide), f32),
            pltpu.VMEM((places, span, wide), f32),
            pltpu.VMEM((places, 1, wide), f32),
            pltpu.VMEM((2, span, wide), bf),
            pltpu.VMEM((2, span, wide), bf),
            pltpu.VMEM((2, hw, wide), f32),
            pltpu.VMEM((slots, 2, 2, tok, hw), f32),
            pltpu.VMEM((slots, 2, tok, hw), f32),
            pltpu.VMEM((far, CHIPS, 2, tok, hw), bf),
            pltpu.VMEM((far, CHIPS, 2, tok, hw), bf),
            pltpu.VMEM((CHIPS, 2, tok, hw), bf),
            pltpu.VMEM((CHIPS, 2, tok, hw), bf),
            pltpu.VMEM((CHIPS, 2, tok, width), bf),
            pltpu.VMEM((CHIPS, 2, tok, width), bf),
            dma((CHIPS,)), dma((CHIPS,)), dma((CHIPS,)), dma((CHIPS,)),
            dma((CHIPS, 2)), dma((CHIPS, 2)), dma((CHIPS, 2)), dma((CHIPS, 2)),
            dma((CHIPS, 2)), dma((CHIPS, 2)),
            dma((back + 1,)), dma((back + 1,)), dma((back + 1,)), dma((back + 1,)),
            dma((back + 1,)), dma((back + 1,)), dma((back + 1,)), dma((back + 1,)),
            dma((slots,)), dma((slots,)), dma((far, CHIPS)), dma((far, CHIPS)),
            dma((CHIPS,)), dma((CHIPS,)), dma((CHIPS, 2)), dma((CHIPS, 2)),
        ],
        compiler_params=pltpu.CompilerParams(
            collective_id=0, has_side_effects=True, vmem_limit_bytes=56 * 1024 * 1024,
        ),
    )(query[0], keys[0], values[0], output_gradient[0], forward_output[0], doc_ids)
    return grad_query[None], grad_keys[None], grad_values[None]


def solution(mesh):
    wide = P("dp", "seq", None)
    return jax.shard_map(
        functools.partial(on_device, mesh.shape["seq"]),
        mesh=mesh,
        in_specs=(wide, wide, wide, wide, wide, P("dp", "seq")),
        out_specs=(wide, wide, wide),
        check_vma=False,
    )
```

```python
import functools
import math

import jax
import jax.numpy as jnp
from jax import lax
from jax.experimental import pallas as pl
from jax.experimental.pallas import tpu as pltpu
from jax.sharding import PartitionSpec as P

HEAD_WIDTH = 128
LONGEST = 2048
DOC_ROWS = 16
MASKED_LOW = -1e30
SCALE = 1.0 / math.sqrt(HEAD_WIDTH)
LOG2_SCALE = SCALE * math.log2(math.e)
CHIPS = 4
PAIR = 2


def nn(a, b):
    return jnp.dot(a, b, preferred_element_type=jnp.float32)


def kernel(
    rows, back,
    q_ref, k_ref, v_ref, do_ref, o_ref, id_ref,
    dqrecv, frecv,
    ksend, kbuf, vbuf, k_x, k_t,
    rdsend, qbuf, dobuf, rdbuf, q_x, q_h, do_t, do_h, rd_h,
    e_all, m_all, top_all, inv_all, p_low, s_low, dq_t,
    kv_acc, xrecv, ysend, yrecv, fsend, dqsend,
    ks, kr, vs, vr, qs, qr, gs, gr, rs, rr,
    kps, kpr, vps, vpr, kys, kyr, vys, vyr,
    xs, xr, ys, yr, fs, fr, ds, dr,
):
    tok = q_ref.shape[0]
    span = 2 * tok
    width = PAIR * HEAD_WIDTH
    hw = HEAD_WIDTH
    steps = back * CHIPS // 2 + 1
    me = lax.axis_index("seq")
    core = me % 2
    other = 1 - core
    x = (me // 2) % CHIPS
    y = me // (2 * CHIPS)
    mate = x + 1 - 2 * (x % 2)
    near, far = (mate + 2) % CHIPS, (x + 2) % CHIPS
    depth = jnp.minimum(y, back)
    reach = jnp.minimum(rows - 1 - y, back)

    def at(row, col, side):
        return {"seq": (row * CHIPS + col) * 2 + side}

    partner = at(y, x, other)

    barrier = pltpu.get_barrier_semaphore()
    pl.semaphore_signal(barrier, inc=1, device_id=partner)
    for col in (mate, near, far):
        for side in range(2):
            pl.semaphore_signal(barrier, inc=1, device_id=at(y, col, side))

    def greet_back(r, c):
        pl.semaphore_signal(barrier, inc=1, device_id=at(y - r, x, core))
        return c

    def greet_fwd(r, c):
        pl.semaphore_signal(barrier, inc=1, device_id=at(y + r, x, core))
        return c

    lax.fori_loop(1, depth + 1, greet_back, 0)
    lax.fori_loop(1, reach + 1, greet_fwd, 0)

    def feats(head, count):
        return pl.ds(pl.multiple_of(head * hw, hw), count * hw)

    def pair_cols(col, side):
        return feats(col * 2 * PAIR + side * PAIR, PAIR)

    doc_rows = lax.broadcasted_iota(jnp.int32, (DOC_ROWS, tok), 0)
    barred = jnp.where(doc_rows == id_ref[...], 0.0, MASKED_LOW).astype(jnp.bfloat16)
    for col in range(CHIPS):
        ksend[col, :tok, :] = k_ref[:, col * hw:(col + 1) * hw]
        ksend[col, tok:, :] = barred
    kbuf[core, x] = ksend[x]
    vbuf[core, x] = v_ref[:, feats(x, 1)]
    qbuf[x, core] = q_ref[:, pair_cols(x, core)]
    dobuf[x, core] = do_ref[:, pair_cols(x, core)]

    pl.semaphore_wait(barrier, 2 * CHIPS - 1 + depth + reach)

    def remote(src, dst, send, recv, target):
        return pltpu.make_async_remote_copy(
            src_ref=src, dst_ref=dst, send_sem=send, recv_sem=recv, device_id=target)

    def k_copy(col):
        return remote(ksend.at[col], kbuf.at[core, x], ks.at[col], kr.at[x], at(y, col, core))

    def v_copy(col):
        return remote(v_ref.at[:, feats(col, 1)], vbuf.at[core, x], vs.at[col], vr.at[x],
                      at(y, col, core))

    def q_copy(col, side):
        return remote(q_ref.at[:, pair_cols(col, side)], qbuf.at[x, core],
                      qs.at[col, side], qr.at[x, core], at(y, col, side))

    def do_copy(col, side):
        return remote(do_ref.at[:, pair_cols(col, side)], dobuf.at[x, core],
                      gs.at[col, side], gr.at[x, core], at(y, col, side))

    def rd_copy(col, side):
        return remote(rdsend.at[col, side], rdbuf.at[x, core],
                      rs.at[col, side], rr.at[x, core], at(y, col, side))

    def k_from(col):
        return remote(ksend.at[0], kbuf.at[core, col], ks.at[0], kr.at[col], partner)

    def v_from(col):
        return remote(v_ref.at[:, :hw], vbuf.at[core, col], vs.at[0], vr.at[col], partner)

    def q_from(col, side):
        return remote(q_ref.at[:, :width], qbuf.at[col, side], qs.at[0, 0], qr.at[col, side],
                      partner)

    def do_from(col, side):
        return remote(do_ref.at[:, :width], dobuf.at[col, side], gs.at[0, 0], gr.at[col, side],
                      partner)

    def rd_from(col, side):
        return remote(rdsend.at[0, 0], rdbuf.at[col, side], rs.at[0, 0], rr.at[col, side], partner)

    def row_of(r):
        return pl.ds(r * CHIPS, CHIPS)

    def k_pass(r, side):
        return remote(kbuf.at[side, row_of(r)], kbuf.at[side, row_of(r)], kps.at[r], kpr.at[r],
                      partner)

    def v_pass(r, side):
        return remote(vbuf.at[side, row_of(r)], vbuf.at[side, row_of(r)], vps.at[r], vpr.at[r],
                      partner)

    def k_row(r, target):
        return remote(kbuf.at[core, row_of(0)], kbuf.at[core, row_of(r)], kys.at[r], kyr.at[r],
                      target)

    def v_row(r, target):
        return remote(vbuf.at[core, row_of(0)], vbuf.at[core, row_of(r)], vys.at[r], vyr.at[r],
                      target)

    for col in (mate, far, near):
        k_copy(col).start()
    for col in (mate, far, near):
        v_copy(col).start()
    def start_k_row(r, c):
        k_row(r, at(y + r, x, core)).start()
        return c

    def start_v_row(r, c):
        v_row(r, at(y + r, x, core)).start()
        return c

    def build_keys(r):
        def one(i, c):
            slot = r * CHIPS + i
            both = jnp.concatenate([kbuf[0, slot, :tok, :], kbuf[1, slot, :tok, :]], axis=0)
            bars = jnp.concatenate([kbuf[0, slot, tok:, :], kbuf[1, slot, tok:, :]], axis=1)
            pad = jnp.zeros((hw - DOC_ROWS, span), jnp.bfloat16)
            k_x[slot, :, :hw] = both
            k_x[slot, :, hw:] = jnp.transpose(jnp.concatenate([bars, pad], axis=0))
            k_t[slot] = jnp.transpose(both)
            return c

        lax.fori_loop(0, CHIPS, one, 0)

    for col in (mate, near, far):
        k_from(col).wait_recv()
    k_pass(0, core).start()
    lax.fori_loop(1, reach + 1, start_k_row, 0)
    for col in (mate, near, far):
        v_from(col).wait_recv()
    v_pass(0, core).start()
    lax.fori_loop(1, reach + 1, start_v_row, 0)
    q_copy(x, other).start()
    for col in (mate, near, far):
        for side in range(2):
            q_copy(col, side).start()

    for col in range(CHIPS):
        for side in range(2):
            for g in range(PAIR):
                h = (col * 2 + side) * PAIR + g
                cols = slice(h * hw, (h + 1) * hw)
                prod = do_ref[:, cols].astype(jnp.float32) * o_ref[:, cols].astype(jnp.float32)
                rdsend[col, side, g:g + 1, :] = jnp.sum(
                    jnp.transpose(prod), axis=0, keepdims=True)
            rdsend[col, side, PAIR:, :] = jnp.zeros((8 - PAIR, tok), jnp.float32)
    rdbuf[x, core] = rdsend[x, core]
    rd_copy(x, other).start()
    for col in (mate, near, far):
        for side in range(2):
            rd_copy(col, side).start()
    kv_acc[...] = jnp.zeros(kv_acc.shape, jnp.float32)
    dq_t[...] = jnp.zeros(dq_t.shape, jnp.float32)

    k_pass(0, other).wait_recv()
    build_keys(0)

    def pass_k_row(r, c):
        k_row(r, partner).wait_recv()
        k_pass(r, core).start()
        return c

    def have_k_row(r, c):
        k_pass(r, other).wait_recv()
        build_keys(r)
        return c

    def pass_v_row(r, c):
        v_row(r, partner).wait_recv()
        v_pass(r, core).start()
        return c

    def have_v_row(r, c):
        v_pass(r, other).wait_recv()
        return c

    lax.fori_loop(1, depth + 1, pass_k_row, 0)
    lax.fori_loop(1, depth + 1, have_k_row, 0)

    tiles = [(c, g, slice((c * PAIR + g) * span, (c * PAIR + g + 1) * span))
             for c in range(2) for g in range(PAIR)]

    def place_of(block):
        return (y - block // 2) * 2 + block % 2

    def x_copy(place):
        return remote(kv_acc.at[place, other], xrecv.at[place], xs.at[place], xr.at[place], partner)

    def y_copy(r, part):
        return remote(ysend.at[r - 1, part], yrecv.at[r - 1, part], ys.at[r - 1, part],
                      yr.at[r - 1, part], at(y - r, x, core))

    def dq_copy(col, side):
        return remote(dqsend.at[col, side], dqrecv.at[x, core], ds.at[col, side],
                      dr.at[x, core], at(y, col, side))

    def settle(block):
        place = place_of(block)
        r, part = place // 2, place % 2
        x_copy(place).wait_recv()
        kv_sum = kv_acc[place, core] + xrecv[place]

        @pl.when(r > 0)
        def _():
            ysend[r - 1, part] = kv_sum.astype(jnp.bfloat16)
            y_copy(r, part).start()

        @pl.when(r == 0)
        def _():
            xrecv[place] = kv_sum

    def chunks_of(p):
        a = (x // 2 + p) % 2
        top = 2 * y + a
        return a, top, jnp.minimum(top + 1, steps)

    def first_pass(p, carry):
        a, top, count = chunks_of(p)

        @pl.when(p == 1)
        def _():
            lax.fori_loop(1, depth + 1, pass_v_row, 0)

        for c in range(2):
            qc = 2 * a + c
            for side in range(2):
                @pl.when((qc != x) | (core != side))
                def _():
                    q_from(qc, side).wait_recv()
        @pl.when(p == 0)
        def _():
            do_copy(x, other).start()
            for col in (mate, near, far):
                for side in range(2):
                    do_copy(col, side).start()

        for c, g, cols in tiles:
            qc = 2 * a + c
            head = slice(g * hw, (g + 1) * hw)
            both = jnp.concatenate([qbuf[qc, 0, :, head], qbuf[qc, 1, :, head]], axis=0)
            q_h[a, cols, :] = both
            q_x[a, :hw, cols] = jnp.transpose(both)
            bars = jnp.concatenate([kbuf[0, qc, tok:, :], kbuf[1, qc, tok:, :]], axis=1)
            q_x[a, hw:hw + DOC_ROWS, cols] = jnp.where(
                bars.astype(jnp.float32) == 0.0, 1.0, 0.0).astype(jnp.bfloat16)
        q_x[a, hw + DOC_ROWS:, :] = jnp.zeros((hw - DOC_ROWS, 2 * PAIR * span), jnp.bfloat16)

        def powers(t, stats, causal):
            place = place_of(top - t)
            keys_x = k_x[pl.ds(2 * place, 2)].reshape(2 * span, 2 * hw)
            out = []
            for (c, g, cols), (m_run, l_run) in zip(tiles, stats):
                s = nn(keys_x, q_x[a, :, cols])
                if causal:
                    key_pos = lax.broadcasted_iota(jnp.int32, (2 * span, span), 0)
                    query_pos = lax.broadcasted_iota(jnp.int32, (2 * span, span), 1)
                    s = jnp.where(key_pos <= query_pos + c * span, s, MASKED_LOW)
                m = jnp.max(s, axis=0, keepdims=True)
                e = jnp.exp2((s - m) * LOG2_SCALE)
                e_all[a, t, :, cols] = e
                m_all[a, t, :, cols] = m
                l = jnp.sum(e, axis=0, keepdims=True)
                m_new = jnp.maximum(m_run, m)
                l_run = (l_run * jnp.exp2((m_run - m_new) * LOG2_SCALE)
                         + l * jnp.exp2((m - m_new) * LOG2_SCALE))
                out.append((m_new, l_run))
            return tuple(out)

        def later_powers(t, stats):
            return powers(t, stats, False)

        start = tuple((jnp.full((1, span), MASKED_LOW, jnp.float32),
                       jnp.zeros((1, span), jnp.float32)) for _ in tiles)
        stats = powers(0, start, True)
        stats = lax.fori_loop(1, count, later_powers, stats)
        top_all[a] = jnp.concatenate([m for m, _ in stats], axis=1)
        inv_all[a] = 1.0 / jnp.concatenate([l for _, l in stats], axis=1)
        return carry

    lax.fori_loop(0, 2, first_pass, 0)
    def take_gradients(p, carry):
        a = (x // 2 + p) % 2
        for c in range(2):
            qc = 2 * a + c
            for side in range(2):
                @pl.when((qc != x) | (core != side))
                def _():
                    do_from(qc, side).wait_recv()
                    rd_from(qc, side).wait_recv()
        for c, g, cols in tiles:
            qc = 2 * a + c
            head = slice(g * hw, (g + 1) * hw)
            both = jnp.concatenate([dobuf[qc, 0, :, head], dobuf[qc, 1, :, head]], axis=0)
            do_h[a, cols, :] = both
            do_t[a, :, cols] = jnp.transpose(both)
            rd_h[a, :, cols] = jnp.concatenate(
                [rdbuf[qc, 0, g:g + 1, :], rdbuf[qc, 1, g:g + 1, :]], axis=1)
        return carry

    lax.fori_loop(0, 2, take_gradients, 0)
    lax.fori_loop(0, depth + 1, have_v_row, 0)

    own = x // 2
    away = 1 - own
    low = 2 * y - 2 * back
    lead = 1 + away
    shared = 4 * back - 1

    def item(n):
        i = n - lead
        j = i - 1
        in_lead, in_tail = n < lead, i >= shared
        block = jnp.where(
            in_lead, 2 * y + n,
            jnp.where(in_tail, 2 * y + i - shared,
                      jnp.where(i == 0, low, low + 1 + j // 2)))
        a = jnp.where(
            in_lead, away,
            jnp.where(in_tail, own, jnp.where(i == 0, 0, jnp.where(j % 2 == 0, away, own))))
        final = jnp.where(in_lead, n == 1, in_tail | (i % 2 == 0))
        return a, block, final & (block >= 0)

    def send_queries(a):
        for c, g, cols in tiles:
            qc = 2 * a + c
            piece = jnp.transpose(dq_t[a, :, cols] * SCALE).astype(jnp.bfloat16)
            head = slice(g * hw, (g + 1) * hw)
            dqsend[qc, 0, :, head] = piece[:tok]
            dqsend[qc, 1, :, head] = piece[tok:]
        for c in range(2):
            qc = 2 * a + c
            for side in range(2):
                @pl.when((qc != x) | (core != side))
                def _():
                    dq_copy(qc, side).start()

    def terms(n, c):
        a, block, final = item(n)

        @pl.when(block >= 0)
        def _():
            t = 2 * y + a - block
            place = place_of(block)
            v_both = jnp.concatenate(
                [vbuf[i, 2 * place + u] for u in range(2) for i in range(2)], axis=0)
            ratio = jnp.exp2((m_all[a, t] - top_all[a]) * LOG2_SCALE) * inv_all[a]
            for _, _, cols in tiles:
                dp = nn(v_both, do_t[a, :, cols])
                pr = e_all[a, t, :, cols] * ratio[:, cols]
                p_low[:, cols] = pr.astype(jnp.bfloat16)
                s_low[:, cols] = (pr * (dp - rd_h[a, :, cols])).astype(jnp.bfloat16)
            dv = nn(p_low[...], do_h[a])
            dk = nn(s_low[...], q_h[a]) * SCALE
            for u in range(2):
                for side in range(2):
                    piece = slice((2 * u + side) * tok, (2 * u + side + 1) * tok)
                    kv_acc[place, side, u, 0] += dk[piece]
                    kv_acc[place, side, u, 1] += dv[piece]
            dq_t[a] += nn(jnp.concatenate([k_t[2 * place], k_t[2 * place + 1]], axis=1), s_low[...])

        @pl.when(final)
        def _():
            x_copy(place_of(block)).start()

        before, final_before = item(n - 1)[1:]

        @pl.when((n > 0) & final_before)
        def _():
            settle(before)

        @pl.when(n == lead + shared - 2)
        def _():
            send_queries(away)

        return c

    last = lead + shared + own
    lax.fori_loop(0, last + 1, terms, 0)
    send_queries(own)
    settle(item(last)[1])

    def f_copy(col):
        return remote(fsend.at[col], frecv.at[x], fs.at[col], fr.at[x], at(y, col, core))

    def deliver(part, c):
        def more(r, t):
            remote(ysend.at[0, 0], yrecv.at[r - 1, part], ys.at[0, 0], yr.at[r - 1, part],
                   partner).wait_recv()
            return t + yrecv[r - 1, part].astype(jnp.float32)

        both = lax.fori_loop(1, reach + 1, more, xrecv[part]).astype(jnp.bfloat16)
        for u in range(2):
            kc = 2 * part + u
            fsend[kc] = both[u]

            @pl.when(kc != x)
            def _():
                f_copy(kc).start()

        return c

    lax.fori_loop(0, 2, deliver, 0)

    frecv[x] = fsend[x]
    dqrecv[x, core] = dqsend[x, core]

    def dq_from(col, side):
        return remote(dqsend.at[0, 0], dqrecv.at[col, side], ds.at[0, 0], dr.at[col, side], partner)

    dq_from(x, other).wait_recv()
    for col in (mate, near, far):
        for side in range(2):
            dq_from(col, side).wait_recv()
    for col in (mate, near, far):
        remote(fsend.at[0], frecv.at[col], fs.at[0], fr.at[col], partner).wait_recv()
    q_copy(x, other).wait_send()
    do_copy(x, other).wait_send()
    rd_copy(x, other).wait_send()
    dq_copy(x, other).wait_send()
    for col in (mate, near, far):
        k_copy(col).wait_send()
        v_copy(col).wait_send()
        f_copy(col).wait_send()
        for side in range(2):
            q_copy(col, side).wait_send()
            do_copy(col, side).wait_send()
            rd_copy(col, side).wait_send()
            dq_copy(col, side).wait_send()

    def sent_rows(r, c):
        k_row(r, partner).wait_send()
        v_row(r, partner).wait_send()
        return c

    def sent_on_chip(r, c):
        k_pass(r, core).wait_send()
        v_pass(r, core).wait_send()
        for part in range(2):
            x_copy(r * 2 + part).wait_send()
        return c

    def sent_terms(r, c):
        for part in range(2):
            y_copy(r, part).wait_send()
        return c

    lax.fori_loop(1, reach + 1, sent_rows, 0)
    lax.fori_loop(0, depth + 1, sent_on_chip, 0)
    lax.fori_loop(1, depth + 1, sent_terms, 0)


def lay_out(dq_raw, kv_raw, dq_out, dk_out, dv_out):
    width = dq_raw.shape[3]
    hw = kv_raw.shape[3]
    for col in range(CHIPS):
        for side in range(2):
            start = (col * 2 + side) * width
            dq_out[0, :, start:start + width] = dq_raw[col, side]
        cols = slice(col * hw, (col + 1) * hw)
        dk_out[0, :, cols] = kv_raw[col, 0]
        dv_out[0, :, cols] = kv_raw[col, 1]


def on_device(seq_size, query, keys, values, output_gradient, forward_output, doc_ids):
    tok = query.shape[1]
    span = 2 * tok
    hw = HEAD_WIDTH
    width = PAIR * hw
    rows = seq_size // (2 * CHIPS)
    back = LONGEST // (CHIPS * span)
    slots = (back + 1) * CHIPS
    wide = 2 * PAIR * span
    far = max(back, 1)
    bf, f32 = jnp.bfloat16, jnp.float32
    vmem = pl.BlockSpec(memory_space=pltpu.VMEM)
    dma = pltpu.SemaphoreType.DMA
    dq_raw, kv_raw = pl.pallas_call(
        functools.partial(kernel, rows, back),
        out_shape=(
            jax.ShapeDtypeStruct((CHIPS, 2, tok, width), bf),
            jax.ShapeDtypeStruct((CHIPS, 2, tok, hw), bf),
        ),
        in_specs=[vmem] * 6,
        out_specs=(vmem,) * 2,
        scratch_shapes=[
            pltpu.VMEM((CHIPS, tok + DOC_ROWS, hw), bf),
            pltpu.VMEM((2, slots, tok + DOC_ROWS, hw), bf),
            pltpu.VMEM((2, slots, tok, hw), bf),
            pltpu.VMEM((slots, span, 2 * hw), bf),
            pltpu.VMEM((slots, hw, span), bf),
            pltpu.VMEM((CHIPS, 2, 8, tok), f32),
            pltpu.VMEM((CHIPS, 2, tok, width), bf),
            pltpu.VMEM((CHIPS, 2, tok, width), bf),
            pltpu.VMEM((CHIPS, 2, 8, tok), f32),
            pltpu.VMEM((2, 2 * hw, wide), bf),
            pltpu.VMEM((2, wide, hw), bf),
            pltpu.VMEM((2, hw, wide), bf),
            pltpu.VMEM((2, wide, hw), bf),
            pltpu.VMEM((2, 1, wide), f32),
            pltpu.VMEM((2, back * 2 + 1, 2 * span, wide), f32),
            pltpu.VMEM((2, back * 2 + 1, 1, wide), f32),
            pltpu.VMEM((2, 1, wide), f32),
            pltpu.VMEM((2, 1, wide), f32),
            pltpu.VMEM((2 * span, wide), bf),
            pltpu.VMEM((2 * span, wide), bf),
            pltpu.VMEM((2, hw, wide), f32),
            pltpu.VMEM((slots // 2, 2, 2, 2, tok, hw), f32),
            pltpu.VMEM((slots // 2, 2, 2, tok, hw), f32),
            pltpu.VMEM((far, 2, 2, 2, tok, hw), bf),
            pltpu.VMEM((far, 2, 2, 2, tok, hw), bf),
            pltpu.VMEM((CHIPS, 2, tok, hw), bf),
            pltpu.VMEM((CHIPS, 2, tok, width), bf),
            dma((CHIPS,)), dma((CHIPS,)), dma((CHIPS,)), dma((CHIPS,)),
            dma((CHIPS, 2)), dma((CHIPS, 2)), dma((CHIPS, 2)), dma((CHIPS, 2)),
            dma((CHIPS, 2)), dma((CHIPS, 2)),
            dma((back + 1,)), dma((back + 1,)), dma((back + 1,)), dma((back + 1,)),
            dma((back + 1,)), dma((back + 1,)), dma((back + 1,)), dma((back + 1,)),
            dma((slots // 2,)), dma((slots // 2,)), dma((far, 2)), dma((far, 2)),
            dma((CHIPS,)), dma((CHIPS,)), dma((CHIPS, 2)), dma((CHIPS, 2)),
        ],
        compiler_params=pltpu.CompilerParams(
            collective_id=0, has_side_effects=True, vmem_limit_bytes=56 * 1024 * 1024,
        ),
    )(query[0], keys[0], values[0], output_gradient[0], forward_output[0], doc_ids)
    return pl.pallas_call(
        lay_out,
        out_shape=(
            jax.ShapeDtypeStruct(query.shape, bf),
            jax.ShapeDtypeStruct(keys.shape, bf),
            jax.ShapeDtypeStruct(keys.shape, bf),
        ),
        in_specs=[vmem] * 2,
        out_specs=(vmem,) * 3,
    )(dq_raw, kv_raw)


def solution(mesh):
    wide = P("dp", "seq", None)
    return jax.shard_map(
        functools.partial(on_device, mesh.shape["seq"]),
        mesh=mesh,
        in_specs=(wide, wide, wide, wide, wide, P("dp", "seq")),
        out_specs=(wide, wide, wide),
        check_vma=False,
    )
```

```python
import functools
import math

import jax
import jax.numpy as jnp
from jax import lax
from jax.experimental import pallas as pl
from jax.experimental.pallas import tpu as pltpu
from jax.sharding import PartitionSpec as P

HEAD_WIDTH = 128
LONGEST = 2048
DOC_ROWS = 16
MASKED_LOW = -1e30
SCALE = 1.0 / math.sqrt(HEAD_WIDTH)
LOG2_SCALE = SCALE * math.log2(math.e)
CHIPS = 4
PAIR = 2


def nn(a, b):
    return jnp.dot(a, b, preferred_element_type=jnp.float32)


def kernel(
    rows, back,
    q_hbm, k_ref, v_ref, do_hbm, o_hbm, id_ref,
    dqrecv, frecv,
    q_ref, do_ref, o_ref, ksend, kbuf, vbuf, k_x, k_t,
    rdsend, qbuf, dobuf, rdbuf, q_x, q_h, do_t, do_h, rd_h,
    e_all, m_all, top_all, inv_all, p_low, s_low, dq_t,
    kv_acc, xrecv, ysend, yrecv, fsend, dqsend,
    ks, kr, vs, vr, qs, qr, gs, gr, rs, rr,
    kps, kpr, vps, vpr, kys, kyr, vys, vyr,
    xs, xr, ys, yr, fs, fr, ds, dr, ins,
):
    tok = q_ref.shape[0]
    span = 2 * tok
    width = PAIR * HEAD_WIDTH
    hw = HEAD_WIDTH
    steps = back * CHIPS // 2 + 1
    me = lax.axis_index("seq")
    core = me % 2
    other = 1 - core
    x = (me // 2) % CHIPS
    y = me // (2 * CHIPS)
    mate = x + 1 - 2 * (x % 2)
    near, far = (mate + 2) % CHIPS, (x + 2) % CHIPS
    depth = jnp.minimum(y, back)
    reach = jnp.minimum(rows - 1 - y, back)

    def at(row, col, side):
        return {"seq": (row * CHIPS + col) * 2 + side}

    partner = at(y, x, other)

    q_in = pltpu.make_async_copy(q_hbm, q_ref, ins.at[0])
    do_in = pltpu.make_async_copy(do_hbm, do_ref, ins.at[1])
    o_in = pltpu.make_async_copy(o_hbm, o_ref, ins.at[2])
    q_in.start()
    do_in.start()
    o_in.start()
    barrier = pltpu.get_barrier_semaphore()
    pl.semaphore_signal(barrier, inc=1, device_id=partner)
    for col in (mate, near, far):
        for side in range(2):
            pl.semaphore_signal(barrier, inc=1, device_id=at(y, col, side))

    def greet_back(r, c):
        pl.semaphore_signal(barrier, inc=1, device_id=at(y - r, x, core))
        return c

    def greet_fwd(r, c):
        pl.semaphore_signal(barrier, inc=1, device_id=at(y + r, x, core))
        return c

    lax.fori_loop(1, depth + 1, greet_back, 0)
    lax.fori_loop(1, reach + 1, greet_fwd, 0)

    def feats(head, count):
        return pl.ds(pl.multiple_of(head * hw, hw), count * hw)

    def pair_cols(col, side):
        return feats(col * 2 * PAIR + side * PAIR, PAIR)

    doc_rows = lax.broadcasted_iota(jnp.int32, (DOC_ROWS, tok), 0)
    barred = jnp.where(doc_rows == id_ref[...], 0.0, MASKED_LOW).astype(jnp.bfloat16)
    for col in range(CHIPS):
        ksend[col, :tok, :] = k_ref[:, col * hw:(col + 1) * hw]
        ksend[col, tok:, :] = barred
    kbuf[core, x] = ksend[x]
    vbuf[core, x] = v_ref[:, feats(x, 1)]

    pl.semaphore_wait(barrier, 2 * CHIPS - 1 + depth + reach)

    def remote(src, dst, send, recv, target):
        return pltpu.make_async_remote_copy(
            src_ref=src, dst_ref=dst, send_sem=send, recv_sem=recv, device_id=target)

    def k_copy(col):
        return remote(ksend.at[col], kbuf.at[core, x], ks.at[col], kr.at[x], at(y, col, core))

    def v_copy(col):
        return remote(v_ref.at[:, feats(col, 1)], vbuf.at[core, x], vs.at[col], vr.at[x],
                      at(y, col, core))

    def q_copy(col, side):
        return remote(q_ref.at[:, pair_cols(col, side)], qbuf.at[x, core],
                      qs.at[col, side], qr.at[x, core], at(y, col, side))

    def do_copy(col, side):
        return remote(do_ref.at[:, pair_cols(col, side)], dobuf.at[x, core],
                      gs.at[col, side], gr.at[x, core], at(y, col, side))

    def rd_copy(col, side):
        return remote(rdsend.at[col, side], rdbuf.at[x, core],
                      rs.at[col, side], rr.at[x, core], at(y, col, side))

    def k_from(col):
        return remote(ksend.at[0], kbuf.at[core, col], ks.at[0], kr.at[col], partner)

    def v_from(col):
        return remote(v_ref.at[:, :hw], vbuf.at[core, col], vs.at[0], vr.at[col], partner)

    def q_from(col, side):
        return remote(q_ref.at[:, :width], qbuf.at[col, side], qs.at[0, 0], qr.at[col, side],
                      partner)

    def do_from(col, side):
        return remote(do_ref.at[:, :width], dobuf.at[col, side], gs.at[0, 0], gr.at[col, side],
                      partner)

    def rd_from(col, side):
        return remote(rdsend.at[0, 0], rdbuf.at[col, side], rs.at[0, 0], rr.at[col, side], partner)

    def row_of(r):
        return pl.ds(r * CHIPS, CHIPS)

    def k_pass(r, side):
        return remote(kbuf.at[side, row_of(r)], kbuf.at[side, row_of(r)], kps.at[r], kpr.at[r],
                      partner)

    def v_pass(r, side):
        return remote(vbuf.at[side, row_of(r)], vbuf.at[side, row_of(r)], vps.at[r], vpr.at[r],
                      partner)

    def k_row(r, target):
        return remote(kbuf.at[core, row_of(0)], kbuf.at[core, row_of(r)], kys.at[r], kyr.at[r],
                      target)

    def v_row(r, target):
        return remote(vbuf.at[core, row_of(0)], vbuf.at[core, row_of(r)], vys.at[r], vyr.at[r],
                      target)

    for col in (mate, far, near):
        k_copy(col).start()
    for col in (mate, far, near):
        v_copy(col).start()
    def start_k_row(r, c):
        k_row(r, at(y + r, x, core)).start()
        return c

    def start_v_row(r, c):
        v_row(r, at(y + r, x, core)).start()
        return c

    def build_keys(r):
        def one(i, c):
            slot = r * CHIPS + i
            both = jnp.concatenate([kbuf[0, slot, :tok, :], kbuf[1, slot, :tok, :]], axis=0)
            bars = jnp.concatenate([kbuf[0, slot, tok:, :], kbuf[1, slot, tok:, :]], axis=1)
            pad = jnp.zeros((hw - DOC_ROWS, span), jnp.bfloat16)
            k_x[slot, :, :hw] = both
            k_x[slot, :, hw:] = jnp.transpose(jnp.concatenate([bars, pad], axis=0))
            k_t[slot] = jnp.transpose(both)
            return c

        lax.fori_loop(0, CHIPS, one, 0)

    q_in.wait()
    q_copy(x, other).start()
    q_copy(mate, core).start()
    for col in (mate, near, far):
        k_from(col).wait_recv()
    k_pass(0, core).start()
    lax.fori_loop(1, reach + 1, start_k_row, 0)
    for col in (mate, near, far):
        v_from(col).wait_recv()
    v_pass(0, core).start()
    lax.fori_loop(1, reach + 1, start_v_row, 0)
    for col in (near, far):
        for side in range(2):
            q_copy(col, side).start()
    q_copy(mate, other).start()
    qbuf[x, core] = q_ref[:, pair_cols(x, core)]
    do_in.wait()
    o_in.wait()
    dobuf[x, core] = do_ref[:, pair_cols(x, core)]

    for col in range(CHIPS):
        for side in range(2):
            for g in range(PAIR):
                h = (col * 2 + side) * PAIR + g
                cols = slice(h * hw, (h + 1) * hw)
                prod = do_ref[:, cols].astype(jnp.float32) * o_ref[:, cols].astype(jnp.float32)
                rdsend[col, side, g:g + 1, :] = jnp.sum(
                    jnp.transpose(prod), axis=0, keepdims=True)
            rdsend[col, side, PAIR:, :] = jnp.zeros((8 - PAIR, tok), jnp.float32)
    rdbuf[x, core] = rdsend[x, core]
    rd_copy(x, other).start()
    for col in (mate, near, far):
        for side in range(2):
            rd_copy(col, side).start()
    kv_acc[...] = jnp.zeros(kv_acc.shape, jnp.float32)
    dq_t[...] = jnp.zeros(dq_t.shape, jnp.float32)

    k_pass(0, other).wait_recv()
    build_keys(0)

    def pass_k_row(r, c):
        k_row(r, partner).wait_recv()
        k_pass(r, core).start()
        return c

    def have_k_row(r, c):
        k_pass(r, other).wait_recv()
        build_keys(r)
        return c

    def pass_v_row(r, c):
        v_row(r, partner).wait_recv()
        v_pass(r, core).start()
        return c

    def have_v_row(r, c):
        v_pass(r, other).wait_recv()
        return c

    @pl.when(depth > 0)
    def _():
        pass_k_row(1, 0)

    tiles = [(c, g, slice((c * PAIR + g) * span, (c * PAIR + g + 1) * span))
             for c in range(2) for g in range(PAIR)]

    def place_of(block):
        return (y - block // 2) * 2 + block % 2

    def x_copy(place):
        return remote(kv_acc.at[place, other], xrecv.at[place], xs.at[place], xr.at[place], partner)

    def y_copy(r, part):
        return remote(ysend.at[r - 1, part], yrecv.at[r - 1, part], ys.at[r - 1, part],
                      yr.at[r - 1, part], at(y - r, x, core))

    def dq_copy(col, side):
        return remote(dqsend.at[col, side], dqrecv.at[x, core], ds.at[col, side],
                      dr.at[x, core], at(y, col, side))

    def settle(block):
        place = place_of(block)
        r, part = place // 2, place % 2
        x_copy(place).wait_recv()
        kv_sum = kv_acc[place, core] + xrecv[place]

        @pl.when(r > 0)
        def _():
            ysend[r - 1, part] = kv_sum.astype(jnp.bfloat16)
            y_copy(r, part).start()

        @pl.when(r == 0)
        def _():
            xrecv[place] = kv_sum

    def chunks_of(p):
        a = (x // 2 + p) % 2
        top = 2 * y + a
        return a, top, jnp.minimum(top + 1, steps)

    def powers(a, top, t, stats, causal):
        place = place_of(top - t)
        keys_x = k_x[pl.ds(2 * place, 2)].reshape(2 * span, 2 * hw)
        out = []
        for (c, g, cols), (m_run, l_run) in zip(tiles, stats):
            s = nn(keys_x, q_x[a, :, cols])
            if causal:
                key_pos = lax.broadcasted_iota(jnp.int32, (2 * span, span), 0)
                query_pos = lax.broadcasted_iota(jnp.int32, (2 * span, span), 1)
                s = jnp.where(key_pos <= query_pos + c * span, s, MASKED_LOW)
            m = jnp.max(s, axis=0, keepdims=True)
            e = jnp.exp2((s - m) * LOG2_SCALE)
            e_all[a, t, :, cols] = e
            m_all[a, t, :, cols] = m
            l = jnp.sum(e, axis=0, keepdims=True)
            m_new = jnp.maximum(m_run, m)
            l_run = (l_run * jnp.exp2((m_run - m_new) * LOG2_SCALE)
                     + l * jnp.exp2((m - m_new) * LOG2_SCALE))
            out.append((m_new, l_run))
        return tuple(out)

    def keep(a, stats):
        top_all[a] = jnp.concatenate([m for m, _ in stats], axis=1)
        inv_all[a] = jnp.concatenate([l for _, l in stats], axis=1)

    def more_powers(a, top, start, stop):
        stats = tuple((top_all[a, :, cols], inv_all[a, :, cols]) for _, _, cols in tiles)
        keep(a, lax.fori_loop(start, stop, lambda t, now: powers(a, top, t, now, False), stats))

    def first_pass(p, carry):
        a, top, count = chunks_of(p)

        for c in range(2):
            qc = 2 * a + c
            for side in range(2):
                @pl.when((qc != x) | (core != side))
                def _():
                    q_from(qc, side).wait_recv()
        @pl.when(p == 0)
        def _():
            do_copy(x, other).start()
            for col in (mate, near, far):
                for side in range(2):
                    do_copy(col, side).start()

        for c, g, cols in tiles:
            qc = 2 * a + c
            head = slice(g * hw, (g + 1) * hw)
            both = jnp.concatenate([qbuf[qc, 0, :, head], qbuf[qc, 1, :, head]], axis=0)
            q_h[a, cols, :] = both
            q_x[a, :hw, cols] = jnp.transpose(both)
            bars = jnp.concatenate([kbuf[0, qc, tok:, :], kbuf[1, qc, tok:, :]], axis=1)
            q_x[a, hw:hw + DOC_ROWS, cols] = jnp.where(
                bars.astype(jnp.float32) == 0.0, 1.0, 0.0).astype(jnp.bfloat16)
        q_x[a, hw + DOC_ROWS:, :] = jnp.zeros((hw - DOC_ROWS, 2 * PAIR * span), jnp.bfloat16)

        start = tuple((jnp.full((1, span), MASKED_LOW, jnp.float32),
                       jnp.zeros((1, span), jnp.float32)) for _ in tiles)
        keep(a, powers(a, top, 0, start, True))

        @pl.when((p == 0) & (depth > 0))
        def _():
            have_k_row(1, 0)

        @pl.when((p == 1) & (depth > 1))
        def _():
            lax.fori_loop(2, depth + 1, pass_k_row, 0)

        more_powers(a, top, 1, jnp.minimum(count, 3 + a))
        return carry

    def farthest_row(p, carry):
        a, top, count = chunks_of(p)
        more_powers(a, top, 3 + a, count)
        return carry

    lax.fori_loop(0, 2, first_pass, 0)

    @pl.when(depth > 1)
    def _():
        lax.fori_loop(2, depth + 1, have_k_row, 0)
        pass_v_row(1, 0)
        lax.fori_loop(0, 2, farthest_row, 0)

    for a in range(2):
        inv_all[a] = 1.0 / inv_all[a]

    def take_gradients(p, carry):
        a = (x // 2 + p) % 2
        for c in range(2):
            qc = 2 * a + c
            for side in range(2):
                @pl.when((qc != x) | (core != side))
                def _():
                    do_from(qc, side).wait_recv()
                    rd_from(qc, side).wait_recv()
        for c, g, cols in tiles:
            qc = 2 * a + c
            head = slice(g * hw, (g + 1) * hw)
            both = jnp.concatenate([dobuf[qc, 0, :, head], dobuf[qc, 1, :, head]], axis=0)
            do_h[a, cols, :] = both
            do_t[a, :, cols] = jnp.transpose(both)
            rd_h[a, :, cols] = jnp.concatenate(
                [rdbuf[qc, 0, g:g + 1, :], rdbuf[qc, 1, g:g + 1, :]], axis=1)
        return carry

    @pl.when(depth == 1)
    def _():
        pass_v_row(1, 0)

    take_gradients(0, 0)
    have_v_row(0, 0)

    @pl.when(depth > 0)
    def _():
        have_v_row(1, 0)

    own = x // 2
    away = 1 - own
    low = 2 * y - 2 * back
    ahead = 2 * back - 1
    late = 2 * ahead + 1

    def item(n):
        in_own, in_low, in_far = n < ahead, n == ahead, n < late
        in_lead = n < late + 1 + away
        block = jnp.where(
            in_own, jnp.where(n < 2, 2 * y - 2 + n, low - 1 + n),
            jnp.where(in_far, low + n - ahead,
                      jnp.where(in_lead, 2 * y + n - late, 2 * y + n - late - 1 - away)))
        a = jnp.where(
            in_own, own,
            jnp.where(in_low, 0, jnp.where(in_lead, away, own)))
        final = jnp.where(in_own, False, jnp.where(in_far, True, ~in_lead | (n == late + 1)))
        return a, block, final & (block >= 0)

    def send_queries(a):
        for c, g, cols in tiles:
            qc = 2 * a + c
            piece = jnp.transpose(dq_t[a, :, cols] * SCALE).astype(jnp.bfloat16)
            head = slice(g * hw, (g + 1) * hw)
            dqsend[qc, 0, :, head] = piece[:tok]
            dqsend[qc, 1, :, head] = piece[tok:]
        for c in range(2):
            qc = 2 * a + c
            for side in range(2):
                @pl.when((qc != x) | (core != side))
                def _():
                    dq_copy(qc, side).start()

    def terms(n, c):
        a, block, final = item(n)

        @pl.when((n == 1) & (depth > 1))
        def _():
            lax.fori_loop(2, depth + 1, pass_v_row, 0)

        @pl.when((n == 2) & (depth > 1))
        def _():
            lax.fori_loop(2, depth + 1, have_v_row, 0)

        @pl.when(n == ahead)
        def _():
            take_gradients(1, 0)

        @pl.when(block >= 0)
        def _():
            t = 2 * y + a - block
            place = place_of(block)
            v_both = jnp.concatenate(
                [vbuf[i, 2 * place + u] for u in range(2) for i in range(2)], axis=0)
            ratio = jnp.exp2((m_all[a, t] - top_all[a]) * LOG2_SCALE) * inv_all[a]
            for _, _, cols in tiles:
                dp = nn(v_both, do_t[a, :, cols])
                pr = e_all[a, t, :, cols] * ratio[:, cols]
                p_low[:, cols] = pr.astype(jnp.bfloat16)
                s_low[:, cols] = (pr * (dp - rd_h[a, :, cols])).astype(jnp.bfloat16)
            dv = nn(p_low[...], do_h[a])
            dk = nn(s_low[...], q_h[a]) * SCALE
            for u in range(2):
                for side in range(2):
                    piece = slice((2 * u + side) * tok, (2 * u + side + 1) * tok)
                    kv_acc[place, side, u, 0] += dk[piece]
                    kv_acc[place, side, u, 1] += dv[piece]
            dq_t[a] += nn(jnp.concatenate([k_t[2 * place], k_t[2 * place + 1]], axis=1), s_low[...])

        @pl.when(final)
        def _():
            x_copy(place_of(block)).start()

        before, final_before = item(n - 1)[1:]

        @pl.when((n > 0) & final_before)
        def _():
            settle(before)

        @pl.when(n == late + away)
        def _():
            send_queries(away)

        return c

    last = late + 2
    lax.fori_loop(0, last + 1, terms, 0)
    send_queries(own)
    settle(item(last)[1])

    def f_copy(col):
        return remote(fsend.at[col], frecv.at[x], fs.at[col], fr.at[x], at(y, col, core))

    def deliver(part, c):
        def more(r, t):
            remote(ysend.at[0, 0], yrecv.at[r - 1, part], ys.at[0, 0], yr.at[r - 1, part],
                   partner).wait_recv()
            return t + yrecv[r - 1, part].astype(jnp.float32)

        both = lax.fori_loop(1, reach + 1, more, xrecv[part]).astype(jnp.bfloat16)
        for u in range(2):
            kc = 2 * part + u
            fsend[kc] = both[u]

            @pl.when(kc != x)
            def _():
                f_copy(kc).start()

        return c

    lax.fori_loop(0, 2, deliver, 0)

    frecv[x] = fsend[x]
    dqrecv[x, core] = dqsend[x, core]

    def dq_from(col, side):
        return remote(dqsend.at[0, 0], dqrecv.at[col, side], ds.at[0, 0], dr.at[col, side], partner)

    dq_from(x, other).wait_recv()
    for col in (mate, near, far):
        for side in range(2):
            dq_from(col, side).wait_recv()
    for col in (mate, near, far):
        remote(fsend.at[0], frecv.at[col], fs.at[0], fr.at[col], partner).wait_recv()
    q_copy(x, other).wait_send()
    do_copy(x, other).wait_send()
    rd_copy(x, other).wait_send()
    dq_copy(x, other).wait_send()
    for col in (mate, near, far):
        k_copy(col).wait_send()
        v_copy(col).wait_send()
        f_copy(col).wait_send()
        for side in range(2):
            q_copy(col, side).wait_send()
            do_copy(col, side).wait_send()
            rd_copy(col, side).wait_send()
            dq_copy(col, side).wait_send()

    def sent_rows(r, c):
        k_row(r, partner).wait_send()
        v_row(r, partner).wait_send()
        return c

    def sent_on_chip(r, c):
        k_pass(r, core).wait_send()
        v_pass(r, core).wait_send()
        for part in range(2):
            x_copy(r * 2 + part).wait_send()
        return c

    def sent_terms(r, c):
        for part in range(2):
            y_copy(r, part).wait_send()
        return c

    lax.fori_loop(1, reach + 1, sent_rows, 0)
    lax.fori_loop(0, depth + 1, sent_on_chip, 0)
    lax.fori_loop(1, depth + 1, sent_terms, 0)


def lay_out(dq_raw, kv_raw, dq_out, dk_out, dv_out):
    width = dq_raw.shape[3]
    hw = kv_raw.shape[3]
    for col in range(CHIPS):
        for side in range(2):
            start = (col * 2 + side) * width
            dq_out[0, :, start:start + width] = dq_raw[col, side]
        cols = slice(col * hw, (col + 1) * hw)
        dk_out[0, :, cols] = kv_raw[col, 0]
        dv_out[0, :, cols] = kv_raw[col, 1]


def on_device(seq_size, query, keys, values, output_gradient, forward_output, doc_ids):
    tok = query.shape[1]
    span = 2 * tok
    hw = HEAD_WIDTH
    width = PAIR * hw
    rows = seq_size // (2 * CHIPS)
    back = LONGEST // (CHIPS * span)
    slots = (back + 1) * CHIPS
    wide = 2 * PAIR * span
    far = max(back, 1)
    bf, f32 = jnp.bfloat16, jnp.float32
    vmem = pl.BlockSpec(memory_space=pltpu.VMEM)
    anywhere = pl.BlockSpec(memory_space=pl.ANY)
    dma = pltpu.SemaphoreType.DMA
    dq_raw, kv_raw = pl.pallas_call(
        functools.partial(kernel, rows, back),
        out_shape=(
            jax.ShapeDtypeStruct((CHIPS, 2, tok, width), bf),
            jax.ShapeDtypeStruct((CHIPS, 2, tok, hw), bf),
        ),
        in_specs=[anywhere, vmem, vmem, anywhere, anywhere, vmem],
        out_specs=(vmem,) * 2,
        scratch_shapes=[
            pltpu.VMEM((tok, query.shape[2]), bf),
            pltpu.VMEM((tok, query.shape[2]), bf),
            pltpu.VMEM((tok, query.shape[2]), bf),
            pltpu.VMEM((CHIPS, tok + DOC_ROWS, hw), bf),
            pltpu.VMEM((2, slots, tok + DOC_ROWS, hw), bf),
            pltpu.VMEM((2, slots, tok, hw), bf),
            pltpu.VMEM((slots, span, 2 * hw), bf),
            pltpu.VMEM((slots, hw, span), bf),
            pltpu.VMEM((CHIPS, 2, 8, tok), f32),
            pltpu.VMEM((CHIPS, 2, tok, width), bf),
            pltpu.VMEM((CHIPS, 2, tok, width), bf),
            pltpu.VMEM((CHIPS, 2, 8, tok), f32),
            pltpu.VMEM((2, 2 * hw, wide), bf),
            pltpu.VMEM((2, wide, hw), bf),
            pltpu.VMEM((2, hw, wide), bf),
            pltpu.VMEM((2, wide, hw), bf),
            pltpu.VMEM((2, 1, wide), f32),
            pltpu.VMEM((2, back * 2 + 1, 2 * span, wide), f32),
            pltpu.VMEM((2, back * 2 + 1, 1, wide), f32),
            pltpu.VMEM((2, 1, wide), f32),
            pltpu.VMEM((2, 1, wide), f32),
            pltpu.VMEM((2 * span, wide), bf),
            pltpu.VMEM((2 * span, wide), bf),
            pltpu.VMEM((2, hw, wide), f32),
            pltpu.VMEM((slots // 2, 2, 2, 2, tok, hw), f32),
            pltpu.VMEM((slots // 2, 2, 2, tok, hw), f32),
            pltpu.VMEM((far, 2, 2, 2, tok, hw), bf),
            pltpu.VMEM((far, 2, 2, 2, tok, hw), bf),
            pltpu.VMEM((CHIPS, 2, tok, hw), bf),
            pltpu.VMEM((CHIPS, 2, tok, width), bf),
            dma((CHIPS,)), dma((CHIPS,)), dma((CHIPS,)), dma((CHIPS,)),
            dma((CHIPS, 2)), dma((CHIPS, 2)), dma((CHIPS, 2)), dma((CHIPS, 2)),
            dma((CHIPS, 2)), dma((CHIPS, 2)),
            dma((back + 1,)), dma((back + 1,)), dma((back + 1,)), dma((back + 1,)),
            dma((back + 1,)), dma((back + 1,)), dma((back + 1,)), dma((back + 1,)),
            dma((slots // 2,)), dma((slots // 2,)), dma((far, 2)), dma((far, 2)),
            dma((CHIPS,)), dma((CHIPS,)), dma((CHIPS, 2)), dma((CHIPS, 2)),
            dma((3,)),
        ],
        compiler_params=pltpu.CompilerParams(
            collective_id=0, has_side_effects=True, vmem_limit_bytes=56 * 1024 * 1024,
        ),
    )(query[0], keys[0], values[0], output_gradient[0], forward_output[0], doc_ids)
    return pl.pallas_call(
        lay_out,
        out_shape=(
            jax.ShapeDtypeStruct(query.shape, bf),
            jax.ShapeDtypeStruct(keys.shape, bf),
            jax.ShapeDtypeStruct(keys.shape, bf),
        ),
        in_specs=[vmem] * 2,
        out_specs=(vmem,) * 3,
    )(dq_raw, kv_raw)


def solution(mesh):
    wide = P("dp", "seq", None)
    return jax.shard_map(
        functools.partial(on_device, mesh.shape["seq"]),
        mesh=mesh,
        in_specs=(wide, wide, wide, wide, wide, P("dp", "seq")),
        out_specs=(wide, wide, wide),
        check_vma=False,
    )
```

```python
import functools
import math

import jax
import jax.numpy as jnp
from jax import lax
from jax.experimental import pallas as pl
from jax.experimental.pallas import tpu as pltpu
from jax.sharding import PartitionSpec as P

HEAD_WIDTH = 128
LONGEST = 2048
DOC_ROWS = 16
MASKED_LOW = -1e30
SCALE = 1.0 / math.sqrt(HEAD_WIDTH)
LOG2_SCALE = SCALE * math.log2(math.e)
CHIPS = 4
PAIR = 2


def nn(a, b):
    return jnp.dot(a, b, preferred_element_type=jnp.float32)


def kernel(
    rows, back,
    q_hbm, k_ref, v_ref, do_hbm, o_hbm, id_ref,
    dqrecv, frecv,
    q_ref, do_ref, o_ref, ksend, kbuf, vbuf, k_x, k_t,
    rdsend, qbuf, dobuf, rdbuf, q_x, q_h, do_t, do_h, rd_h,
    e_all, m_all, top_all, inv_all, p_low, s_low, dq_t,
    kv_acc, xrecv, ysend, yrecv, fsend, dqsend,
    ks, kr, vs, vr, qs, qr, gs, gr, rs, rr,
    kps, kpr, vps, vpr, kys, kyr, vys, vyr,
    xs, xr, ys, yr, fs, fr, ds, dr, ins,
):
    tok = q_ref.shape[0]
    span = 2 * tok
    width = PAIR * HEAD_WIDTH
    hw = HEAD_WIDTH
    steps = back * CHIPS // 2 + 1
    me = lax.axis_index("seq")
    core = me % 2
    other = 1 - core
    x = (me // 2) % CHIPS
    y = me // (2 * CHIPS)
    mate = x + 1 - 2 * (x % 2)
    near, far = (mate + 2) % CHIPS, (x + 2) % CHIPS
    depth = jnp.minimum(y, back)
    reach = jnp.minimum(rows - 1 - y, back)

    def at(row, col, side):
        return {"seq": (row * CHIPS + col) * 2 + side}

    partner = at(y, x, other)

    q_in = pltpu.make_async_copy(q_hbm, q_ref, ins.at[0])
    do_in = pltpu.make_async_copy(do_hbm, do_ref, ins.at[1])
    o_in = pltpu.make_async_copy(o_hbm, o_ref, ins.at[2])
    q_in.start()
    do_in.start()
    o_in.start()
    barrier = pltpu.get_barrier_semaphore()
    pl.semaphore_signal(barrier, inc=1, device_id=partner)
    for col in (mate, near, far):
        for side in range(2):
            pl.semaphore_signal(barrier, inc=1, device_id=at(y, col, side))

    def greet_back(r, c):
        pl.semaphore_signal(barrier, inc=1, device_id=at(y - r, x, core))
        return c

    def greet_fwd(r, c):
        pl.semaphore_signal(barrier, inc=1, device_id=at(y + r, x, core))
        return c

    lax.fori_loop(1, depth + 1, greet_back, 0)
    lax.fori_loop(1, reach + 1, greet_fwd, 0)

    def feats(head, count):
        return pl.ds(pl.multiple_of(head * hw, hw), count * hw)

    def pair_cols(col, side):
        return feats(col * 2 * PAIR + side * PAIR, PAIR)

    doc_rows = lax.broadcasted_iota(jnp.int32, (DOC_ROWS, tok), 0)
    barred = jnp.where(doc_rows == id_ref[...], 0.0, MASKED_LOW).astype(jnp.bfloat16)
    for col in range(CHIPS):
        ksend[col, :tok, :] = k_ref[:, col * hw:(col + 1) * hw]
        ksend[col, tok:, :] = barred
    kbuf[core, x] = ksend[x]
    vbuf[core, x] = v_ref[:, feats(x, 1)]

    pl.semaphore_wait(barrier, 2 * CHIPS - 1 + depth + reach)

    def remote(src, dst, send, recv, target):
        return pltpu.make_async_remote_copy(
            src_ref=src, dst_ref=dst, send_sem=send, recv_sem=recv, device_id=target)

    def k_copy(col):
        return remote(ksend.at[col], kbuf.at[core, x], ks.at[col], kr.at[x], at(y, col, core))

    def v_copy(col):
        return remote(v_ref.at[:, feats(col, 1)], vbuf.at[core, x], vs.at[col], vr.at[x],
                      at(y, col, core))

    def q_copy(col, side):
        return remote(q_ref.at[:, pair_cols(col, side)], qbuf.at[x, core],
                      qs.at[col, side], qr.at[x, core], at(y, col, side))

    def do_copy(col, side):
        return remote(do_ref.at[:, pair_cols(col, side)], dobuf.at[x, core],
                      gs.at[col, side], gr.at[x, core], at(y, col, side))

    def rd_copy(col, side):
        return remote(rdsend.at[col, side], rdbuf.at[x, core],
                      rs.at[col, side], rr.at[x, core], at(y, col, side))

    def k_from(col):
        return remote(ksend.at[0], kbuf.at[core, col], ks.at[0], kr.at[col], partner)

    def v_from(col):
        return remote(v_ref.at[:, :hw], vbuf.at[core, col], vs.at[0], vr.at[col], partner)

    def q_from(col, side):
        return remote(q_ref.at[:, :width], qbuf.at[col, side], qs.at[0, 0], qr.at[col, side],
                      partner)

    def do_from(col, side):
        return remote(do_ref.at[:, :width], dobuf.at[col, side], gs.at[0, 0], gr.at[col, side],
                      partner)

    def rd_from(col, side):
        return remote(rdsend.at[0, 0], rdbuf.at[col, side], rs.at[0, 0], rr.at[col, side], partner)

    def row_of(r):
        return pl.ds(r * CHIPS, CHIPS)

    def k_pass(r, side):
        return remote(kbuf.at[side, row_of(r)], kbuf.at[side, row_of(r)], kps.at[r], kpr.at[r],
                      partner)

    def v_pass(r, side):
        return remote(vbuf.at[side, row_of(r)], vbuf.at[side, row_of(r)], vps.at[r], vpr.at[r],
                      partner)

    def k_row(r, target):
        return remote(kbuf.at[core, row_of(0)], kbuf.at[core, row_of(r)], kys.at[r], kyr.at[r],
                      target)

    def v_row(r, target):
        return remote(vbuf.at[core, row_of(0)], vbuf.at[core, row_of(r)], vys.at[r], vyr.at[r],
                      target)

    for col in (mate, far, near):
        k_copy(col).start()
    for col in (mate, far, near):
        v_copy(col).start()
    def start_k_row(r, c):
        k_row(r, at(y + r, x, core)).start()
        return c

    def start_v_row(r, c):
        v_row(r, at(y + r, x, core)).start()
        return c

    def build_keys(r):
        def one(i, c):
            slot = r * CHIPS + i
            both = jnp.concatenate([kbuf[0, slot, :tok, :], kbuf[1, slot, :tok, :]], axis=0)
            bars = jnp.concatenate([kbuf[0, slot, tok:, :], kbuf[1, slot, tok:, :]], axis=1)
            pad = jnp.zeros((hw - DOC_ROWS, span), jnp.bfloat16)
            k_x[slot, :, :hw] = both
            k_x[slot, :, hw:] = jnp.transpose(jnp.concatenate([bars, pad], axis=0))
            k_t[slot] = jnp.transpose(both)
            return c

        lax.fori_loop(0, CHIPS, one, 0)

    q_in.wait()
    q_copy(x, other).start()
    q_copy(mate, core).start()
    for col in (mate, near, far):
        k_from(col).wait_recv()
    k_pass(0, core).start()
    lax.fori_loop(1, reach + 1, start_k_row, 0)
    q_copy(mate, other).start()
    for col in (near, far):
        for side in range(2):
            q_copy(col, side).start()
    for col in (mate, near, far):
        v_from(col).wait_recv()
    v_pass(0, core).start()
    lax.fori_loop(1, reach + 1, start_v_row, 0)
    qbuf[x, core] = q_ref[:, pair_cols(x, core)]
    do_in.wait()
    o_in.wait()
    dobuf[x, core] = do_ref[:, pair_cols(x, core)]

    for col in range(CHIPS):
        for side in range(2):
            for g in range(PAIR):
                h = (col * 2 + side) * PAIR + g
                cols = slice(h * hw, (h + 1) * hw)
                prod = do_ref[:, cols].astype(jnp.float32) * o_ref[:, cols].astype(jnp.float32)
                rdsend[col, side, g:g + 1, :] = jnp.sum(
                    jnp.transpose(prod), axis=0, keepdims=True)
            rdsend[col, side, PAIR:, :] = jnp.zeros((8 - PAIR, tok), jnp.float32)
    rdbuf[x, core] = rdsend[x, core]
    rd_copy(x, other).start()
    for col in (mate, near, far):
        for side in range(2):
            rd_copy(col, side).start()
    kv_acc[...] = jnp.zeros(kv_acc.shape, jnp.float32)
    dq_t[...] = jnp.zeros(dq_t.shape, jnp.float32)

    k_pass(0, other).wait_recv()
    build_keys(0)

    def pass_k_row(r, c):
        k_row(r, partner).wait_recv()
        k_pass(r, core).start()
        return c

    def have_k_row(r, c):
        k_pass(r, other).wait_recv()
        build_keys(r)
        return c

    def pass_v_row(r, c):
        v_row(r, partner).wait_recv()
        v_pass(r, core).start()
        return c

    def have_v_row(r, c):
        v_pass(r, other).wait_recv()
        return c

    @pl.when(depth > 0)
    def _():
        pass_k_row(1, 0)

    tiles = [(c, g, slice((c * PAIR + g) * span, (c * PAIR + g + 1) * span))
             for c in range(2) for g in range(PAIR)]

    def place_of(block):
        return (y - block // 2) * 2 + block % 2

    def x_copy(place):
        return remote(kv_acc.at[place, other], xrecv.at[place], xs.at[place], xr.at[place], partner)

    def y_copy(r, part):
        return remote(ysend.at[r - 1, part], yrecv.at[r - 1, part], ys.at[r - 1, part],
                      yr.at[r - 1, part], at(y - r, x, core))

    def dq_copy(col, side):
        return remote(dqsend.at[col, side], dqrecv.at[x, core], ds.at[col, side],
                      dr.at[x, core], at(y, col, side))

    def settle(block):
        place = place_of(block)
        r, part = place // 2, place % 2
        x_copy(place).wait_recv()
        kv_sum = kv_acc[place, core] + xrecv[place]

        @pl.when(r > 0)
        def _():
            ysend[r - 1, part] = kv_sum.astype(jnp.bfloat16)
            y_copy(r, part).start()

        @pl.when(r == 0)
        def _():
            xrecv[place] = kv_sum

    def chunks_of(p):
        a = (x // 2 + p) % 2
        top = 2 * y + a
        return a, top, jnp.minimum(top + 1, steps)

    FIRST, BETWEEN, LAST = 0, 1, 2

    def key_rows(kind, c):
        low = 1 if kind == LAST and c == 1 else 0
        high = 1 if kind == FIRST and c == 0 else 2
        return low * span, high * span

    def powers(a, top, t, stats, kind):
        place = place_of(top - t)
        keys_x = k_x[pl.ds(2 * place, 2)].reshape(2 * span, 2 * hw)
        out = []
        for (c, g, cols), (m_run, l_run) in zip(tiles, stats):
            low, high = key_rows(kind, c)
            s = nn(keys_x[low:high], q_x[a, :, cols])
            if kind == FIRST:
                key_pos = lax.broadcasted_iota(jnp.int32, (high - low, span), 0)
                query_pos = lax.broadcasted_iota(jnp.int32, (high - low, span), 1)
                s = jnp.where(key_pos <= query_pos + c * span, s, MASKED_LOW)
            m = jnp.max(s, axis=0, keepdims=True)
            e = jnp.exp2((s - m) * LOG2_SCALE)
            e_all[a, t, low:high, cols] = e
            m_all[a, t, :, cols] = m
            l = jnp.sum(e, axis=0, keepdims=True)
            m_new = jnp.maximum(m_run, m)
            l_run = (l_run * jnp.exp2((m_run - m_new) * LOG2_SCALE)
                     + l * jnp.exp2((m - m_new) * LOG2_SCALE))
            out.append((m_new, l_run))
        return tuple(out)

    def keep(a, stats):
        top_all[a] = jnp.concatenate([m for m, _ in stats], axis=1)
        inv_all[a] = jnp.concatenate([l for _, l in stats], axis=1)

    def more_powers(a, top, start, stop):
        stats = tuple((top_all[a, :, cols], inv_all[a, :, cols]) for _, _, cols in tiles)
        keep(a, lax.fori_loop(start, stop, lambda t, now: powers(a, top, t, now, BETWEEN), stats))

    def first_pass(p, carry):
        a, top, count = chunks_of(p)

        for c in range(2):
            qc = 2 * a + c
            for side in range(2):
                @pl.when((qc != x) | (core != side))
                def _():
                    q_from(qc, side).wait_recv()
        @pl.when(p == 0)
        def _():
            do_copy(x, other).start()
            for col in (mate, near, far):
                for side in range(2):
                    do_copy(col, side).start()

        for c, g, cols in tiles:
            qc = 2 * a + c
            head = slice(g * hw, (g + 1) * hw)
            both = jnp.concatenate([qbuf[qc, 0, :, head], qbuf[qc, 1, :, head]], axis=0)
            q_h[a, cols, :] = both
            q_x[a, :hw, cols] = jnp.transpose(both)
            bars = jnp.concatenate([kbuf[0, qc, tok:, :], kbuf[1, qc, tok:, :]], axis=1)
            q_x[a, hw:hw + DOC_ROWS, cols] = jnp.where(
                bars.astype(jnp.float32) == 0.0, 1.0, 0.0).astype(jnp.bfloat16)
        q_x[a, hw + DOC_ROWS:, :] = jnp.zeros((hw - DOC_ROWS, 2 * PAIR * span), jnp.bfloat16)

        start = tuple((jnp.full((1, span), MASKED_LOW, jnp.float32),
                       jnp.zeros((1, span), jnp.float32)) for _ in tiles)
        keep(a, powers(a, top, 0, start, FIRST))

        @pl.when((p == 0) & (depth > 0))
        def _():
            have_k_row(1, 0)

        @pl.when((p == 1) & (depth > 1))
        def _():
            lax.fori_loop(2, depth + 1, pass_k_row, 0)

        more_powers(a, top, 1, jnp.minimum(count, 3 + a))
        return carry

    def farthest_row(p, carry):
        a, top, count = chunks_of(p)
        more_powers(a, top, 3 + a, steps - 1)
        stats = tuple((top_all[a, :, cols], inv_all[a, :, cols]) for _, _, cols in tiles)
        keep(a, powers(a, top, steps - 1, stats, LAST))
        return carry

    lax.fori_loop(0, 2, first_pass, 0)

    @pl.when(depth > 1)
    def _():
        lax.fori_loop(2, depth + 1, have_k_row, 0)
        pass_v_row(1, 0)
        lax.fori_loop(0, 2, farthest_row, 0)

    for a in range(2):
        inv_all[a] = 1.0 / inv_all[a]

    def take_gradients(p, carry):
        a = (x // 2 + p) % 2
        for c in range(2):
            qc = 2 * a + c
            for side in range(2):
                @pl.when((qc != x) | (core != side))
                def _():
                    do_from(qc, side).wait_recv()
                    rd_from(qc, side).wait_recv()
        for c, g, cols in tiles:
            qc = 2 * a + c
            head = slice(g * hw, (g + 1) * hw)
            both = jnp.concatenate([dobuf[qc, 0, :, head], dobuf[qc, 1, :, head]], axis=0)
            do_h[a, cols, :] = both
            do_t[a, :, cols] = jnp.transpose(both)
            rd_h[a, :, cols] = jnp.concatenate(
                [rdbuf[qc, 0, g:g + 1, :], rdbuf[qc, 1, g:g + 1, :]], axis=1)
        return carry

    @pl.when(depth == 1)
    def _():
        pass_v_row(1, 0)

    take_gradients(0, 0)
    lax.fori_loop(2, depth + 1, pass_v_row, 0)
    take_gradients(1, 0)
    lax.fori_loop(0, depth + 1, have_v_row, 0)

    own = x // 2
    away = 1 - own
    low = 2 * y - 2 * back
    middle = 4 + away
    tail = middle + 4

    def item(n):
        in_low, in_lead, in_middle = n < 3, n < middle, n < tail
        k = n - middle
        block = jnp.where(
            in_low, low + (n + 1) // 2,
            jnp.where(in_lead, 2 * y + n - 3,
                      jnp.where(in_middle, 2 * y - 2 + k // 2, 2 * y + n - tail)))
        a = jnp.where(
            in_low, jnp.where(n == 0, 0, jnp.where(n == 1, away, own)),
            jnp.where(in_lead, away,
                      jnp.where(in_middle, jnp.where(k % 2 == 0, away, own), own)))
        final = jnp.where(
            in_low, n != 1, jnp.where(in_lead, n == 4, ~in_middle | (k % 2 == 1)))
        return a, block, final & (block >= 0)

    def send_queries(a):
        for c, g, cols in tiles:
            qc = 2 * a + c
            piece = jnp.transpose(dq_t[a, :, cols] * SCALE).astype(jnp.bfloat16)
            head = slice(g * hw, (g + 1) * hw)
            dqsend[qc, 0, :, head] = piece[:tok]
            dqsend[qc, 1, :, head] = piece[tok:]
        for c in range(2):
            qc = 2 * a + c
            for side in range(2):
                @pl.when((qc != x) | (core != side))
                def _():
                    dq_copy(qc, side).start()

    def add_terms(a, t, block, kind):
        place = place_of(block)
        v_both = jnp.concatenate(
            [vbuf[i, 2 * place + u] for u in range(2) for i in range(2)], axis=0)
        ratio = jnp.exp2((m_all[a, t] - top_all[a]) * LOG2_SCALE) * inv_all[a]
        for c, _, cols in tiles:
            low, high = key_rows(kind, c)
            dp = nn(v_both[low:high], do_t[a, :, cols])
            pr = e_all[a, t, low:high, cols] * ratio[:, cols]
            p_low[low:high, cols] = pr.astype(jnp.bfloat16)
            s_low[low:high, cols] = (pr * (dp - rd_h[a, :, cols])).astype(jnp.bfloat16)

        def add_keys(low, high, cols):
            dv = nn(p_low[low:high, cols], do_h[a, cols, :])
            dk = nn(s_low[low:high, cols], q_h[a, cols, :]) * SCALE
            for start in range(low, high, tok):
                u, side = start // span, start // tok % 2
                piece = slice(start - low, start - low + tok)
                kv_acc[place, side, u, 0] += dk[piece]
                kv_acc[place, side, u, 1] += dv[piece]

        every = 2 * PAIR * span
        k_both = jnp.concatenate([k_t[2 * place], k_t[2 * place + 1]], axis=1)
        if kind == BETWEEN:
            add_keys(0, 2 * span, slice(0, every))
            dq_t[a] += nn(k_both, s_low[...])
        else:
            cut = slice(every // 2, every) if kind == FIRST else slice(0, every // 2)
            add_keys(0, span, slice(0, every) if kind == FIRST else cut)
            add_keys(span, 2 * span, slice(0, every) if kind == LAST else cut)
            for c in range(2):
                low, high = key_rows(kind, c)
                cols = slice(c * every // 2, (c + 1) * every // 2)
                dq_t[a, :, cols] += nn(k_both[:, low:high], s_low[low:high, cols])

    def terms(n, c):
        a, block, final = item(n)

        t = 2 * y + a - block

        @pl.when((block >= 0) & (t == 0))
        def _():
            add_terms(a, t, block, FIRST)

        @pl.when((block >= 0) & (t > 0) & (t < steps - 1))
        def _():
            add_terms(a, t, block, BETWEEN)

        @pl.when((block >= 0) & (t == steps - 1))
        def _():
            add_terms(a, t, block, LAST)

        @pl.when(final)
        def _():
            x_copy(place_of(block)).start()

        before, final_before = item(n - 1)[1:]

        @pl.when((n > 0) & final_before)
        def _():
            settle(before)

        @pl.when(n == middle + 2)
        def _():
            send_queries(away)

        return c

    last = tail + own
    lax.fori_loop(0, last + 1, terms, 0)
    send_queries(own)
    settle(item(last)[1])

    def f_copy(col):
        return remote(fsend.at[col], frecv.at[x], fs.at[col], fr.at[x], at(y, col, core))

    def deliver(part, c):
        def more(r, t):
            remote(ysend.at[0, 0], yrecv.at[r - 1, part], ys.at[0, 0], yr.at[r - 1, part],
                   partner).wait_recv()
            return t + yrecv[r - 1, part].astype(jnp.float32)

        both = lax.fori_loop(1, reach + 1, more, xrecv[part]).astype(jnp.bfloat16)
        for u in range(2):
            kc = 2 * part + u
            fsend[kc] = both[u]

            @pl.when(kc != x)
            def _():
                f_copy(kc).start()

        return c

    lax.fori_loop(0, 2, deliver, 0)

    frecv[x] = fsend[x]
    dqrecv[x, core] = dqsend[x, core]

    def dq_from(col, side):
        return remote(dqsend.at[0, 0], dqrecv.at[col, side], ds.at[0, 0], dr.at[col, side], partner)

    dq_from(x, other).wait_recv()
    for col in (mate, near, far):
        for side in range(2):
            dq_from(col, side).wait_recv()
    for col in (mate, near, far):
        remote(fsend.at[0], frecv.at[col], fs.at[0], fr.at[col], partner).wait_recv()
    q_copy(x, other).wait_send()
    do_copy(x, other).wait_send()
    rd_copy(x, other).wait_send()
    dq_copy(x, other).wait_send()
    for col in (mate, near, far):
        k_copy(col).wait_send()
        v_copy(col).wait_send()
        f_copy(col).wait_send()
        for side in range(2):
            q_copy(col, side).wait_send()
            do_copy(col, side).wait_send()
            rd_copy(col, side).wait_send()
            dq_copy(col, side).wait_send()

    def sent_rows(r, c):
        k_row(r, partner).wait_send()
        v_row(r, partner).wait_send()
        return c

    def sent_on_chip(r, c):
        k_pass(r, core).wait_send()
        v_pass(r, core).wait_send()
        for part in range(2):
            x_copy(r * 2 + part).wait_send()
        return c

    def sent_terms(r, c):
        for part in range(2):
            y_copy(r, part).wait_send()
        return c

    lax.fori_loop(1, reach + 1, sent_rows, 0)
    lax.fori_loop(0, depth + 1, sent_on_chip, 0)
    lax.fori_loop(1, depth + 1, sent_terms, 0)


def lay_out(dq_raw, kv_raw, dq_out, dk_out, dv_out):
    width = dq_raw.shape[3]
    hw = kv_raw.shape[3]
    for col in range(CHIPS):
        for side in range(2):
            start = (col * 2 + side) * width
            dq_out[0, :, start:start + width] = dq_raw[col, side]
        cols = slice(col * hw, (col + 1) * hw)
        dk_out[0, :, cols] = kv_raw[col, 0]
        dv_out[0, :, cols] = kv_raw[col, 1]


def on_device(seq_size, query, keys, values, output_gradient, forward_output, doc_ids):
    tok = query.shape[1]
    span = 2 * tok
    hw = HEAD_WIDTH
    width = PAIR * hw
    rows = seq_size // (2 * CHIPS)
    back = LONGEST // (CHIPS * span)
    slots = (back + 1) * CHIPS
    wide = 2 * PAIR * span
    far = max(back, 1)
    bf, f32 = jnp.bfloat16, jnp.float32
    vmem = pl.BlockSpec(memory_space=pltpu.VMEM)
    anywhere = pl.BlockSpec(memory_space=pl.ANY)
    dma = pltpu.SemaphoreType.DMA
    dq_raw, kv_raw = pl.pallas_call(
        functools.partial(kernel, rows, back),
        out_shape=(
            jax.ShapeDtypeStruct((CHIPS, 2, tok, width), bf),
            jax.ShapeDtypeStruct((CHIPS, 2, tok, hw), bf),
        ),
        in_specs=[anywhere, vmem, vmem, anywhere, anywhere, vmem],
        out_specs=(vmem,) * 2,
        scratch_shapes=[
            pltpu.VMEM((tok, query.shape[2]), bf),
            pltpu.VMEM((tok, query.shape[2]), bf),
            pltpu.VMEM((tok, query.shape[2]), bf),
            pltpu.VMEM((CHIPS, tok + DOC_ROWS, hw), bf),
            pltpu.VMEM((2, slots, tok + DOC_ROWS, hw), bf),
            pltpu.VMEM((2, slots, tok, hw), bf),
            pltpu.VMEM((slots, span, 2 * hw), bf),
            pltpu.VMEM((slots, hw, span), bf),
            pltpu.VMEM((CHIPS, 2, 8, tok), f32),
            pltpu.VMEM((CHIPS, 2, tok, width), bf),
            pltpu.VMEM((CHIPS, 2, tok, width), bf),
            pltpu.VMEM((CHIPS, 2, 8, tok), f32),
            pltpu.VMEM((2, 2 * hw, wide), bf),
            pltpu.VMEM((2, wide, hw), bf),
            pltpu.VMEM((2, hw, wide), bf),
            pltpu.VMEM((2, wide, hw), bf),
            pltpu.VMEM((2, 1, wide), f32),
            pltpu.VMEM((2, back * 2 + 1, 2 * span, wide), f32),
            pltpu.VMEM((2, back * 2 + 1, 1, wide), f32),
            pltpu.VMEM((2, 1, wide), f32),
            pltpu.VMEM((2, 1, wide), f32),
            pltpu.VMEM((2 * span, wide), bf),
            pltpu.VMEM((2 * span, wide), bf),
            pltpu.VMEM((2, hw, wide), f32),
            pltpu.VMEM((slots // 2, 2, 2, 2, tok, hw), f32),
            pltpu.VMEM((slots // 2, 2, 2, tok, hw), f32),
            pltpu.VMEM((far, 2, 2, 2, tok, hw), bf),
            pltpu.VMEM((far, 2, 2, 2, tok, hw), bf),
            pltpu.VMEM((CHIPS, 2, tok, hw), bf),
            pltpu.VMEM((CHIPS, 2, tok, width), bf),
            dma((CHIPS,)), dma((CHIPS,)), dma((CHIPS,)), dma((CHIPS,)),
            dma((CHIPS, 2)), dma((CHIPS, 2)), dma((CHIPS, 2)), dma((CHIPS, 2)),
            dma((CHIPS, 2)), dma((CHIPS, 2)),
            dma((back + 1,)), dma((back + 1,)), dma((back + 1,)), dma((back + 1,)),
            dma((back + 1,)), dma((back + 1,)), dma((back + 1,)), dma((back + 1,)),
            dma((slots // 2,)), dma((slots // 2,)), dma((far, 2)), dma((far, 2)),
            dma((CHIPS,)), dma((CHIPS,)), dma((CHIPS, 2)), dma((CHIPS, 2)),
            dma((3,)),
        ],
        compiler_params=pltpu.CompilerParams(
            collective_id=0, has_side_effects=True, vmem_limit_bytes=56 * 1024 * 1024,
        ),
    )(query[0], keys[0], values[0], output_gradient[0], forward_output[0], doc_ids)
    return pl.pallas_call(
        lay_out,
        out_shape=(
            jax.ShapeDtypeStruct(query.shape, bf),
            jax.ShapeDtypeStruct(keys.shape, bf),
            jax.ShapeDtypeStruct(keys.shape, bf),
        ),
        in_specs=[vmem] * 2,
        out_specs=(vmem,) * 3,
    )(dq_raw, kv_raw)


def solution(mesh):
    wide = P("dp", "seq", None)
    return jax.shard_map(
        functools.partial(on_device, mesh.shape["seq"]),
        mesh=mesh,
        in_specs=(wide, wide, wide, wide, wide, P("dp", "seq")),
        out_specs=(wide, wide, wide),
        check_vma=False,
    )
```

```python
import functools
import math

import jax
import jax.numpy as jnp
from jax import lax
from jax.experimental import pallas as pl
from jax.experimental.pallas import tpu as pltpu
from jax.sharding import PartitionSpec as P

HEAD_WIDTH = 128
LONGEST = 2048
DOC_ROWS = 16
MASKED_LOW = -1e30
SCALE = 1.0 / math.sqrt(HEAD_WIDTH)
LOG2_SCALE = SCALE * math.log2(math.e)
CHIPS = 4
PAIR = 2


def nn(a, b):
    return jnp.dot(a, b, preferred_element_type=jnp.float32)


def kernel(
    rows, back,
    q_hbm, k_ref, v_ref, do_hbm, o_hbm, id_ref,
    dqrecv, frecv,
    q_ref, do_ref, o_ref, ksend, kbuf, vbuf, k_x, k_t,
    rdsend, qbuf, dobuf, rdbuf, q_x, q_h, do_t, do_h, rd_h,
    e_all, m_all, top_all, inv_all, p_low, s_low, dq_t,
    kv_acc, xrecv, ysend, yrecv, fsend, dqsend,
    ks, kr, vs, vr, qs, qr, gs, gr, rs, rr,
    kps, kpr, vps, vpr, kys, kyr, vys, vyr,
    xs, xr, ys, yr, fs, fr, ds, dr, ins,
):
    tok = q_ref.shape[0]
    span = 2 * tok
    width = PAIR * HEAD_WIDTH
    hw = HEAD_WIDTH
    steps = back * CHIPS // 2 + 1
    me = lax.axis_index("seq")
    core = me % 2
    other = 1 - core
    x = (me // 2) % CHIPS
    y = me // (2 * CHIPS)
    mate = x + 1 - 2 * (x % 2)
    near, far = (mate + 2) % CHIPS, (x + 2) % CHIPS
    depth = jnp.minimum(y, back)
    reach = jnp.minimum(rows - 1 - y, back)

    def at(row, col, side):
        return {"seq": (row * CHIPS + col) * 2 + side}

    partner = at(y, x, other)

    q_in = pltpu.make_async_copy(q_hbm, q_ref, ins.at[0])
    do_in = pltpu.make_async_copy(do_hbm, do_ref, ins.at[1])
    o_in = pltpu.make_async_copy(o_hbm, o_ref, ins.at[2])
    q_in.start()
    do_in.start()
    o_in.start()
    barrier = pltpu.get_barrier_semaphore()
    pl.semaphore_signal(barrier, inc=1, device_id=partner)
    for col in (mate, near, far):
        for side in range(2):
            pl.semaphore_signal(barrier, inc=1, device_id=at(y, col, side))

    def greet_back(r, c):
        pl.semaphore_signal(barrier, inc=1, device_id=at(y - r, x, core))
        return c

    def greet_fwd(r, c):
        pl.semaphore_signal(barrier, inc=1, device_id=at(y + r, x, core))
        return c

    lax.fori_loop(1, depth + 1, greet_back, 0)
    lax.fori_loop(1, reach + 1, greet_fwd, 0)

    def feats(head, count):
        return pl.ds(pl.multiple_of(head * hw, hw), count * hw)

    def pair_cols(col, side):
        return feats(col * 2 * PAIR + side * PAIR, PAIR)

    doc_rows = lax.broadcasted_iota(jnp.int32, (DOC_ROWS, tok), 0)
    barred = jnp.where(doc_rows == id_ref[...], 0.0, MASKED_LOW).astype(jnp.bfloat16)
    for col in range(CHIPS):
        ksend[col, :tok, :] = k_ref[:, col * hw:(col + 1) * hw]
        ksend[col, tok:, :] = barred
    kbuf[core, x] = ksend[x]
    vbuf[core, x] = v_ref[:, feats(x, 1)]

    pl.semaphore_wait(barrier, 2 * CHIPS - 1 + depth + reach)

    def remote(src, dst, send, recv, target):
        return pltpu.make_async_remote_copy(
            src_ref=src, dst_ref=dst, send_sem=send, recv_sem=recv, device_id=target)

    def k_copy(col):
        return remote(ksend.at[col], kbuf.at[core, x], ks.at[col], kr.at[x], at(y, col, core))

    def v_copy(col):
        return remote(v_ref.at[:, feats(col, 1)], vbuf.at[core, x], vs.at[col], vr.at[x],
                      at(y, col, core))

    def q_copy(col, side):
        return remote(q_ref.at[:, pair_cols(col, side)], qbuf.at[x, core],
                      qs.at[col, side], qr.at[x, core], at(y, col, side))

    def do_copy(col, side):
        return remote(do_ref.at[:, pair_cols(col, side)], dobuf.at[x, core],
                      gs.at[col, side], gr.at[x, core], at(y, col, side))

    def rd_copy(col, side):
        return remote(rdsend.at[col, side], rdbuf.at[x, core],
                      rs.at[col, side], rr.at[x, core], at(y, col, side))

    def k_from(col):
        return remote(ksend.at[0], kbuf.at[core, col], ks.at[0], kr.at[col], partner)

    def v_from(col):
        return remote(v_ref.at[:, :hw], vbuf.at[core, col], vs.at[0], vr.at[col], partner)

    def q_from(col, side):
        return remote(q_ref.at[:, :width], qbuf.at[col, side], qs.at[0, 0], qr.at[col, side],
                      partner)

    def do_from(col, side):
        return remote(do_ref.at[:, :width], dobuf.at[col, side], gs.at[0, 0], gr.at[col, side],
                      partner)

    def rd_from(col, side):
        return remote(rdsend.at[0, 0], rdbuf.at[col, side], rs.at[0, 0], rr.at[col, side], partner)

    def row_of(r):
        return pl.ds(r * CHIPS, CHIPS)

    def k_pass(r, side):
        return remote(kbuf.at[side, row_of(r)], kbuf.at[side, row_of(r)], kps.at[r], kpr.at[r],
                      partner)

    def v_pass(r, side):
        return remote(vbuf.at[side, row_of(r)], vbuf.at[side, row_of(r)], vps.at[r], vpr.at[r],
                      partner)

    def k_row(r, target):
        return remote(kbuf.at[core, row_of(0)], kbuf.at[core, row_of(r)], kys.at[r], kyr.at[r],
                      target)

    def v_row(r, target):
        return remote(vbuf.at[core, row_of(0)], vbuf.at[core, row_of(r)], vys.at[r], vyr.at[r],
                      target)

    for col in (mate, far, near):
        k_copy(col).start()
    for col in (mate, far, near):
        v_copy(col).start()
    def start_k_row(r, c):
        k_row(r, at(y + r, x, core)).start()
        return c

    def start_v_row(r, c):
        v_row(r, at(y + r, x, core)).start()
        return c

    def build_keys(r):
        bars = [jnp.concatenate([kbuf[side, r * CHIPS + i, tok:, :] for side in range(2)], axis=1)
                for i in range(CHIPS)]
        pad = jnp.zeros((hw - CHIPS * DOC_ROWS, span), jnp.bfloat16)
        turned = jnp.transpose(jnp.concatenate(bars + [pad], axis=0)).astype(jnp.float32)
        owner = lax.broadcasted_iota(jnp.int32, (span, hw), 1) // DOC_ROWS
        for i in range(CHIPS):
            slot = r * CHIPS + i
            both = jnp.concatenate([kbuf[0, slot, :tok, :], kbuf[1, slot, :tok, :]], axis=0)
            k_x[slot, :, :hw] = both
            k_x[slot, :, hw:] = jnp.where(owner == i, turned, 0.0).astype(jnp.bfloat16)
            k_t[slot] = jnp.transpose(both)

    q_in.wait()
    q_copy(x, other).start()
    q_copy(mate, core).start()
    for col in (mate, near, far):
        k_from(col).wait_recv()
    k_pass(0, core).start()
    lax.fori_loop(1, reach + 1, start_k_row, 0)
    q_copy(mate, other).start()
    for col in (near, far):
        for side in range(2):
            q_copy(col, side).start()
    for col in (mate, near, far):
        v_from(col).wait_recv()
    v_pass(0, core).start()
    lax.fori_loop(1, reach + 1, start_v_row, 0)
    qbuf[x, core] = q_ref[:, pair_cols(x, core)]
    do_in.wait()
    o_in.wait()
    dobuf[x, core] = do_ref[:, pair_cols(x, core)]

    for col in range(CHIPS):
        for side in range(2):
            for g in range(PAIR):
                h = (col * 2 + side) * PAIR + g
                cols = slice(h * hw, (h + 1) * hw)
                prod = do_ref[:, cols].astype(jnp.float32) * o_ref[:, cols].astype(jnp.float32)
                rdsend[col, side, g:g + 1, :] = jnp.sum(
                    jnp.transpose(prod), axis=0, keepdims=True)
            rdsend[col, side, PAIR:, :] = jnp.zeros((8 - PAIR, tok), jnp.float32)
    rdbuf[x, core] = rdsend[x, core]
    rd_copy(x, other).start()
    for col in (mate, near, far):
        for side in range(2):
            rd_copy(col, side).start()
    kv_acc[...] = jnp.zeros(kv_acc.shape, jnp.float32)
    dq_t[...] = jnp.zeros(dq_t.shape, jnp.float32)

    k_pass(0, other).wait_recv()
    build_keys(0)

    def pass_k_row(r, c):
        k_row(r, partner).wait_recv()
        k_pass(r, core).start()
        return c

    def have_k_row(r, c):
        k_pass(r, other).wait_recv()
        build_keys(r)
        return c

    def pass_v_row(r, c):
        v_row(r, partner).wait_recv()
        v_pass(r, core).start()
        return c

    def have_v_row(r, c):
        v_pass(r, other).wait_recv()
        return c

    @pl.when(depth > 0)
    def _():
        pass_k_row(1, 0)

    tiles = [(c, g, slice((c * PAIR + g) * span, (c * PAIR + g + 1) * span))
             for c in range(2) for g in range(PAIR)]

    def place_of(block):
        return (y - block // 2) * 2 + block % 2

    def x_copy(place):
        return remote(kv_acc.at[place, other], xrecv.at[place], xs.at[place], xr.at[place], partner)

    def y_copy(r, part):
        return remote(ysend.at[r - 1, part], yrecv.at[r - 1, part], ys.at[r - 1, part],
                      yr.at[r - 1, part], at(y - r, x, core))

    def dq_copy(col, side):
        return remote(dqsend.at[col, side], dqrecv.at[x, core], ds.at[col, side],
                      dr.at[x, core], at(y, col, side))

    def settle(block):
        place = place_of(block)
        r, part = place // 2, place % 2
        x_copy(place).wait_recv()
        kv_sum = kv_acc[place, core] + xrecv[place]

        @pl.when(r > 0)
        def _():
            ysend[r - 1, part] = kv_sum.astype(jnp.bfloat16)
            y_copy(r, part).start()

        @pl.when(r == 0)
        def _():
            xrecv[place] = kv_sum

    def chunks_of(p):
        a = (x // 2 + p) % 2
        top = 2 * y + a
        return a, top, jnp.minimum(top + 1, steps)

    FIRST, BETWEEN, LAST = 0, 1, 2

    def key_rows(kind, c):
        low = 1 if kind == LAST and c == 1 else 0
        high = 1 if kind == FIRST and c == 0 else 2
        return low * span, high * span

    def powers(a, top, t, stats, kind):
        place = place_of(top - t)
        keys_x = k_x[pl.ds(2 * place, 2)].reshape(2 * span, 2 * hw)
        out = []
        for (c, g, cols), (m_run, l_run) in zip(tiles, stats):
            low, high = key_rows(kind, c)
            s = nn(keys_x[low:high], q_x[a, :, cols])
            if kind == FIRST:
                key_pos = lax.broadcasted_iota(jnp.int32, (high - low, span), 0)
                query_pos = lax.broadcasted_iota(jnp.int32, (high - low, span), 1)
                s = jnp.where(key_pos <= query_pos + c * span, s, MASKED_LOW)
            m = jnp.max(s, axis=0, keepdims=True)
            e = jnp.exp2((s - m) * LOG2_SCALE)
            e_all[a, t, low:high, cols] = e
            m_all[a, t, :, cols] = m
            l = jnp.sum(e, axis=0, keepdims=True)
            m_new = jnp.maximum(m_run, m)
            l_run = (l_run * jnp.exp2((m_run - m_new) * LOG2_SCALE)
                     + l * jnp.exp2((m - m_new) * LOG2_SCALE))
            out.append((m_new, l_run))
        return tuple(out)

    def keep(a, stats):
        top_all[a] = jnp.concatenate([m for m, _ in stats], axis=1)
        inv_all[a] = jnp.concatenate([l for _, l in stats], axis=1)

    def more_powers(a, top, start, stop):
        stats = tuple((top_all[a, :, cols], inv_all[a, :, cols]) for _, _, cols in tiles)
        keep(a, lax.fori_loop(start, stop, lambda t, now: powers(a, top, t, now, BETWEEN), stats))

    def first_pass(p, carry):
        a, top, count = chunks_of(p)

        for c in range(2):
            qc = 2 * a + c
            for side in range(2):
                @pl.when((qc != x) | (core != side))
                def _():
                    q_from(qc, side).wait_recv()
        @pl.when(p == 0)
        def _():
            do_copy(x, other).start()
            for col in (mate, near, far):
                for side in range(2):
                    do_copy(col, side).start()

        for c, g, cols in tiles:
            qc = 2 * a + c
            head = slice(g * hw, (g + 1) * hw)
            both = jnp.concatenate([qbuf[qc, 0, :, head], qbuf[qc, 1, :, head]], axis=0)
            q_h[a, cols, :] = both
            q_x[a, :hw, cols] = jnp.transpose(both)
            bars = jnp.concatenate([kbuf[0, qc, tok:, :], kbuf[1, qc, tok:, :]], axis=1)
            match = jnp.where(bars.astype(jnp.float32) == 0.0, 1.0, 0.0).astype(jnp.bfloat16)
            for i in range(CHIPS):
                q_x[a, hw + i * DOC_ROWS:hw + (i + 1) * DOC_ROWS, cols] = match
        q_x[a, hw + CHIPS * DOC_ROWS:, :] = jnp.zeros(
            (hw - CHIPS * DOC_ROWS, 2 * PAIR * span), jnp.bfloat16)

        start = tuple((jnp.full((1, span), MASKED_LOW, jnp.float32),
                       jnp.zeros((1, span), jnp.float32)) for _ in tiles)
        keep(a, powers(a, top, 0, start, FIRST))

        @pl.when((p == 0) & (depth > 0))
        def _():
            have_k_row(1, 0)

        @pl.when((p == 1) & (depth > 1))
        def _():
            lax.fori_loop(2, depth + 1, pass_k_row, 0)

        more_powers(a, top, 1, jnp.minimum(count, 3 + a))
        return carry

    def farthest_row(p, carry):
        a, top, count = chunks_of(p)
        more_powers(a, top, 3 + a, steps - 1)
        stats = tuple((top_all[a, :, cols], inv_all[a, :, cols]) for _, _, cols in tiles)
        keep(a, powers(a, top, steps - 1, stats, LAST))
        return carry

    lax.fori_loop(0, 2, first_pass, 0)

    @pl.when(depth > 1)
    def _():
        lax.fori_loop(2, depth + 1, have_k_row, 0)
        pass_v_row(1, 0)
        lax.fori_loop(0, 2, farthest_row, 0)

    for a in range(2):
        inv_all[a] = 1.0 / inv_all[a]

    def take_gradients(p, carry):
        a = (x // 2 + p) % 2
        for c in range(2):
            qc = 2 * a + c
            for side in range(2):
                @pl.when((qc != x) | (core != side))
                def _():
                    do_from(qc, side).wait_recv()
                    rd_from(qc, side).wait_recv()
        for c, g, cols in tiles:
            qc = 2 * a + c
            head = slice(g * hw, (g + 1) * hw)
            both = jnp.concatenate([dobuf[qc, 0, :, head], dobuf[qc, 1, :, head]], axis=0)
            do_h[a, cols, :] = both
            do_t[a, :, cols] = jnp.transpose(both)
            rd_h[a, :, cols] = jnp.concatenate(
                [rdbuf[qc, 0, g:g + 1, :], rdbuf[qc, 1, g:g + 1, :]], axis=1)
        return carry

    @pl.when(depth == 1)
    def _():
        pass_v_row(1, 0)

    take_gradients(0, 0)
    have_v_row(0, 0)
    take_gradients(1, 0)

    @pl.when(depth > 0)
    def _():
        have_v_row(1, 0)

    own = x // 2
    away = 1 - own
    low = 2 * y - 2 * back
    close = 8 + away

    def item(n):
        in_far, in_lead = (n >= 2) & (n < 5), n < close
        block = jnp.where(
            n < 2, 2 * y - 2,
            jnp.where(in_far, low + (n - 1) // 2,
                      jnp.where(n < 7, 2 * y - 1,
                                jnp.where(in_lead, 2 * y + n - 7, 2 * y + n - close))))
        second = (n == 1) | (n == 4) | (n == 6)
        a = jnp.where(n == 2, 0, jnp.where(second, own, jnp.where(in_lead, away, own)))
        final = second | (n == 2) | (n == 8) | (n >= close)
        return a, block, final & (block >= 0)

    def send_queries(a):
        for c, g, cols in tiles:
            qc = 2 * a + c
            piece = jnp.transpose((dq_t[a, :, cols] * SCALE).astype(jnp.bfloat16))
            head = slice(g * hw, (g + 1) * hw)
            dqsend[qc, 0, :, head] = piece[:tok]
            dqsend[qc, 1, :, head] = piece[tok:]
        for c in range(2):
            qc = 2 * a + c
            for side in range(2):
                @pl.when((qc != x) | (core != side))
                def _():
                    dq_copy(qc, side).start()

    def add_terms(a, t, block, kind):
        place = place_of(block)
        v_both = jnp.concatenate(
            [vbuf[i, 2 * place + u] for u in range(2) for i in range(2)], axis=0)
        ratio = jnp.exp2((m_all[a, t] - top_all[a]) * LOG2_SCALE) * inv_all[a]
        for c, _, cols in tiles:
            low, high = key_rows(kind, c)
            dp = nn(v_both[low:high], do_t[a, :, cols])
            pr = e_all[a, t, low:high, cols] * ratio[:, cols]
            p_low[low:high, cols] = pr.astype(jnp.bfloat16)
            s_low[low:high, cols] = (pr * (dp - rd_h[a, :, cols])).astype(jnp.bfloat16)

        def add_keys(low, high, cols):
            dv = nn(p_low[low:high, cols], do_h[a, cols, :])
            dk = nn(s_low[low:high, cols], q_h[a, cols, :]) * SCALE
            for start in range(low, high, tok):
                u, side = start // span, start // tok % 2
                piece = slice(start - low, start - low + tok)
                kv_acc[place, side, u, 0] += dk[piece]
                kv_acc[place, side, u, 1] += dv[piece]

        every = 2 * PAIR * span
        k_both = jnp.concatenate([k_t[2 * place], k_t[2 * place + 1]], axis=1)
        if kind == BETWEEN:
            add_keys(0, 2 * span, slice(0, every))
            dq_t[a] += nn(k_both, s_low[...])
        else:
            cut = slice(every // 2, every) if kind == FIRST else slice(0, every // 2)
            add_keys(0, span, slice(0, every) if kind == FIRST else cut)
            add_keys(span, 2 * span, slice(0, every) if kind == LAST else cut)
            for c in range(2):
                low, high = key_rows(kind, c)
                cols = slice(c * every // 2, (c + 1) * every // 2)
                dq_t[a, :, cols] += nn(k_both[:, low:high], s_low[low:high, cols])

    def terms(n, c):
        a, block, final = item(n)

        t = 2 * y + a - block

        @pl.when((n == 0) & (depth > 1))
        def _():
            lax.fori_loop(2, depth + 1, pass_v_row, 0)

        @pl.when((n == 2) & (depth > 1))
        def _():
            lax.fori_loop(2, depth + 1, have_v_row, 0)

        @pl.when((block >= 0) & (t == 0))
        def _():
            add_terms(a, t, block, FIRST)

        @pl.when((block >= 0) & (t > 0) & (t < steps - 1))
        def _():
            add_terms(a, t, block, BETWEEN)

        @pl.when((block >= 0) & (t == steps - 1))
        def _():
            add_terms(a, t, block, LAST)

        @pl.when(final)
        def _():
            x_copy(place_of(block)).start()

        before, final_before = item(n - 1)[1:]

        @pl.when((n > 0) & final_before)
        def _():
            settle(before)

        @pl.when(n == close - 1)
        def _():
            send_queries(away)

        return c

    last = close + own
    lax.fori_loop(0, last + 1, terms, 0)
    send_queries(own)
    settle(item(last)[1])

    def f_copy(col):
        return remote(fsend.at[col], frecv.at[x], fs.at[col], fr.at[x], at(y, col, core))

    def deliver(part, c):
        def more(r, t):
            remote(ysend.at[0, 0], yrecv.at[r - 1, part], ys.at[0, 0], yr.at[r - 1, part],
                   partner).wait_recv()
            return t + yrecv[r - 1, part].astype(jnp.float32)

        both = lax.fori_loop(1, reach + 1, more, xrecv[part]).astype(jnp.bfloat16)
        for u in range(2):
            kc = 2 * part + u
            fsend[kc] = both[u]

            @pl.when(kc != x)
            def _():
                f_copy(kc).start()

        return c

    lax.fori_loop(0, 2, deliver, 0)

    frecv[x] = fsend[x]
    dqrecv[x, core] = dqsend[x, core]

    def dq_from(col, side):
        return remote(dqsend.at[0, 0], dqrecv.at[col, side], ds.at[0, 0], dr.at[col, side], partner)

    dq_from(x, other).wait_recv()
    for col in (mate, near, far):
        for side in range(2):
            dq_from(col, side).wait_recv()
    for col in (mate, near, far):
        remote(fsend.at[0], frecv.at[col], fs.at[0], fr.at[col], partner).wait_recv()
    q_copy(x, other).wait_send()
    do_copy(x, other).wait_send()
    rd_copy(x, other).wait_send()
    dq_copy(x, other).wait_send()
    for col in (mate, near, far):
        k_copy(col).wait_send()
        v_copy(col).wait_send()
        f_copy(col).wait_send()
        for side in range(2):
            q_copy(col, side).wait_send()
            do_copy(col, side).wait_send()
            rd_copy(col, side).wait_send()
            dq_copy(col, side).wait_send()

    def sent_rows(r, c):
        k_row(r, partner).wait_send()
        v_row(r, partner).wait_send()
        return c

    def sent_on_chip(r, c):
        k_pass(r, core).wait_send()
        v_pass(r, core).wait_send()
        for part in range(2):
            x_copy(r * 2 + part).wait_send()
        return c

    def sent_terms(r, c):
        for part in range(2):
            y_copy(r, part).wait_send()
        return c

    lax.fori_loop(1, reach + 1, sent_rows, 0)
    lax.fori_loop(0, depth + 1, sent_on_chip, 0)
    lax.fori_loop(1, depth + 1, sent_terms, 0)


def lay_out(dq_raw, kv_raw, dq_out, dk_out, dv_out):
    width = dq_raw.shape[3]
    hw = kv_raw.shape[3]
    for col in range(CHIPS):
        for side in range(2):
            start = (col * 2 + side) * width
            dq_out[0, :, start:start + width] = dq_raw[col, side]
        cols = slice(col * hw, (col + 1) * hw)
        dk_out[0, :, cols] = kv_raw[col, 0]
        dv_out[0, :, cols] = kv_raw[col, 1]


def on_device(seq_size, query, keys, values, output_gradient, forward_output, doc_ids):
    tok = query.shape[1]
    span = 2 * tok
    hw = HEAD_WIDTH
    width = PAIR * hw
    rows = seq_size // (2 * CHIPS)
    back = LONGEST // (CHIPS * span)
    slots = (back + 1) * CHIPS
    wide = 2 * PAIR * span
    far = max(back, 1)
    bf, f32 = jnp.bfloat16, jnp.float32
    vmem = pl.BlockSpec(memory_space=pltpu.VMEM)
    anywhere = pl.BlockSpec(memory_space=pl.ANY)
    dma = pltpu.SemaphoreType.DMA
    dq_raw, kv_raw = pl.pallas_call(
        functools.partial(kernel, rows, back),
        out_shape=(
            jax.ShapeDtypeStruct((CHIPS, 2, tok, width), bf),
            jax.ShapeDtypeStruct((CHIPS, 2, tok, hw), bf),
        ),
        in_specs=[anywhere, vmem, vmem, anywhere, anywhere, vmem],
        out_specs=(vmem,) * 2,
        scratch_shapes=[
            pltpu.VMEM((tok, query.shape[2]), bf),
            pltpu.VMEM((tok, query.shape[2]), bf),
            pltpu.VMEM((tok, query.shape[2]), bf),
            pltpu.VMEM((CHIPS, tok + DOC_ROWS, hw), bf),
            pltpu.VMEM((2, slots, tok + DOC_ROWS, hw), bf),
            pltpu.VMEM((2, slots, tok, hw), bf),
            pltpu.VMEM((slots, span, 2 * hw), bf),
            pltpu.VMEM((slots, hw, span), bf),
            pltpu.VMEM((CHIPS, 2, 8, tok), f32),
            pltpu.VMEM((CHIPS, 2, tok, width), bf),
            pltpu.VMEM((CHIPS, 2, tok, width), bf),
            pltpu.VMEM((CHIPS, 2, 8, tok), f32),
            pltpu.VMEM((2, 2 * hw, wide), bf),
            pltpu.VMEM((2, wide, hw), bf),
            pltpu.VMEM((2, hw, wide), bf),
            pltpu.VMEM((2, wide, hw), bf),
            pltpu.VMEM((2, 1, wide), f32),
            pltpu.VMEM((2, back * 2 + 1, 2 * span, wide), f32),
            pltpu.VMEM((2, back * 2 + 1, 1, wide), f32),
            pltpu.VMEM((2, 1, wide), f32),
            pltpu.VMEM((2, 1, wide), f32),
            pltpu.VMEM((2 * span, wide), bf),
            pltpu.VMEM((2 * span, wide), bf),
            pltpu.VMEM((2, hw, wide), f32),
            pltpu.VMEM((slots // 2, 2, 2, 2, tok, hw), f32),
            pltpu.VMEM((slots // 2, 2, 2, tok, hw), f32),
            pltpu.VMEM((far, 2, 2, 2, tok, hw), bf),
            pltpu.VMEM((far, 2, 2, 2, tok, hw), bf),
            pltpu.VMEM((CHIPS, 2, tok, hw), bf),
            pltpu.VMEM((CHIPS, 2, tok, width), bf),
            dma((CHIPS,)), dma((CHIPS,)), dma((CHIPS,)), dma((CHIPS,)),
            dma((CHIPS, 2)), dma((CHIPS, 2)), dma((CHIPS, 2)), dma((CHIPS, 2)),
            dma((CHIPS, 2)), dma((CHIPS, 2)),
            dma((back + 1,)), dma((back + 1,)), dma((back + 1,)), dma((back + 1,)),
            dma((back + 1,)), dma((back + 1,)), dma((back + 1,)), dma((back + 1,)),
            dma((slots // 2,)), dma((slots // 2,)), dma((far, 2)), dma((far, 2)),
            dma((CHIPS,)), dma((CHIPS,)), dma((CHIPS, 2)), dma((CHIPS, 2)),
            dma((3,)),
        ],
        compiler_params=pltpu.CompilerParams(
            collective_id=0, has_side_effects=True, vmem_limit_bytes=56 * 1024 * 1024,
        ),
    )(query[0], keys[0], values[0], output_gradient[0], forward_output[0], doc_ids)
    return pl.pallas_call(
        lay_out,
        out_shape=(
            jax.ShapeDtypeStruct(query.shape, bf),
            jax.ShapeDtypeStruct(keys.shape, bf),
            jax.ShapeDtypeStruct(keys.shape, bf),
        ),
        in_specs=[vmem] * 2,
        out_specs=(vmem,) * 3,
    )(dq_raw, kv_raw)


def solution(mesh):
    wide = P("dp", "seq", None)
    return jax.shard_map(
        functools.partial(on_device, mesh.shape["seq"]),
        mesh=mesh,
        in_specs=(wide, wide, wide, wide, wide, P("dp", "seq")),
        out_specs=(wide, wide, wide),
        check_vma=False,
    )
```

```python
import functools
import math

import jax
import jax.numpy as jnp
from jax import lax
from jax.experimental import pallas as pl
from jax.experimental.pallas import tpu as pltpu
from jax.sharding import PartitionSpec as P

HEAD_WIDTH = 128
LONGEST = 2048
DOC_ROWS = 16
MASKED_LOW = -1e30
SCALE = 1.0 / math.sqrt(HEAD_WIDTH)
LOG2_SCALE = SCALE * math.log2(math.e)
CHIPS = 4
PAIR = 2


def nn(a, b):
    return jnp.dot(a, b, preferred_element_type=jnp.float32)


def kernel(
    rows, back,
    q_hbm, k_ref, v_ref, do_hbm, o_hbm, id_ref,
    dqrecv, frecv,
    q_ref, do_ref, o_ref, ksend, kbuf, vbuf, k_x, k_t,
    rdsend, qbuf, dobuf, rdbuf, q_x, q_h, do_t, do_h, rd_h,
    e_all, m_all, top_all, inv_all, p_low, s_low, dq_t,
    kv_acc, xrecv, ysend, yrecv, fsend, dqsend,
    ks, kr, vs, vr, qs, qr, gs, gr, rs, rr,
    kps, kpr, vps, vpr, kys, kyr, vys, vyr,
    xs, xr, ys, yr, fs, fr, ds, dr, ins,
):
    tok = q_ref.shape[0]
    span = 2 * tok
    width = PAIR * HEAD_WIDTH
    hw = HEAD_WIDTH
    steps = back * CHIPS // 2 + 1
    me = lax.axis_index("seq")
    core = me % 2
    other = 1 - core
    x = (me // 2) % CHIPS
    y = me // (2 * CHIPS)
    mate = x + 1 - 2 * (x % 2)
    near, far = (mate + 2) % CHIPS, (x + 2) % CHIPS
    depth = jnp.minimum(y, back)
    reach = jnp.minimum(rows - 1 - y, back)

    def at(row, col, side):
        return {"seq": (row * CHIPS + col) * 2 + side}

    partner = at(y, x, other)

    q_in = pltpu.make_async_copy(q_hbm, q_ref, ins.at[0])
    do_in = pltpu.make_async_copy(do_hbm, do_ref, ins.at[1])
    o_in = pltpu.make_async_copy(o_hbm, o_ref, ins.at[2])
    q_in.start()
    do_in.start()
    o_in.start()
    barrier = pltpu.get_barrier_semaphore()
    pl.semaphore_signal(barrier, inc=1, device_id=partner)
    for col in (mate, near, far):
        for side in range(2):
            pl.semaphore_signal(barrier, inc=1, device_id=at(y, col, side))

    def greet_back(r, c):
        pl.semaphore_signal(barrier, inc=1, device_id=at(y - r, x, core))
        return c

    def greet_fwd(r, c):
        pl.semaphore_signal(barrier, inc=1, device_id=at(y + r, x, core))
        return c

    lax.fori_loop(1, depth + 1, greet_back, 0)
    lax.fori_loop(1, reach + 1, greet_fwd, 0)

    def feats(head, count):
        return pl.ds(pl.multiple_of(head * hw, hw), count * hw)

    def pair_cols(col, side):
        return feats(col * 2 * PAIR + side * PAIR, PAIR)

    doc_rows = lax.broadcasted_iota(jnp.int32, (DOC_ROWS, tok), 0)
    barred = jnp.where(doc_rows == id_ref[...], 0.0, MASKED_LOW).astype(jnp.bfloat16)
    for col in range(CHIPS):
        ksend[col, :tok, :] = k_ref[:, col * hw:(col + 1) * hw]
        ksend[col, tok:, :] = barred
    kbuf[core, x] = ksend[x]
    vbuf[core, x] = v_ref[:, feats(x, 1)]

    pl.semaphore_wait(barrier, 2 * CHIPS - 1 + depth + reach)

    def remote(src, dst, send, recv, target):
        return pltpu.make_async_remote_copy(
            src_ref=src, dst_ref=dst, send_sem=send, recv_sem=recv, device_id=target)

    def k_copy(col):
        return remote(ksend.at[col], kbuf.at[core, x], ks.at[col], kr.at[x], at(y, col, core))

    def v_copy(col):
        return remote(v_ref.at[:, feats(col, 1)], vbuf.at[core, x], vs.at[col], vr.at[x],
                      at(y, col, core))

    def q_copy(col, side):
        return remote(q_ref.at[:, pair_cols(col, side)], qbuf.at[x, core],
                      qs.at[col, side], qr.at[x, core], at(y, col, side))

    def do_copy(col, side):
        return remote(do_ref.at[:, pair_cols(col, side)], dobuf.at[x, core],
                      gs.at[col, side], gr.at[x, core], at(y, col, side))

    def rd_copy(col, side):
        return remote(rdsend.at[col, side], rdbuf.at[x, core],
                      rs.at[col, side], rr.at[x, core], at(y, col, side))

    def k_from(col):
        return remote(ksend.at[0], kbuf.at[core, col], ks.at[0], kr.at[col], partner)

    def v_from(col):
        return remote(v_ref.at[:, :hw], vbuf.at[core, col], vs.at[0], vr.at[col], partner)

    def q_from(col, side):
        return remote(q_ref.at[:, :width], qbuf.at[col, side], qs.at[0, 0], qr.at[col, side],
                      partner)

    def do_from(col, side):
        return remote(do_ref.at[:, :width], dobuf.at[col, side], gs.at[0, 0], gr.at[col, side],
                      partner)

    def rd_from(col, side):
        return remote(rdsend.at[0, 0], rdbuf.at[col, side], rs.at[0, 0], rr.at[col, side], partner)

    def row_of(r):
        return pl.ds(r * CHIPS, CHIPS)

    def k_pass(r, side):
        return remote(kbuf.at[side, row_of(r)], kbuf.at[side, row_of(r)], kps.at[r], kpr.at[r],
                      partner)

    def v_pass(r, side):
        return remote(vbuf.at[side, row_of(r)], vbuf.at[side, row_of(r)], vps.at[r], vpr.at[r],
                      partner)

    def k_row(r, target):
        return remote(kbuf.at[core, row_of(0)], kbuf.at[core, row_of(r)], kys.at[r], kyr.at[r],
                      target)

    def v_row(r, target):
        return remote(vbuf.at[core, row_of(0)], vbuf.at[core, row_of(r)], vys.at[r], vyr.at[r],
                      target)

    for col in (mate, far, near):
        k_copy(col).start()
    for col in (mate, far, near):
        v_copy(col).start()
    def start_k_row(i, c):
        r = jnp.where(y == 0, reach + 1 - i, i)
        k_row(r, at(y + r, x, core)).start()
        return c

    def start_v_row(r, c):
        v_row(r, at(y + r, x, core)).start()
        return c

    def build_keys(r):
        bars = [jnp.concatenate([kbuf[side, r * CHIPS + i, tok:, :] for side in range(2)], axis=1)
                for i in range(CHIPS)]
        pad = jnp.zeros((hw - CHIPS * DOC_ROWS, span), jnp.bfloat16)
        turned = jnp.transpose(jnp.concatenate(bars + [pad], axis=0)).astype(jnp.float32)
        owner = lax.broadcasted_iota(jnp.int32, (span, hw), 1) // DOC_ROWS
        for i in range(CHIPS):
            slot = r * CHIPS + i
            both = jnp.concatenate([kbuf[0, slot, :tok, :], kbuf[1, slot, :tok, :]], axis=0)
            k_x[slot, :, :hw] = both
            k_x[slot, :, hw:] = jnp.where(owner == i, turned, 0.0).astype(jnp.bfloat16)
            k_t[slot] = jnp.transpose(both)

    q_in.wait()
    q_copy(x, other).start()
    q_copy(mate, core).start()
    for col in (mate, near, far):
        k_from(col).wait_recv()
    k_pass(0, core).start()
    lax.fori_loop(1, reach + 1, start_k_row, 0)
    q_copy(mate, other).start()
    for col in (near, far):
        for side in range(2):
            q_copy(col, side).start()
    for col in (mate, near, far):
        v_from(col).wait_recv()
    v_pass(0, core).start()
    lax.fori_loop(1, reach + 1, start_v_row, 0)
    qbuf[x, core] = q_ref[:, pair_cols(x, core)]
    do_in.wait()
    o_in.wait()
    dobuf[x, core] = do_ref[:, pair_cols(x, core)]

    for col in range(CHIPS):
        for side in range(2):
            for g in range(PAIR):
                h = (col * 2 + side) * PAIR + g
                cols = slice(h * hw, (h + 1) * hw)
                prod = do_ref[:, cols].astype(jnp.float32) * o_ref[:, cols].astype(jnp.float32)
                rdsend[col, side, g:g + 1, :] = jnp.sum(
                    jnp.transpose(prod), axis=0, keepdims=True)
            rdsend[col, side, PAIR:, :] = jnp.zeros((8 - PAIR, tok), jnp.float32)
    rdbuf[x, core] = rdsend[x, core]
    rd_copy(x, other).start()
    for col in (mate, near, far):
        for side in range(2):
            rd_copy(col, side).start()
    kv_acc[...] = jnp.zeros(kv_acc.shape, jnp.float32)
    dq_t[...] = jnp.zeros(dq_t.shape, jnp.float32)

    k_pass(0, other).wait_recv()
    build_keys(0)

    def pass_k_row(r, c):
        k_row(r, partner).wait_recv()
        k_pass(r, core).start()
        return c

    def have_k_row(r, c):
        k_pass(r, other).wait_recv()
        build_keys(r)
        return c

    def pass_v_row(r, c):
        v_row(r, partner).wait_recv()
        v_pass(r, core).start()
        return c

    def have_v_row(r, c):
        v_pass(r, other).wait_recv()
        return c

    @pl.when(depth > 0)
    def _():
        pass_k_row(1, 0)

    tiles = [(c, g, slice((c * PAIR + g) * span, (c * PAIR + g + 1) * span))
             for c in range(2) for g in range(PAIR)]

    def place_of(block):
        return (y - block // 2) * 2 + block % 2

    def x_copy(place):
        return remote(kv_acc.at[place, other], xrecv.at[place], xs.at[place], xr.at[place], partner)

    def y_copy(r, part):
        return remote(ysend.at[r - 1, part], yrecv.at[r - 1, part], ys.at[r - 1, part],
                      yr.at[r - 1, part], at(y - r, x, core))

    def dq_copy(col, side):
        return remote(dqsend.at[col, side], dqrecv.at[x, core], ds.at[col, side],
                      dr.at[x, core], at(y, col, side))

    def settle(block):
        place = place_of(block)
        r, part = place // 2, place % 2
        x_copy(place).wait_recv()
        kv_sum = kv_acc[place, core] + xrecv[place]

        @pl.when(r > 0)
        def _():
            ysend[r - 1, part] = kv_sum.astype(jnp.bfloat16)
            y_copy(r, part).start()

        @pl.when(r == 0)
        def _():
            xrecv[place] = kv_sum

    def chunks_of(p):
        a = (x // 2 + p) % 2
        top = 2 * y + a
        return a, top, jnp.minimum(top + 1, steps)

    FIRST, BETWEEN, LAST = 0, 1, 2

    def key_rows(kind, c):
        low = 1 if kind == LAST and c == 1 else 0
        high = 1 if kind == FIRST and c == 0 else 2
        return low * span, high * span

    def powers(a, top, t, stats, kind):
        place = place_of(top - t)
        keys_x = k_x[pl.ds(2 * place, 2)].reshape(2 * span, 2 * hw)
        out = []
        for (c, g, cols), (m_run, l_run) in zip(tiles, stats):
            low, high = key_rows(kind, c)
            s = nn(keys_x[low:high], q_x[a, :, cols])
            if kind == FIRST:
                key_pos = lax.broadcasted_iota(jnp.int32, (high - low, span), 0)
                query_pos = lax.broadcasted_iota(jnp.int32, (high - low, span), 1)
                s = jnp.where(key_pos <= query_pos + c * span, s, MASKED_LOW)
            m = jnp.max(s, axis=0, keepdims=True)
            e = jnp.exp2((s - m) * LOG2_SCALE)
            e_all[a, t, low:high, cols] = e
            m_all[a, t, :, cols] = m
            l = jnp.sum(e, axis=0, keepdims=True)
            m_new = jnp.maximum(m_run, m)
            l_run = (l_run * jnp.exp2((m_run - m_new) * LOG2_SCALE)
                     + l * jnp.exp2((m - m_new) * LOG2_SCALE))
            out.append((m_new, l_run))
        return tuple(out)

    def keep(a, stats):
        top_all[a] = jnp.concatenate([m for m, _ in stats], axis=1)
        inv_all[a] = jnp.concatenate([l for _, l in stats], axis=1)

    def more_powers(a, top, start, stop):
        stats = tuple((top_all[a, :, cols], inv_all[a, :, cols]) for _, _, cols in tiles)
        keep(a, lax.fori_loop(start, stop, lambda t, now: powers(a, top, t, now, BETWEEN), stats))

    def first_pass(p, carry):
        a, top, count = chunks_of(p)

        for c in range(2):
            qc = 2 * a + c
            for side in range(2):
                @pl.when((qc != x) | (core != side))
                def _():
                    q_from(qc, side).wait_recv()
        @pl.when(p == 0)
        def _():
            do_copy(x, other).start()
            for col in (mate, near, far):
                for side in range(2):
                    do_copy(col, side).start()

        for c, g, cols in tiles:
            qc = 2 * a + c
            head = slice(g * hw, (g + 1) * hw)
            both = jnp.concatenate([qbuf[qc, 0, :, head], qbuf[qc, 1, :, head]], axis=0)
            q_h[a, cols, :] = both
            q_x[a, :hw, cols] = jnp.transpose(both)
            bars = jnp.concatenate([kbuf[0, qc, tok:, :], kbuf[1, qc, tok:, :]], axis=1)
            match = jnp.where(bars.astype(jnp.float32) == 0.0, 1.0, 0.0).astype(jnp.bfloat16)
            for i in range(CHIPS):
                q_x[a, hw + i * DOC_ROWS:hw + (i + 1) * DOC_ROWS, cols] = match
        q_x[a, hw + CHIPS * DOC_ROWS:, :] = jnp.zeros(
            (hw - CHIPS * DOC_ROWS, 2 * PAIR * span), jnp.bfloat16)

        start = tuple((jnp.full((1, span), MASKED_LOW, jnp.float32),
                       jnp.zeros((1, span), jnp.float32)) for _ in tiles)
        keep(a, powers(a, top, 0, start, FIRST))

        @pl.when((p == 0) & (depth > 0))
        def _():
            have_k_row(1, 0)

        @pl.when((p == 1) & (depth > 1))
        def _():
            lax.fori_loop(2, depth + 1, pass_k_row, 0)

        more_powers(a, top, 1, jnp.minimum(count, 3 + a))
        return carry

    def farthest_row(p, carry):
        a, top, count = chunks_of(p)
        more_powers(a, top, 3 + a, steps - 1)
        stats = tuple((top_all[a, :, cols], inv_all[a, :, cols]) for _, _, cols in tiles)
        keep(a, powers(a, top, steps - 1, stats, LAST))
        return carry

    lax.fori_loop(0, 2, first_pass, 0)

    @pl.when(depth > 1)
    def _():
        lax.fori_loop(2, depth + 1, have_k_row, 0)
        pass_v_row(1, 0)
        lax.fori_loop(0, 2, farthest_row, 0)

    for a in range(2):
        inv_all[a] = 1.0 / inv_all[a]

    def take_gradients(p, carry):
        a = (x // 2 + p) % 2
        for c in range(2):
            qc = 2 * a + c
            for side in range(2):
                @pl.when((qc != x) | (core != side))
                def _():
                    do_from(qc, side).wait_recv()
                    rd_from(qc, side).wait_recv()
        for c, g, cols in tiles:
            qc = 2 * a + c
            head = slice(g * hw, (g + 1) * hw)
            both = jnp.concatenate([dobuf[qc, 0, :, head], dobuf[qc, 1, :, head]], axis=0)
            do_h[a, cols, :] = both
            do_t[a, :, cols] = jnp.transpose(both)
            rd_h[a, :, cols] = jnp.concatenate(
                [rdbuf[qc, 0, g:g + 1, :], rdbuf[qc, 1, g:g + 1, :]], axis=1)
        return carry

    @pl.when(depth == 1)
    def _():
        pass_v_row(1, 0)

    take_gradients(0, 0)
    have_v_row(0, 0)
    take_gradients(1, 0)

    @pl.when(depth > 0)
    def _():
        have_v_row(1, 0)

    own = x // 2
    away = 1 - own
    low = 2 * y - 2 * back
    close = 8 + away

    def item(n):
        in_far, in_lead = (n >= 2) & (n < 5), n < close
        block = jnp.where(
            n < 2, 2 * y - 2,
            jnp.where(in_far, low + (n - 1) // 2,
                      jnp.where(n < 7, 2 * y - 1,
                                jnp.where(in_lead, 2 * y + n - 7, 2 * y + n - close))))
        second = (n == 1) | (n == 4) | (n == 6)
        a = jnp.where(n == 2, 0, jnp.where(second, own, jnp.where(in_lead, away, own)))
        final = second | (n == 2) | (n == 8) | (n >= close)
        return a, block, final & (block >= 0)

    def send_queries(a):
        for c, g, cols in tiles:
            qc = 2 * a + c
            piece = jnp.transpose((dq_t[a, :, cols] * SCALE).astype(jnp.bfloat16))
            head = slice(g * hw, (g + 1) * hw)
            dqsend[qc, 0, :, head] = piece[:tok]
            dqsend[qc, 1, :, head] = piece[tok:]
        for c in range(2):
            qc = 2 * a + c
            for side in range(2):
                @pl.when((qc != x) | (core != side))
                def _():
                    dq_copy(qc, side).start()

    def add_terms(a, t, block, kind):
        place = place_of(block)
        v_both = jnp.concatenate(
            [vbuf[i, 2 * place + u] for u in range(2) for i in range(2)], axis=0)
        ratio = jnp.exp2((m_all[a, t] - top_all[a]) * LOG2_SCALE) * inv_all[a]
        for c, _, cols in tiles:
            low, high = key_rows(kind, c)
            dp = nn(v_both[low:high], do_t[a, :, cols])
            pr = e_all[a, t, low:high, cols] * ratio[:, cols]
            p_low[low:high, cols] = pr.astype(jnp.bfloat16)
            s_low[low:high, cols] = (pr * (dp - rd_h[a, :, cols])).astype(jnp.bfloat16)

        def add_keys(low, high, cols):
            dv = nn(p_low[low:high, cols], do_h[a, cols, :])
            dk = nn(s_low[low:high, cols], q_h[a, cols, :]) * SCALE
            for start in range(low, high, tok):
                u, side = start // span, start // tok % 2
                piece = slice(start - low, start - low + tok)
                kv_acc[place, side, u, 0] += dk[piece]
                kv_acc[place, side, u, 1] += dv[piece]

        every = 2 * PAIR * span
        k_both = jnp.concatenate([k_t[2 * place], k_t[2 * place + 1]], axis=1)
        if kind == BETWEEN:
            add_keys(0, 2 * span, slice(0, every))
            dq_t[a] += nn(k_both, s_low[...])
        else:
            cut = slice(every // 2, every) if kind == FIRST else slice(0, every // 2)
            add_keys(0, span, slice(0, every) if kind == FIRST else cut)
            add_keys(span, 2 * span, slice(0, every) if kind == LAST else cut)
            for c in range(2):
                low, high = key_rows(kind, c)
                cols = slice(c * every // 2, (c + 1) * every // 2)
                dq_t[a, :, cols] += nn(k_both[:, low:high], s_low[low:high, cols])

    def terms(n, c):
        a, block, final = item(n)

        t = 2 * y + a - block

        @pl.when((n == 0) & (depth > 1))
        def _():
            lax.fori_loop(2, depth + 1, pass_v_row, 0)

        @pl.when((n == 2) & (depth > 1))
        def _():
            lax.fori_loop(2, depth + 1, have_v_row, 0)

        @pl.when((block >= 0) & (t == 0))
        def _():
            add_terms(a, t, block, FIRST)

        @pl.when((block >= 0) & (t > 0) & (t < steps - 1))
        def _():
            add_terms(a, t, block, BETWEEN)

        @pl.when((block >= 0) & (t == steps - 1))
        def _():
            add_terms(a, t, block, LAST)

        @pl.when(final)
        def _():
            x_copy(place_of(block)).start()

        before, final_before = item(n - 1)[1:]

        @pl.when((n > 0) & final_before)
        def _():
            settle(before)

        @pl.when(n == close - 1)
        def _():
            send_queries(away)

        return c

    last = close + own
    lax.fori_loop(0, last + 1, terms, 0)
    send_queries(own)
    settle(item(last)[1])

    def f_copy(col):
        return remote(fsend.at[col], frecv.at[x], fs.at[col], fr.at[x], at(y, col, core))

    def deliver(part, c):
        def more(r, t):
            remote(ysend.at[0, 0], yrecv.at[r - 1, part], ys.at[0, 0], yr.at[r - 1, part],
                   partner).wait_recv()
            return t + yrecv[r - 1, part].astype(jnp.float32)

        both = lax.fori_loop(1, reach + 1, more, xrecv[part]).astype(jnp.bfloat16)
        for u in range(2):
            kc = 2 * part + u
            fsend[kc] = both[u]

            @pl.when(kc != x)
            def _():
                f_copy(kc).start()

        return c

    lax.fori_loop(0, 2, deliver, 0)

    frecv[x] = fsend[x]
    dqrecv[x, core] = dqsend[x, core]

    def dq_from(col, side):
        return remote(dqsend.at[0, 0], dqrecv.at[col, side], ds.at[0, 0], dr.at[col, side], partner)

    dq_from(x, other).wait_recv()
    for col in (mate, near, far):
        for side in range(2):
            dq_from(col, side).wait_recv()
    for col in (mate, near, far):
        remote(fsend.at[0], frecv.at[col], fs.at[0], fr.at[col], partner).wait_recv()
    q_copy(x, other).wait_send()
    do_copy(x, other).wait_send()
    rd_copy(x, other).wait_send()
    dq_copy(x, other).wait_send()
    for col in (mate, near, far):
        k_copy(col).wait_send()
        v_copy(col).wait_send()
        f_copy(col).wait_send()
        for side in range(2):
            q_copy(col, side).wait_send()
            do_copy(col, side).wait_send()
            rd_copy(col, side).wait_send()
            dq_copy(col, side).wait_send()

    def sent_rows(r, c):
        k_row(r, partner).wait_send()
        v_row(r, partner).wait_send()
        return c

    def sent_on_chip(r, c):
        k_pass(r, core).wait_send()
        v_pass(r, core).wait_send()
        for part in range(2):
            x_copy(r * 2 + part).wait_send()
        return c

    def sent_terms(r, c):
        for part in range(2):
            y_copy(r, part).wait_send()
        return c

    lax.fori_loop(1, reach + 1, sent_rows, 0)
    lax.fori_loop(0, depth + 1, sent_on_chip, 0)
    lax.fori_loop(1, depth + 1, sent_terms, 0)


def lay_out(dq_raw, kv_raw, dq_out, dk_out, dv_out):
    width = dq_raw.shape[3]
    hw = kv_raw.shape[3]
    for col in range(CHIPS):
        for side in range(2):
            start = (col * 2 + side) * width
            dq_out[0, :, start:start + width] = dq_raw[col, side]
        cols = slice(col * hw, (col + 1) * hw)
        dk_out[0, :, cols] = kv_raw[col, 0]
        dv_out[0, :, cols] = kv_raw[col, 1]


def on_device(seq_size, query, keys, values, output_gradient, forward_output, doc_ids):
    tok = query.shape[1]
    span = 2 * tok
    hw = HEAD_WIDTH
    width = PAIR * hw
    rows = seq_size // (2 * CHIPS)
    back = LONGEST // (CHIPS * span)
    slots = (back + 1) * CHIPS
    wide = 2 * PAIR * span
    far = max(back, 1)
    bf, f32 = jnp.bfloat16, jnp.float32
    vmem = pl.BlockSpec(memory_space=pltpu.VMEM)
    anywhere = pl.BlockSpec(memory_space=pl.ANY)
    dma = pltpu.SemaphoreType.DMA
    dq_raw, kv_raw = pl.pallas_call(
        functools.partial(kernel, rows, back),
        out_shape=(
            jax.ShapeDtypeStruct((CHIPS, 2, tok, width), bf),
            jax.ShapeDtypeStruct((CHIPS, 2, tok, hw), bf),
        ),
        in_specs=[anywhere, vmem, vmem, anywhere, anywhere, vmem],
        out_specs=(vmem,) * 2,
        scratch_shapes=[
            pltpu.VMEM((tok, query.shape[2]), bf),
            pltpu.VMEM((tok, query.shape[2]), bf),
            pltpu.VMEM((tok, query.shape[2]), bf),
            pltpu.VMEM((CHIPS, tok + DOC_ROWS, hw), bf),
            pltpu.VMEM((2, slots, tok + DOC_ROWS, hw), bf),
            pltpu.VMEM((2, slots, tok, hw), bf),
            pltpu.VMEM((slots, span, 2 * hw), bf),
            pltpu.VMEM((slots, hw, span), bf),
            pltpu.VMEM((CHIPS, 2, 8, tok), f32),
            pltpu.VMEM((CHIPS, 2, tok, width), bf),
            pltpu.VMEM((CHIPS, 2, tok, width), bf),
            pltpu.VMEM((CHIPS, 2, 8, tok), f32),
            pltpu.VMEM((2, 2 * hw, wide), bf),
            pltpu.VMEM((2, wide, hw), bf),
            pltpu.VMEM((2, hw, wide), bf),
            pltpu.VMEM((2, wide, hw), bf),
            pltpu.VMEM((2, 1, wide), f32),
            pltpu.VMEM((2, back * 2 + 1, 2 * span, wide), f32),
            pltpu.VMEM((2, back * 2 + 1, 1, wide), f32),
            pltpu.VMEM((2, 1, wide), f32),
            pltpu.VMEM((2, 1, wide), f32),
            pltpu.VMEM((2 * span, wide), bf),
            pltpu.VMEM((2 * span, wide), bf),
            pltpu.VMEM((2, hw, wide), f32),
            pltpu.VMEM((slots // 2, 2, 2, 2, tok, hw), f32),
            pltpu.VMEM((slots // 2, 2, 2, tok, hw), f32),
            pltpu.VMEM((far, 2, 2, 2, tok, hw), bf),
            pltpu.VMEM((far, 2, 2, 2, tok, hw), bf),
            pltpu.VMEM((CHIPS, 2, tok, hw), bf),
            pltpu.VMEM((CHIPS, 2, tok, width), bf),
            dma((CHIPS,)), dma((CHIPS,)), dma((CHIPS,)), dma((CHIPS,)),
            dma((CHIPS, 2)), dma((CHIPS, 2)), dma((CHIPS, 2)), dma((CHIPS, 2)),
            dma((CHIPS, 2)), dma((CHIPS, 2)),
            dma((back + 1,)), dma((back + 1,)), dma((back + 1,)), dma((back + 1,)),
            dma((back + 1,)), dma((back + 1,)), dma((back + 1,)), dma((back + 1,)),
            dma((slots // 2,)), dma((slots // 2,)), dma((far, 2)), dma((far, 2)),
            dma((CHIPS,)), dma((CHIPS,)), dma((CHIPS, 2)), dma((CHIPS, 2)),
            dma((3,)),
        ],
        compiler_params=pltpu.CompilerParams(
            collective_id=0, has_side_effects=True, vmem_limit_bytes=56 * 1024 * 1024,
        ),
    )(query[0], keys[0], values[0], output_gradient[0], forward_output[0], doc_ids)
    return pl.pallas_call(
        lay_out,
        out_shape=(
            jax.ShapeDtypeStruct(query.shape, bf),
            jax.ShapeDtypeStruct(keys.shape, bf),
            jax.ShapeDtypeStruct(keys.shape, bf),
        ),
        in_specs=[vmem] * 2,
        out_specs=(vmem,) * 3,
    )(dq_raw, kv_raw)


def solution(mesh):
    wide = P("dp", "seq", None)
    return jax.shard_map(
        functools.partial(on_device, mesh.shape["seq"]),
        mesh=mesh,
        in_specs=(wide, wide, wide, wide, wide, P("dp", "seq")),
        out_specs=(wide, wide, wide),
        check_vma=False,
    )
```
